32 devices in a mesh: shard: 2 (over y), ctx: 4 (over x, core), tp: 4 (over z).
Axes of the slice: x: 2, y: 2, z: 4, core: 2. Of those that a mesh axis runs over, the one named last changes fastest.
Arguments:
- hidden_in: bfloat16 [8192, 1024], P(('shard', 'ctx', 'tp')), may hold values from -6 to 6
- w_qkv: bfloat16 [3, 1024, 1024], P(None, 'shard', 'tp'), may hold values from -0.1875 to 0.1875
- bias_qkv: bfloat16 [3, 16, 64], P(None, 'tp', 'shard'), may hold values from -3 to 3
- w_dense: bfloat16 [1024, 1024], P('tp', 'shard'), may hold values from -2 to 2
- w_up: bfloat16 [1024, 4096], P('shard', 'tp'), may hold values from -0.1875 to 0.1875
- bias_up: bfloat16 [64, 64], P('tp', 'shard'), may hold values from -3 to 3
- w_down: bfloat16 [4096, 1024], P('tp', 'shard'), may hold values from -0.09375 to 0.09375
- vectors: float32 [6, 1024], P(None, 'shard')
- block_deal: int32 [2, 16], P('shard'), may hold values from 0 to 15, as said below
- segments: int32 [2, 4096], P('shard'), may hold values from 0 to 6, as said below
- cotangent: bfloat16 [8192, 1024], P(('shard', 'ctx', 'tp')), may hold values from -6 to 6
Outputs:
- output: bfloat16 [8192, 1024], P(('shard', 'ctx', 'tp'))
- grad_input: bfloat16 [8192, 1024], P(('shard', 'ctx', 'tp'))
- grad_qkv: float32 [3, 1024, 1024], P(None, ('shard', 'ctx'), 'tp')
- grad_bias_qkv: float32 [3, 16, 64], P(None, 'tp', ('shard', 'ctx'))
- grad_dense: float32 [1024, 1024], P('tp', ('shard', 'ctx'))
- grad_up: float32 [1024, 4096], P(('shard', 'ctx'), 'tp')
- grad_bias_up: float32 [64, 64], P('tp', ('shard', 'ctx'))
- grad_down: float32 [4096, 1024], P('tp', ('shard', 'ctx'))
- grad_vectors: float32 [6, 1024], P(None, ('shard', 'ctx', 'tp'))
The draws below stay inside these ranges and needn't reach their ends.
Inputs may be any that keep to these rules, and one draw needn't show every extreme that they name: `block_deal`: each row is a permutation of the numbers of the batch's blocks; the batch's tokens form four equal quarters, and dealt block j (for every j) comes from quarter j mod 4, so each context rank holds one block of each quarter. `segments`: each row starts at 0 and rises by one at the first token of each new sequence; every quarter of the batch begins a new sequence, so no sequence crosses a quarter; a batch holds 7 sequences, none longer than 1024 tokens, and one of exactly 1024.
All inputs are finite; a program needn't handle non-finite values.
Results may differ from the reference program's by a relative error of at most 0.03.
Values may be sent and summed in bfloat16 or wider, within the bound.
No kernel may reach another device: no remote copies, remote signals or barrier semaphores. Data moves between devices by JAX's collectives and lax.ppermute only.
A program may use at most 192 MiB of HBM per device.

```python
import jax
import jax.numpy as jnp
from jax import lax

D = 1024
HEADS = 16
HEAD = 64
FF = 4096
ROT = 16
TOK_DEV = 1024
BLOCKS = 4
GROUP = 4096
TOKENS = 8192
LONGEST = 1024


def draw_vectors(key, part):
    key = jax.random.fold_in(key, 37)
    noise = jax.random.normal(key, (6, D), jnp.float32)
    spread = jnp.array([0.15, 0.3, 0.15, 0.3, 0.3, 0.3], jnp.float32)[:, None]
    center = jnp.array([1.0, 0.0, 1.0, 0.0, 0.0, 0.0], jnp.float32)[:, None]
    return center + spread * noise


def draw_block_deal(key, part):
    key = jax.random.fold_in(key, 11)
    groups = TOKENS // GROUP
    ranks = GROUP // TOK_DEV

    def one_batch(batch_key):
        quarter_keys = jax.random.split(batch_key, BLOCKS)
        perms = jax.vmap(lambda quarter_key: jax.random.permutation(quarter_key, ranks))(quarter_keys)
        base = jnp.arange(BLOCKS, dtype=jnp.int32)[:, None] * ranks
        return (base + perms.astype(jnp.int32)).T.reshape(BLOCKS * ranks)
    return jax.vmap(one_batch)(jax.random.split(key, groups)).astype(jnp.int32)


def draw_segments(key, part):
    key = jax.random.fold_in(key, 23)
    groups = TOKENS // GROUP

    def one_batch(batch_key):
        pick_key, cut_key = jax.random.split(batch_key)
        long_quarter = jax.random.randint(pick_key, (), 0, BLOCKS)
        cut_at = jax.random.randint(cut_key, (BLOCKS,), 1, LONGEST)
        index_row = jnp.arange(GROUP, dtype=jnp.int32)
        quarter = index_row // LONGEST
        inside = index_row % LONGEST
        cut_here = (inside == jnp.take(cut_at, quarter)) & (quarter != long_quarter)
        starts = (inside == 0) | cut_here
        return jnp.cumsum(starts.astype(jnp.int32)) - 1
    return jax.vmap(one_batch)(jax.random.split(key, groups)).astype(jnp.int32)


def raised(values, key, source, target, parts, factor):
    owner, partner = [(jnp.arange(values.shape[position]) // (values.shape[position] // parts)).reshape([-1 if axis == position else 1 for axis in range(values.ndim)]) for position in (source, target)]
    chosen = jax.random.permutation(key, parts)[partner]
    strong = (owner == chosen) | (owner == (partner + parts // 2) % parts)
    return jnp.where(strong, factor * values, values)


def block_levels(stream_key, dims, cuts, smallest, largest):
    loudness = 1.0
    for dim, parts in cuts:
        steps = jax.random.uniform(jax.random.fold_in(jax.random.fold_in(stream_key, 6), dim), (parts,), jnp.float32, smallest / len(cuts), largest / len(cuts))
        loudness = loudness * jnp.repeat(jnp.exp(steps), dims[dim] // parts).reshape((-1,) + (1,) * (len(dims) - 1 - dim))
    return loudness


def bell_draw(own_key, extent, width, most, cuts=(), kind=jnp.bfloat16):
    values = width * jax.random.normal(own_key, extent, jnp.float32)
    if cuts:
        values = values * block_levels(own_key, extent, cuts, -0.22, 0.18)
    return jnp.clip(values, -most, most).astype(kind)


def bell_draw_with(key, dims, scale, bound, cuts, heavy, kind=jnp.bfloat16):
    drawn = scale * jax.random.normal(key, dims, jnp.float32)
    if cuts:
        drawn = drawn * block_levels(key, dims, cuts, -0.22, 0.18)
    return jnp.clip(raised(drawn, jax.random.fold_in(key, 3), *heavy), -bound, bound).astype(kind)


def setup_inputs(seed: int = 0) -> dict:
    keys = jax.random.split(jax.random.key(seed), 12)
    return {
        "hidden_in": bell_draw(keys[0], (TOKENS, D), 1.0, 6.0, ((0, 32),)),
        "w_qkv": bell_draw(keys[1], (3, D, D), D ** -0.5, 0.1875, ((1, 2), (2, 4))),
        "bias_qkv": bell_draw(keys[2], (3, HEADS, HEAD), 0.5, 3.0, ((1, 4), (2, 2))),
        "w_dense": bell_draw(keys[3], (D, D), (D // 128) ** -0.5, 2.0, ((0, 4), (1, 2))),
        "w_up": bell_draw(keys[4], (D, FF), D ** -0.5, 0.1875, ((0, 2), (1, 4))),
        "bias_up": bell_draw(keys[5], (FF // HEAD, HEAD), 0.5, 3.0, ((0, 4), (1, 2))),
        "w_down": bell_draw(keys[6], (FF, D), FF ** -0.5, 0.09375, ((0, 4), (1, 2))),
        "vectors": draw_vectors(jax.random.fold_in(keys[11], 71), 0),
        "block_deal": draw_block_deal(jax.random.fold_in(keys[11], 71), 0),
        "segments": draw_segments(jax.random.fold_in(keys[11], 71), 0),
        "cotangent": bell_draw_with(keys[10], (TOKENS, D), 1.0, 6.0, ((0, 32),), (0, 1, 32, 2.75)),
    }


@jax.custom_vjp
def low(v):
    return lax.optimization_barrier(v.astype(jnp.bfloat16)).astype(jnp.float32)

@jax.custom_vjp
def low_back(v):
    return v

def low_keep(v):
    return (low(v), None)

def low_pass(kept, grad):
    return (grad,)

def back_keep(v):
    return (v, None)

def back_low(kept, grad):
    return (low(grad),)
low.defvjp(low_keep, low_pass)
low_back.defvjp(back_keep, back_low)
NORM_EPS = 1e-05
SCORE_SCALE = 0.125
ROPE_BASE = 10000.0
MASK_FILL = 1e+30

def exact_dot(left, right):
    return jnp.dot(left, right, precision=lax.Precision.HIGHEST, preferred_element_type=jnp.float32)

def layer_norm(row_vals, gain_row, shift_row):
    center = row_vals - lax.optimization_barrier(jnp.mean(row_vals, axis=-1, keepdims=True))
    spread = lax.optimization_barrier(jnp.mean(center * center, axis=-1, keepdims=True))
    return center * lax.rsqrt(spread + NORM_EPS) * gain_row + shift_row

def rotate(values, places):
    half_rot = ROT // 2
    frequency = ROPE_BASE ** (-2.0 * jnp.arange(half_rot, dtype=jnp.float32) / ROT)
    angles = places[:, None] * frequency[None, :]
    cosine = jnp.cos(angles)[:, None, :]
    sine_part = jnp.sin(angles)[:, None, :]
    first_half = values[..., :half_rot]
    second = values[..., half_rot:ROT]
    return jnp.concatenate([first_half * cosine - second * sine_part, second * cosine + first_half * sine_part, values[..., ROT:]], axis=-1)

def attend_group(queries, key_low, value_low, global_idx, seg_ids):
    group_rows = queries.shape[0]
    block_len = min(512, group_rows)
    count_blocks = group_rows // block_len
    query_blocks = queries.reshape(count_blocks, block_len, HEADS, HEAD)
    glob_blocks = global_idx.reshape(count_blocks, block_len)
    seg_blocks = seg_ids.reshape(count_blocks, block_len)

    def one_block(block_args):
        query_block, query_glob, query_seg = block_args
        raw = jnp.einsum('qhd,khd->qhk', query_block, key_low, precision=lax.Precision.HIGHEST) * SCORE_SCALE
        scores = low_back(raw)
        allowed = ((query_seg[:, None] == seg_ids[None, :]) & (global_idx[None, :] <= query_glob[:, None]))[:, None, :]
        scores = jnp.where(allowed, scores, -MASK_FILL)
        row_top = lax.optimization_barrier(jnp.max(scores, axis=-1, keepdims=True))
        row_sum = lax.optimization_barrier(jnp.sum(jnp.where(allowed, jnp.exp(scores - row_top), 0.0), axis=-1, keepdims=True))
        log_total = row_top + jnp.log(row_sum)
        probs = low(jnp.where(allowed, jnp.exp(scores - log_total), 0.0))
        return jnp.einsum('qhk,khd->qhd', probs, value_low, precision=lax.Precision.HIGHEST)
    attended = lax.map(jax.checkpoint(one_block), (query_blocks, glob_blocks, seg_blocks))
    return attended.reshape(group_rows, HEADS * HEAD)

def forward(rows_in, w_qkv, bias_qkv, w_dense, w_up, bias_up, w_down, vectors, global_idx, seg_ids, places):
    normed_one = low(layer_norm(rows_in, vectors[0], vectors[1]))
    normed_two = low(layer_norm(rows_in, vectors[2], vectors[3]))
    projected = jnp.einsum('td,cde->cte', normed_one, w_qkv, precision=lax.Precision.HIGHEST) + bias_qkv.reshape(3, 1, D)
    projected = low_back(projected)
    queries = low(rotate(projected[0].reshape(TOKENS, HEADS, HEAD), places))
    key_low = low(rotate(projected[1].reshape(TOKENS, HEADS, HEAD), places))
    value_low = low(projected[2].reshape(TOKENS, HEADS, HEAD))
    groups = TOKENS // GROUP
    shaped = (HEADS, HEAD)
    attended = lax.map(lambda group_args: attend_group(*group_args), (queries.reshape((groups, GROUP) + shaped), key_low.reshape((groups, GROUP) + shaped), value_low.reshape((groups, GROUP) + shaped), global_idx, seg_ids))
    attended = low(low_back(attended.reshape(TOKENS, D)))
    up_pre = low_back(exact_dot(normed_two, w_up) + bias_up.reshape(FF))
    activated = low(jax.nn.gelu(up_pre, approximate=False))
    return rows_in + exact_dot(attended, w_dense) + vectors[4] + exact_dot(activated, w_down) + vectors[5]

def reference(hidden_in, w_qkv, bias_qkv, w_dense, w_up, bias_up, w_down, vectors, block_deal, segments, cotangent):
    groups = TOKENS // GROUP
    block_rows = TOK_DEV // BLOCKS
    offsets = jnp.arange(block_rows, dtype=jnp.int32)
    global_idx = (block_deal[:, :, None] * block_rows + offsets[None, None, :]).reshape(groups, GROUP).astype(jnp.int32)
    index_row = jnp.arange(GROUP, dtype=jnp.int32)[None, :]
    previous = jnp.concatenate([segments[:, :1] - 1, segments[:, :-1]], axis=1)
    starts = lax.cummax(jnp.where(segments != previous, index_row, 0), axis=1)
    seg_ids = jnp.take_along_axis(segments, global_idx, axis=1)
    places = (global_idx - jnp.take_along_axis(starts, global_idx, axis=1)).reshape(TOKENS).astype(jnp.float32)
    params = (hidden_in.astype(jnp.float32), w_qkv.astype(jnp.float32), bias_qkv.astype(jnp.float32), w_dense.astype(jnp.float32), w_up.astype(jnp.float32), bias_up.astype(jnp.float32), w_down.astype(jnp.float32), vectors.astype(jnp.float32))

    def layer(*weights):
        return forward(*weights, global_idx, seg_ids, places)
    result, pull = jax.vjp(layer, *params)
    grads = pull(cotangent.astype(jnp.float32))
    return (result.astype(jnp.bfloat16), grads[0].astype(jnp.bfloat16), grads[1], grads[2], grads[3], grads[4], grads[5], grads[6], grads[7])
```

```python
import functools

import jax
import jax.numpy as jnp
from jax import lax
from jax.experimental import pallas as pl
from jax.experimental.pallas import tpu as pltpu
from jax.sharding import PartitionSpec as P

HEAD = 64
ROT = 16
NORM_EPS = 1e-05
SCORE_SCALE = 0.125
ROPE_BASE = 10000.0
MASK_FILL = 1e30
F32 = jnp.float32
BF16 = jnp.bfloat16
VMEM_LIMIT = 56 * 1024 * 1024


def dot(left, right, left_dim=1, right_dim=0):
    return lax.dot_general(
        left, right, (((left_dim,), (right_dim,)), ((), ())), preferred_element_type=F32
    )


def params():
    return pltpu.CompilerParams(vmem_limit_bytes=VMEM_LIMIT)


def cost(flops, read, exps=0):
    return pl.CostEstimate(flops=int(flops), bytes_accessed=int(read), transcendentals=int(exps))


def swap_halves(values):
    width = values.shape[-1]
    lane = lax.broadcasted_iota(jnp.int32, (1, width), 1) % HEAD
    ahead = pltpu.roll(values, width - ROT // 2, 1)
    behind = pltpu.roll(values, ROT // 2, 1)
    return jnp.where(lane < ROT // 2, ahead, behind)


def widen(table, width):
    return jnp.concatenate([table] * (width // table.shape[-1]), axis=-1)


def norm_rows(rows):
    center = rows - jnp.mean(rows, axis=-1, keepdims=True)
    inverse = lax.rsqrt(jnp.mean(center * center, axis=-1, keepdims=True) + NORM_EPS)
    return center * inverse, inverse


def qkv_kernel(x_ref, vec_ref, w_ref, bias_ref, cos_ref, sin_ref, qkv_ref, one_ref, two_ref):
    hat, _ = norm_rows(x_ref[...].astype(F32))
    one = (hat * vec_ref[0:1, :] + vec_ref[1:2, :]).astype(BF16)
    one_ref[...] = one
    width = w_ref.shape[2]
    cosine, sine = widen(cos_ref[...], width), widen(sin_ref[...], width)
    for part in range(3):
        lin = dot(one, w_ref[part]) + bias_ref[part : part + 1, :]
        if part < 2:
            lin = lin * cosine + swap_halves(lin) * sine
        if part == 0:
            lin = lin * SCORE_SCALE
        qkv_ref[:, part * width : (part + 1) * width] = lin.astype(BF16)
    two_ref[...] = (hat * vec_ref[2:3, :] + vec_ref[3:4, :]).astype(BF16)


def project(rows_all, vec, w_full, bias, cosine, sine, block):
    rows, dim = rows_all.shape
    width = w_full.shape[2]
    row_spec = lambda cols: pl.BlockSpec((block, cols), lambda i: (i, 0))
    whole = lambda a: pl.BlockSpec(a.shape, lambda i: (0,) * a.ndim)
    return pl.pallas_call(
        qkv_kernel,
        grid=(rows // block,),
        in_specs=[
            row_spec(dim), whole(vec), whole(w_full), whole(bias),
            row_spec(cosine.shape[1]), row_spec(sine.shape[1]),
        ],
        out_specs=[row_spec(3 * width), row_spec(dim), row_spec(dim)],
        out_shape=[
            jax.ShapeDtypeStruct((rows, 3 * width), BF16),
            jax.ShapeDtypeStruct((rows, dim), BF16),
            jax.ShapeDtypeStruct((rows, dim), BF16),
        ],
        compiler_params=params(),
        cost_estimate=cost(6 * rows * dim * width, 10 * rows * dim),
        name="norm_qkv",
    )(rows_all, vec, w_full, bias, cosine, sine)


def up_kernel(a_ref, w_ref, bias_ref, act_ref, slope_ref):
    pre = dot(a_ref[...], w_ref[...]) + bias_ref[...]
    phi = 0.5 * (1.0 + lax.erf(pre * 0.7071067811865476))
    act_ref[...] = (pre * phi).astype(BF16)
    slope = phi + pre * (0.3989422804014327 * jnp.exp(-0.5 * pre * pre))
    slope_ref[...] = slope.astype(BF16)


def mlp_up(two, up_full, bias, block):
    rows, dim = two.shape
    hidden = up_full.shape[1]
    row_spec = lambda cols: pl.BlockSpec((block, cols), lambda i: (i, 0))
    whole = lambda a: pl.BlockSpec(a.shape, lambda i: (0,) * a.ndim)
    return pl.pallas_call(
        up_kernel,
        grid=(rows // block,),
        in_specs=[row_spec(dim), whole(up_full), whole(bias)],
        out_specs=[row_spec(hidden), row_spec(hidden)],
        out_shape=[jax.ShapeDtypeStruct((rows, hidden), BF16)] * 2,
        compiler_params=params(),
        cost_estimate=cost(2 * rows * dim * hidden, 8 * rows * dim, 2 * rows * hidden),
        name="mlp_up",
    )(two, up_full, bias)


def pair_bias(start_ref, first, size, keys):
    query_at = lax.broadcasted_iota(jnp.int32, (size, keys), 0) + first
    key_at = lax.broadcasted_iota(jnp.int32, (size, keys), 1)
    allowed = (key_at <= query_at) & (key_at >= start_ref[first : first + size, :])
    return jnp.where(allowed, 0.0, -MASK_FILL)


def attn_fwd_kernel(count, pos_ref, start_ref, *refs):
    blocks, outs = refs[:count], refs[count : 2 * count]
    q_ref, k_ref, v_ref, lse_ref, o_ref = refs[2 * count :]
    size, width = outs[0].shape
    for r in range(count):
        rows = pl.ds(pl.multiple_of(pos_ref[r] * size, size), size)
        q_ref[rows, :] = blocks[r][:, :width]
        k_ref[rows, :] = blocks[r][:, width : 2 * width]
        v_ref[rows, :] = blocks[r][:, 2 * width :]
    group = lax.broadcasted_iota(jnp.int32, (1, width), 1) // HEAD
    lane = lax.broadcasted_iota(jnp.int32, (1, 128), 1)
    zero = jnp.zeros((), BF16)
    for i in range(count):
        first, keys = i * size, (i + 1) * size
        bias = pair_bias(start_ref, first, size, keys)
        query = q_ref[first:keys, :]
        total = jnp.zeros((size, width), F32)
        tops = jnp.zeros((size, 128), F32)
        for head in range(width // HEAD):
            mine = group == head
            scores = dot(jnp.where(mine, query, zero), k_ref[:keys, :], 1, 1) + bias
            top = jnp.max(scores, axis=-1, keepdims=True)
            terms = jnp.exp(scores - top)
            row_sum = jnp.sum(terms, axis=-1, keepdims=True)
            probs = (terms * (1.0 / row_sum)).astype(BF16)
            total = total + dot(probs, jnp.where(mine, v_ref[:keys, :], zero))
            tops = jnp.where(lane == head, top + jnp.log(row_sum), tops)
        o_ref[first:keys, :] = total
        lse_ref[first:keys, :] = tops
    for r in range(count):
        rows = pl.ds(pl.multiple_of(pos_ref[r] * size, size), size)
        outs[r][...] = o_ref[rows, :].astype(BF16)


def attend(pos, start_col, blocks):
    count = len(blocks)
    size, wide = blocks[0].shape
    width, length = wide // 3, size * count
    vmem = pl.BlockSpec(memory_space=pltpu.VMEM)
    result = pl.pallas_call(
        functools.partial(attn_fwd_kernel, count),
        in_specs=[pl.BlockSpec(memory_space=pltpu.SMEM)] + [vmem] * (1 + count),
        out_specs=[vmem] * (count + 4),
        out_shape=[jax.ShapeDtypeStruct((size, width), BF16)] * count
        + [jax.ShapeDtypeStruct((length, width), BF16)] * 3
        + [jax.ShapeDtypeStruct((length, 128), F32)],
        scratch_shapes=[pltpu.VMEM((length, width), F32)],
        compiler_params=params(),
        cost_estimate=cost(8 * length * length * width, 8 * length * width, length * length * 2),
        name="attend",
    )(pos, start_col, *blocks)
    return result[:count], result[count:]


def attn_bwd_kernel(count, pos_ref, start_ref, q_ref, k_ref, v_ref, lse_ref, cos_ref, sin_ref, *refs):
    blocks, outs = refs[:count], refs[count : 2 * count]
    do_ref, dq_ref, dk_ref, dv_ref = refs[2 * count :]
    size, width = blocks[0].shape
    for r in range(count):
        rows = pl.ds(pl.multiple_of(pos_ref[r] * size, size), size)
        do_ref[rows, :] = blocks[r][...]
    dk_ref[...] = jnp.zeros_like(dk_ref)
    dv_ref[...] = jnp.zeros_like(dv_ref)
    group = lax.broadcasted_iota(jnp.int32, (1, width), 1) // HEAD
    zero = jnp.zeros((), BF16)
    for i in range(count):
        first, keys = i * size, (i + 1) * size
        bias = pair_bias(start_ref, first, size, keys)
        total = jnp.zeros((size, width), F32)
        for head in range(width // HEAD):
            mine = group == head
            query = jnp.where(mine, q_ref[first:keys, :], zero)
            grad_out = jnp.where(mine, do_ref[first:keys, :], zero)
            scores = dot(query, k_ref[:keys, :], 1, 1) + bias
            probs = jnp.exp(scores - lse_ref[first:keys, head : head + 1])
            grad_prob = dot(grad_out, v_ref[:keys, :], 1, 1)
            delta = jnp.sum(probs * grad_prob, axis=-1, keepdims=True)
            grad_score = (probs * (grad_prob - delta)).astype(BF16)
            total = total + dot(grad_score, jnp.where(mine, k_ref[:keys, :], zero))
            dk_ref[:keys, :] += dot(grad_score, query, 0, 0)
            dv_ref[:keys, :] += dot(probs.astype(BF16), grad_out, 0, 0)
        dq_ref[first:keys, :] = total * SCORE_SCALE
    for r in range(count):
        rows = pl.ds(pl.multiple_of(pos_ref[r] * size, size), size)
        cosine, sine = widen(cos_ref[rows, :], width), widen(sin_ref[rows, :], width)
        for part, ref in ((0, dq_ref), (1, dk_ref)):
            grad = ref[rows, :]
            grad = grad * cosine - swap_halves(grad) * sine
            outs[r][:, part * width : (part + 1) * width] = grad.astype(BF16)
        outs[r][:, 2 * width :] = dv_ref[rows, :].astype(BF16)


def attend_back(pos, start_col, kept, cosine, sine, blocks):
    count = len(blocks)
    size, width = blocks[0].shape
    length = size * count
    vmem = pl.BlockSpec(memory_space=pltpu.VMEM)
    return pl.pallas_call(
        functools.partial(attn_bwd_kernel, count),
        in_specs=[pl.BlockSpec(memory_space=pltpu.SMEM)] + [vmem] * (7 + count),
        out_specs=[vmem] * count,
        out_shape=[jax.ShapeDtypeStruct((size, 3 * width), BF16)] * count,
        scratch_shapes=[pltpu.VMEM((length, width), BF16)] + [pltpu.VMEM((length, width), F32)] * 3,
        compiler_params=params(),
        cost_estimate=cost(20 * length * length * width, 16 * length * width, length * length * 2),
        name="attend_back",
    )(pos, start_col, *kept, cosine, sine, *blocks)


def place_kernel(count, parts, row_ref, col_ref, *refs):
    blocks, out = refs[:count], refs[count]
    size, wide = blocks[0].shape
    width = wide // parts
    full = out.shape[1] // parts
    for r in range(count):
        rows = pl.ds(pl.multiple_of(row_ref[r] * size, size), size)
        for part in range(parts):
            values = blocks[r][:, part * width : (part + 1) * width]
            if width == full:
                out[rows, part * full : (part + 1) * full] = values
            else:
                column = pl.multiple_of(part * full + col_ref[r] * width, width)
                out[rows, pl.ds(column, width)] = values


def place(row_at, col_at, blocks, rows, full, parts):
    vmem = pl.BlockSpec(memory_space=pltpu.VMEM)
    smem = pl.BlockSpec(memory_space=pltpu.SMEM)
    return pl.pallas_call(
        functools.partial(place_kernel, len(blocks), parts),
        in_specs=[smem, smem] + [vmem] * len(blocks),
        out_specs=vmem,
        out_shape=jax.ShapeDtypeStruct((rows, parts * full), blocks[0].dtype),
        compiler_params=params(),
        cost_estimate=cost(0, 4 * rows * full * parts),
        name="place",
    )(row_at, col_at, *blocks)


def by_xor(axis, count, step):
    return functools.partial(
        lax.ppermute, axis_name=axis, perm=[(i, i ^ step) for i in range(count)]
    )


def pick(values, parts, full, width, size, row_at, col_at):
    rows = lax.dynamic_slice_in_dim(values, row_at * size, size, 0)
    if width == full:
        return rows
    columns = [
        lax.dynamic_slice_in_dim(rows, part * full + col_at * width, width, 1)
        for part in range(parts)
    ]
    return jnp.concatenate(columns, axis=1)


def input_grad_kernel(x_ref, dlin_ref, w_ref, two_ref, vec_ref, sum_ref, grads_ref):
    width = w_ref.shape[2]
    hat, _ = norm_rows(x_ref[...].astype(F32))
    one = dot(dlin_ref[:, :width], w_ref[0], 1, 1)
    for part in (1, 2):
        one = one + dot(dlin_ref[:, part * width : (part + 1) * width], w_ref[part], 1, 1)
    two = two_ref[...]
    sum_ref[...] = (one * vec_ref[0:1, :] + two * vec_ref[2:3, :]).astype(BF16)
    rows = [
        jnp.sum(values, axis=0, keepdims=True) for values in (one * hat, one, two * hat, two)
    ]
    share = jnp.concatenate(rows + [jnp.zeros_like(rows[0])] * 4, axis=0)

    @pl.when(pl.program_id(0) == 0)
    def _():
        grads_ref[...] = share

    @pl.when(pl.program_id(0) > 0)
    def _():
        grads_ref[...] += share


def input_grad(rows_all, dlin, w_full, grad_two, vec, block):
    rows, dim = rows_all.shape
    row_spec = lambda cols: pl.BlockSpec((block, cols), lambda i: (i, 0))
    whole = lambda a: pl.BlockSpec(a.shape, lambda i: (0,) * a.ndim)
    return pl.pallas_call(
        input_grad_kernel,
        grid=(rows // block,),
        in_specs=[row_spec(dim), row_spec(dlin.shape[1]), whole(w_full), row_spec(dim), whole(vec)],
        out_specs=[row_spec(dim), pl.BlockSpec((8, dim), lambda i: (0, 0))],
        out_shape=[
            jax.ShapeDtypeStruct((rows, dim), BF16),
            jax.ShapeDtypeStruct((8, dim), F32),
        ],
        compiler_params=params(),
        cost_estimate=cost(2 * rows * dim * dlin.shape[1], 10 * rows * dim),
        name="input_grad",
    )(rows_all, dlin, w_full, grad_two, vec)


def join(own, axis, dim, count):
    if count != 2:
        return lax.all_gather(own, axis, axis=dim, tiled=True)
    other = by_xor(axis, 2, 1)(own)
    first = lax.axis_index(axis) == 0
    return jnp.concatenate(
        [jnp.where(first, own, other), jnp.where(first, other, own)], axis=dim
    )


def halve(values, dim, axis, count, bit, wire):
    mine = (lax.axis_index(axis) >> bit) & 1
    away = lax.dynamic_index_in_dim(values, 1 - mine, dim, keepdims=False)
    keep = lax.dynamic_index_in_dim(values, mine, dim, keepdims=False)
    came = by_xor(axis, count, 1 << bit)(away.astype(wire))
    return keep.astype(F32) + came.astype(F32)


def scatter_sum(values, dim, axes, wire):
    head, tail = values.shape[:dim], values.shape[dim + 1 :]
    bits = []
    for axis, count in axes:
        bits += [(axis, count, bit) for bit in reversed(range(count.bit_length() - 1))]
    order = [entry for axis, _ in reversed(axes) for entry in reversed([b for b in bits if b[0] == axis])]
    owners = 1
    for _, count in axes:
        owners *= count
    values = values.reshape(head + (2,) * len(bits) + (values.shape[dim] // owners,) + tail)
    left = list(bits)
    for index, entry in enumerate(order):
        at = len(head) + left.index(entry)
        left.remove(entry)
        values = halve(values, at, entry[0], entry[1], entry[2], wire)
        if index < len(order) - 1:
            values = values.astype(wire)
    return values


def body(
    sizes, hidden_in, w_qkv, bias_qkv, w_dense, w_up, bias_up, w_down, vectors, block_deal,
    segments, cotangent,
):
    shards, ranks, tps = sizes
    rank = lax.axis_index("ctx")
    dim = hidden_in.shape[1]
    own_rows = hidden_in.shape[0]

    x_all = lax.all_gather(hidden_in, "tp", axis=0, tiled=True)
    cot_all = lax.all_gather(cotangent, "tp", axis=0, tiled=True)
    heads = bias_qkv.shape[1]
    width = heads * HEAD
    half = vectors.shape[1]
    small = jnp.concatenate(
        [vectors.reshape(-1), bias_qkv.astype(F32).reshape(-1), bias_up.astype(F32).reshape(-1)]
    )
    pad = -small.shape[0] % 1024
    small = jnp.pad(small, (0, pad)).reshape(1, -1, 128)
    small = join(small, "shard", 0, shards).reshape(shards, -1)
    cut = 6 * half
    vec = small[:, :cut].reshape(shards, 6, half).transpose(1, 0, 2).reshape(6, dim)
    vec = jnp.pad(vec, ((0, 2), (0, 0)))
    share = bias_qkv.size
    qkv_bias = small[:, cut : cut + share].reshape((shards,) + bias_qkv.shape)
    qkv_bias = qkv_bias.transpose(1, 2, 0, 3).reshape(3, width)
    up_bias = small[:, cut + share : cut + share + bias_up.size].reshape((shards,) + bias_up.shape)
    up_bias = up_bias.transpose(1, 0, 2).reshape(1, -1)
    qkv_full = join(w_qkv, "shard", 1, shards)
    up_full = join(w_up, "shard", 0, shards)
    down_full = join(w_down, "shard", 1, shards)
    dense_full = join(w_dense, "shard", 1, shards)

    deal = block_deal[0]
    seg_row = segments[0]
    group = seg_row.shape[0]
    block = group // deal.shape[0]
    quarters = deal.shape[0] // ranks
    rank_rows = quarters * block
    split = ranks // quarters
    part_width = width // split
    length = group // quarters
    at = jnp.arange(group, dtype=jnp.int32)
    previous = jnp.concatenate([seg_row[:1] - 1, seg_row[:-1]])
    begins = lax.cummax(jnp.where(seg_row != previous, at, 0), axis=0)
    places = (at - begins).reshape(deal.shape[0], block)
    deal_by_rank = deal.reshape(ranks, quarters)
    my_deal = lax.dynamic_index_in_dim(deal_by_rank, rank, 0, keepdims=False)
    picked = my_deal[:, None] == jnp.arange(deal.shape[0], dtype=jnp.int32)[None, :]
    rank_place = jnp.sum(jnp.where(picked[:, :, None], places[None], 0), axis=1).reshape(-1)
    quarter = rank // split
    partners = rank ^ jnp.arange(ranks, dtype=jnp.int32)
    in_quarter = jnp.take(lax.dynamic_index_in_dim(deal_by_rank, quarter, 1, keepdims=False), partners)
    pos = in_quarter - quarter * ranks
    my_begins = lax.dynamic_slice_in_dim(begins, quarter * length, length) - quarter * length
    quarter_place = jnp.arange(length, dtype=jnp.int32) - my_begins
    start_col = my_begins[:, None]
    lane = jnp.arange(128, dtype=jnp.int32) % HEAD
    frequency = ROPE_BASE ** (-2.0 * (lane % (ROT // 2)).astype(F32) / ROT)
    frequency = jnp.where(lane < ROT, frequency, 0.0)
    sign = jnp.where(lane < ROT // 2, -1.0, 1.0)
    all_places = jnp.concatenate([rank_place, quarter_place]).astype(F32)
    angles = all_places[:, None] * frequency[None, :]
    cosine, sine = jnp.cos(angles), jnp.sin(angles) * sign[None, :]
    target_row, target_col = partners // split, partners % split

    qkv, full_one, full_two = project(
        x_all, vec, qkv_full, qkv_bias, cosine[:rank_rows], sine[:rank_rows], block
    )

    def to_quarters(values, parts):
        sent = []
        for step in range(ranks):
            piece = pick(
                values, parts, width, part_width, block, target_row[step], target_col[step]
            )
            sent.append(by_xor("ctx", ranks, step)(piece) if step else piece)
        return sent

    def to_ranks(pieces, parts):
        came = [by_xor("ctx", ranks, s)(p) if s else p for s, p in enumerate(pieces)]
        return place(target_row, target_col, came, rank_rows, width, parts)

    out_pieces, kept = attend(pos, start_col, to_quarters(qkv, 3))
    activated, slope = mlp_up(full_two, up_full, up_bias, block)
    down_part = dot(activated, down_full)
    attended = to_ranks(out_pieces, 1)
    partial = (down_part + dot(attended, dense_full)).astype(BF16)
    summed = lax.psum_scatter(partial, "tp", scatter_dimension=0, tiled=True).astype(F32)
    rows_in = hidden_in.astype(F32)
    output = (rows_in + summed + vec[4:5] + vec[5:6]).astype(BF16)

    grad_attn = dot(cot_all, dense_full, 1, 1).astype(BF16)
    grad_pieces = attend_back(
        pos, start_col, kept, cosine[rank_rows:], sine[rank_rows:], to_quarters(grad_attn, 1)
    )
    grad_pre = (dot(cot_all, down_full, 1, 1) * slope.astype(F32)).astype(BF16)
    grad_two = dot(grad_pre, up_full, 1, 1)
    axes = (("shard", shards), ("ctx", ranks))
    grad_down = scatter_sum(dot(activated, cot_all, 0, 0).astype(BF16), 1, axes, BF16)
    grad_up = scatter_sum(dot(full_two, grad_pre, 0, 0).astype(BF16), 0, axes, BF16)
    grad_dense = scatter_sum(dot(attended, cot_all, 0, 0).astype(BF16), 1, axes, BF16)
    grad_ubias = jnp.sum(grad_pre.astype(F32), axis=0)
    dlin = to_ranks(grad_pieces, 3)
    row_sum, gains = input_grad(x_all, dlin, qkv_full, grad_two, vec, block)
    own_sum = lax.psum_scatter(row_sum, "tp", scatter_dimension=0, tiled=True).astype(F32)
    grad_qkv = dot(full_one, dlin, 0, 0).astype(BF16).reshape(dim, 3, width).transpose(1, 0, 2)
    grad_qkv = scatter_sum(grad_qkv, 1, axes, BF16)
    grad_qbias = jnp.sum(dlin.astype(F32), axis=0)

    cot_rows = cotangent.astype(F32)
    cot_sum = jnp.sum(cot_rows, axis=0, keepdims=True)
    grad_vec = jnp.concatenate([gains[:4], cot_sum, cot_sum], axis=0)
    owners = shards * ranks
    each = HEAD // owners
    packed = jnp.concatenate(
        [
            grad_vec.reshape(6, owners, -1).transpose(1, 0, 2).reshape(owners, -1),
            grad_qbias.reshape(-1, owners, each).transpose(1, 0, 2).reshape(owners, -1),
            grad_ubias.reshape(-1, owners, each).transpose(1, 0, 2).reshape(owners, -1),
        ],
        axis=1,
    )
    packed = scatter_sum(packed, 0, axes, F32).reshape(-1)
    cut = 6 * (dim // owners)
    count = 3 * heads * each
    grad_vec = scatter_sum(packed[:cut].reshape(6, -1), 1, (("tp", tps),), F32)
    grad_qbias = packed[cut : cut + count].reshape(3, heads, each)
    grad_ubias = packed[cut + count :].reshape(bias_up.shape[0], each)

    hat, inverse = norm_rows(rows_in)
    centered = own_sum - jnp.mean(own_sum, axis=-1, keepdims=True)
    along = jnp.mean(own_sum * hat, axis=-1, keepdims=True)
    grad_in = (cot_rows + inverse * (centered - hat * along)).astype(BF16)
    return (
        output, grad_in, grad_qkv.reshape(3, -1, width), grad_qbias, grad_dense, grad_up, grad_ubias,
        grad_down, grad_vec,
    )


def solution(mesh):
    sizes = tuple(mesh.shape[name] for name in ("shard", "ctx", "tp"))
    return jax.shard_map(
        functools.partial(body, sizes),
        mesh=mesh,
        in_specs=(
            P(("shard", "ctx", "tp"), None),
            P(None, "shard", "tp"),
            P(None, "tp", "shard"),
            P("tp", "shard"),
            P("shard", "tp"),
            P("tp", "shard"),
            P("tp", "shard"),
            P(None, "shard"),
            P("shard", None),
            P("shard", None),
            P(("shard", "ctx", "tp"), None),
        ),
        out_specs=(
            P(("shard", "ctx", "tp"), None),
            P(("shard", "ctx", "tp"), None),
            P(None, ("shard", "ctx"), "tp"),
            P(None, "tp", ("shard", "ctx")),
            P("tp", ("shard", "ctx")),
            P(("shard", "ctx"), "tp"),
            P("tp", ("shard", "ctx")),
            P("tp", ("shard", "ctx")),
            P(None, ("shard", "ctx", "tp")),
        ),
        check_vma=False,
    )
```

```python
import functools

import jax
import jax.numpy as jnp
from jax import lax
from jax.experimental import pallas as pl
from jax.experimental.pallas import tpu as pltpu
from jax.sharding import PartitionSpec as P

HEAD = 64
GROUP = 128
ROT = 16
NORM_EPS = 1e-05
SCORE_SCALE = 0.125
ROPE_BASE = 10000.0
MASK_FILL = 1e30
F32 = jnp.float32
BF16 = jnp.bfloat16
VMEM_LIMIT = 56 * 1024 * 1024


def dot(left, right, left_dim=1, right_dim=0):
    return lax.dot_general(
        left, right, (((left_dim,), (right_dim,)), ((), ())), preferred_element_type=F32
    )


def params():
    return pltpu.CompilerParams(vmem_limit_bytes=VMEM_LIMIT)


def brief(us=0):
    return pl.CostEstimate(flops=int(us * 1.1e9) + 1, bytes_accessed=1, transcendentals=0)


def swap_halves(values):
    width = values.shape[-1]
    lane = lax.broadcasted_iota(jnp.int32, (1, width), 1) % HEAD
    ahead = pltpu.roll(values, width - ROT // 2, 1)
    behind = pltpu.roll(values, ROT // 2, 1)
    return jnp.where(lane < ROT // 2, ahead, behind)


def widen(table, width):
    return jnp.concatenate([table] * (width // table.shape[-1]), axis=-1)


def norm_rows(rows):
    center = rows - jnp.mean(rows, axis=-1, keepdims=True)
    inverse = lax.rsqrt(jnp.mean(center * center, axis=-1, keepdims=True) + NORM_EPS)
    return center * inverse, inverse


def whole(array):
    return pl.BlockSpec(array.shape, lambda *ids: (0,) * array.ndim)


def row_block(block, cols):
    return pl.BlockSpec((block, cols), lambda i, *ids: (i, 0))


def piece_shapes(pieces, ranks, merged, shape):
    shapes = []
    for step in range(ranks):
        if 0 < step < merged:
            shapes.append((pieces,) + shape)
        else:
            shapes += [(1,) + shape] * pieces
    return shapes


def by_step(flat, pieces, ranks, merged):
    steps, at = [], 0
    for step in range(ranks):
        count = 1 if 0 < step < merged else pieces
        steps.append(flat[at : at + count])
        at += count
    return steps


def send_pieces(i, split, merged, flag_ref, flat, groups_ref, ranks):
    pieces = groups_ref.shape[0] // split
    for step, refs in enumerate(by_step(flat, pieces, ranks, merged)):

        @pl.when(i == step // split)
        def _(step=step, refs=refs):
            for p in range(pieces):
                group = p
                if split > 1:
                    group = ((flag_ref[1] ^ step) % split) * pieces + p
                if len(refs) == 1:
                    refs[0][p] = groups_ref[group]
                else:
                    refs[p][0] = groups_ref[group]


def exchange(flat, pieces, ranks, merged):
    came = [[] for _ in range(pieces)]
    for step, arrays in enumerate(by_step(flat, pieces, ranks, merged)):
        if step:
            arrays = [by_xor("ctx", ranks, step)(array) for array in arrays]
        for p in range(pieces):
            came[p].append((arrays[0], p) if len(arrays) == 1 else (arrays[p], 0))
    return came


def quarter_block(block, cols, split):
    return pl.BlockSpec((block, cols), lambda i, flags: ((flags[1] // split) ^ i, 0))


def fixed(shape):
    return pl.BlockSpec(shape, lambda *ids: (0,) * len(shape))


def qkv_kernel(
    split, ranks, at, weights, late, flag_ref, x_ref, vec_ref, bias_ref, cos_ref, sin_ref, *refs
):
    refs = refs[:weights] + refs[weights + late :]
    one_ref, groups_ref, w_ref = refs[weights], refs[-2], refs[-1]
    once((at, flag_ref, refs[:weights], w_ref))
    i = pl.program_id(0)
    hat, _ = norm_rows(x_ref[...].astype(F32))
    one = (hat * vec_ref[0:1, :] + vec_ref[1:2, :]).astype(BF16)
    one_ref[...] = one
    width = w_ref.shape[2]
    cosine, sine = widen(cos_ref[...], width), widen(sin_ref[...], width)
    for part in range(3):
        lin = dot(one, w_ref[part]) + bias_ref[part : part + 1, :]
        if part < 2:
            lin = lin * cosine + swap_halves(lin) * sine
        if part == 0:
            lin = lin * SCORE_SCALE
        low = lin.astype(BF16)
        for g in range(width // GROUP):
            groups_ref[g, :, part * GROUP : (part + 1) * GROUP] = low[:, g * GROUP : (g + 1) * GROUP]
    send_pieces(i, split, 2, flag_ref, refs[weights + 1 : -2], groups_ref, ranks)


def project(flags, split, ranks, rows_all, vec, weight, bias, cosine, sine, block, late):
    rows, dim = rows_all.shape
    width = weight.shape[2]
    groups = width // GROUP
    piece = (block, 3 * GROUP)
    shapes = piece_shapes(groups // split, ranks, 2, piece)
    result = pl.pallas_call(
        functools.partial(
            qkv_kernel, split, ranks, weight.at, len(weight.arrays), len(late)
        ),
        grid_spec=pltpu.PrefetchScalarGridSpec(
            num_scalar_prefetch=1,
            grid=(rows // block,),
            in_specs=[
                quarter_block(block, dim, split), whole(vec), whole(bias),
                quarter_block(block, cosine.shape[1], split),
                quarter_block(block, sine.shape[1], split),
            ]
            + weight.specs()
            + [pl.BlockSpec(memory_space=pl.ANY)] * len(late),
            out_specs=[quarter_block(block, dim, split)] + [fixed(shape) for shape in shapes],
            scratch_shapes=[pltpu.VMEM((groups,) + piece, BF16), weight.scratch()],
        ),
        out_shape=[jax.ShapeDtypeStruct((rows, dim), BF16)]
        + [jax.ShapeDtypeStruct(shape, BF16) for shape in shapes],
        compiler_params=params(),
        cost_estimate=brief(300),
        name="norm_qkv",
    )(flags, rows_all, vec, bias, cosine, sine, *weight.arrays, *late)
    return result[0], result[1:]


def attn_grad_kernel(split, ranks, at, weights, late, flag_ref, cot_ref, *refs):
    refs = refs[:weights] + refs[weights + late :]
    groups_ref, w_ref = refs[-2:]
    once((at, flag_ref, refs[:weights], w_ref))
    grad = dot(cot_ref[...], w_ref[0], 1, 1).astype(BF16)
    for g in range(groups_ref.shape[0]):
        groups_ref[g] = grad[:, g * GROUP : (g + 1) * GROUP]
    send_pieces(pl.program_id(0), split, ranks, flag_ref, refs[weights:-2], groups_ref, ranks)


def attn_grad(flags, split, ranks, cot_all, weight, block, late):
    rows, dim = cot_all.shape
    groups = weight.shape[1] // GROUP
    piece = (block, GROUP)
    shapes = piece_shapes(groups // split, ranks, ranks, piece)
    result = pl.pallas_call(
        functools.partial(
            attn_grad_kernel, split, ranks, weight.at, len(weight.arrays), len(late)
        ),
        grid_spec=pltpu.PrefetchScalarGridSpec(
            num_scalar_prefetch=1,
            grid=(rows // block,),
            in_specs=[quarter_block(block, dim, split)]
            + weight.specs()
            + [pl.BlockSpec(memory_space=pl.ANY)] * len(late),
            out_specs=[fixed(shape) for shape in shapes],
            scratch_shapes=[pltpu.VMEM((groups,) + piece, BF16), weight.scratch()],
        ),
        out_shape=[jax.ShapeDtypeStruct(shape, BF16) for shape in shapes],
        compiler_params=params(),
        cost_estimate=brief(300),
        name="attn_grad",
    )(flags, cot_all, *weight.arrays, *late)
    return result


def mlp_kernel(ats, weights, flag_ref, x_ref, vec_ref, bias_ref, late_ref, *refs):
    two_ref, act_ref, slope_ref, part_ref, up_ref, down_ref = refs[-6:]
    once(
        (ats[0], flag_ref, refs[:weights], up_ref),
        (ats[1], flag_ref, refs[weights : 2 * weights], down_ref),
    )
    hat, _ = norm_rows(x_ref[...].astype(F32))
    two = (hat * vec_ref[2:3, :] + vec_ref[3:4, :]).astype(BF16)
    two_ref[...] = two
    pre = dot(two, up_ref[0]) + bias_ref[...]
    phi = 0.5 * (1.0 + lax.erf(pre * 0.7071067811865476))
    act = (pre * phi).astype(BF16)
    act_ref[...] = act
    slope = phi + pre * (0.3989422804014327 * jnp.exp(-0.5 * pre * pre))
    slope_ref[...] = slope.astype(BF16)
    part_ref[...] = dot(act, down_ref[0])


def mlp(flags, rows_all, vec, up, bias, down, block, late):
    rows, dim = rows_all.shape
    hidden = up.shape[2]
    return pl.pallas_call(
        functools.partial(mlp_kernel, (up.at, down.at), len(up.arrays)),
        grid=(rows // block,),
        in_specs=[
            pl.BlockSpec(memory_space=pltpu.SMEM), row_block(block, dim), whole(vec), whole(bias),
            pl.BlockSpec(memory_space=pl.ANY),
        ]
        + up.specs()
        + down.specs(),
        out_specs=[
            row_block(block, dim), row_block(block, hidden), row_block(block, hidden),
            row_block(block, dim),
        ],
        out_shape=[
            jax.ShapeDtypeStruct((rows, dim), BF16),
            jax.ShapeDtypeStruct((rows, hidden), BF16),
            jax.ShapeDtypeStruct((rows, hidden), BF16),
            jax.ShapeDtypeStruct((rows, dim), F32),
        ],
        scratch_shapes=[up.scratch(), down.scratch()],
        compiler_params=params(),
        cost_estimate=brief(),
        name="mlp",
    )(flags, rows_all, vec, bias, late, *up.arrays, *down.arrays)


def gather_pieces(pieces, parts, row_ref, col_ref, size, out_ref):
    full = out_ref.shape[1] // parts
    ranks = row_ref.shape[0]
    count = len(pieces) // ranks
    for index, piece in enumerate(pieces):
        r, p = index % ranks, index // ranks
        rows = pl.ds(pl.multiple_of(row_ref[r] * size, size), size)
        for part in range(parts):
            values = piece[:, part * GROUP : (part + 1) * GROUP]
            if count * GROUP == full:
                out_ref[rows, part * full + p * GROUP : part * full + (p + 1) * GROUP] = values
            else:
                column = part * full + (col_ref[r] * count + p) * GROUP
                out_ref[rows, pl.ds(pl.multiple_of(column, GROUP), GROUP)] = values


def out_kernel(at, weights, count, flag_ref, row_ref, col_ref, down_ref, late_ref, *refs):
    pieces = refs[weights : weights + count]
    attended_ref, out_ref, w_ref = refs[-3:]
    once((at, flag_ref, refs[:weights], w_ref))
    i = pl.program_id(0)
    block = out_ref.shape[0]

    @pl.when(i == 0)
    def _():
        gather_pieces(pieces, 1, row_ref, col_ref, block, attended_ref)

    rows = pl.ds(pl.multiple_of(i * block, block), block)
    out_ref[...] = (down_ref[...] + dot(attended_ref[rows, :], w_ref[0])).astype(BF16)


def out_partial(flags, row_at, col_at, pieces, down_part, weight, block, late):
    rows, dim = down_part.shape
    width = weight.shape[1]
    return pl.pallas_call(
        functools.partial(out_kernel, weight.at, len(weight.arrays), len(pieces)),
        grid_spec=pltpu.PrefetchScalarGridSpec(
            num_scalar_prefetch=3,
            grid=(rows // block,),
            in_specs=[row_block(block, dim), pl.BlockSpec(memory_space=pl.ANY)]
            + weight.specs()
            + [whole(p) for p in pieces],
            out_specs=[fixed((rows, width)), row_block(block, dim)],
            scratch_shapes=[weight.scratch()],
        ),
        out_shape=[
            jax.ShapeDtypeStruct((rows, width), BF16),
            jax.ShapeDtypeStruct((rows, dim), BF16),
        ],
        compiler_params=params(),
        cost_estimate=brief(),
        name="out_partial",
    )(flags, row_at, col_at, down_part, late, *weight.arrays, *pieces)


def pair_bias(start_ref, first, size, keys):
    query_at = lax.broadcasted_iota(jnp.int32, (size, keys), 0) + first
    key_at = lax.broadcasted_iota(jnp.int32, (size, keys), 1)
    allowed = (key_at <= query_at) & (key_at >= start_ref[first : first + size, :])
    return jnp.where(allowed, 0.0, -MASK_FILL)


def attn_fwd_kernel(at, pos_ref, start_ref, late_ref, *refs):
    count = len(at)
    blocks, outs = [ref.at[p] for ref, p in zip(refs, at)], refs[count : 2 * count]
    q_ref, k_ref, v_ref, lse_ref, o_ref = refs[2 * count :]
    size, width = outs[0].shape
    for r in range(count):
        rows = pl.ds(pl.multiple_of(pos_ref[r] * size, size), size)
        q_ref[rows, :] = blocks[r][:, :width]
        k_ref[rows, :] = blocks[r][:, width : 2 * width]
        v_ref[rows, :] = blocks[r][:, 2 * width :]
    group = lax.broadcasted_iota(jnp.int32, (1, width), 1) // HEAD
    lane = lax.broadcasted_iota(jnp.int32, (1, 128), 1)
    zero, unit = jnp.zeros((), BF16), jnp.ones((), BF16)
    for i in range(count):
        first, keys = i * size, (i + 1) * size
        bias = pair_bias(start_ref, first, size, keys)
        query = q_ref[first:keys, :]
        total = jnp.zeros((size, width), F32)
        tops = jnp.zeros((size, 128), F32)
        for head in range(width // HEAD):
            mine = group == head
            other = HEAD if head == 0 else 0
            scores = dot(jnp.where(mine, query, zero), k_ref[:keys, :], 1, 1) + bias
            top = jnp.max(scores, axis=-1, keepdims=True)
            terms = jnp.exp(scores - top).astype(BF16)
            mixed = dot(terms, jnp.where(mine, v_ref[:keys, :], unit))
            row_sum = mixed[:, other : other + 1]
            total = jnp.where(mine, mixed * (1.0 / row_sum), total)
            tops = jnp.where(lane == head, top + jnp.log(row_sum), tops)
        o_ref[first:keys, :] = total
        lse_ref[first:keys, :] = tops
    for r in range(count):
        rows = pl.ds(pl.multiple_of(pos_ref[r] * size, size), size)
        outs[r][...] = o_ref[rows, :].astype(BF16)


def attend(pos, start_col, blocks, late):
    count = len(blocks)
    size, wide = blocks[0][0].shape[1:]
    width, length = wide // 3, size * count
    vmem = pl.BlockSpec(memory_space=pltpu.VMEM)
    result = pl.pallas_call(
        functools.partial(attn_fwd_kernel, tuple(p for _, p in blocks)),
        in_specs=[pl.BlockSpec(memory_space=pltpu.SMEM), vmem, pl.BlockSpec(memory_space=pl.ANY)]
        + [vmem] * count,
        out_specs=[vmem] * (count + 4),
        out_shape=[jax.ShapeDtypeStruct((size, width), BF16)] * count
        + [jax.ShapeDtypeStruct((length, width), BF16)] * 3
        + [jax.ShapeDtypeStruct((length, 128), F32)],
        scratch_shapes=[pltpu.VMEM((length, width), F32)],
        compiler_params=params(),
        cost_estimate=brief(),
        name="attend",
    )(pos, start_col, late, *(array for array, _ in blocks))
    return list(result[:count]), result[count:]


def attn_bwd_kernel(at, pos_ref, start_ref, late_ref, q_ref, k_ref, v_ref, lse_ref, cos_ref, sin_ref, *refs):
    count = len(at)
    blocks, outs = [ref.at[p] for ref, p in zip(refs, at)], refs[count : 2 * count]
    do_ref, dq_ref, dk_ref, dv_ref = refs[2 * count :]
    size, width = blocks[0].shape
    for r in range(count):
        rows = pl.ds(pl.multiple_of(pos_ref[r] * size, size), size)
        do_ref[rows, :] = blocks[r][...]
    dk_ref[...] = jnp.zeros_like(dk_ref)
    dv_ref[...] = jnp.zeros_like(dv_ref)
    group = lax.broadcasted_iota(jnp.int32, (1, width), 1) // HEAD
    zero = jnp.zeros((), BF16)
    for i in range(count):
        first, keys = i * size, (i + 1) * size
        bias = pair_bias(start_ref, first, size, keys)
        query, grad_out = q_ref[first:keys, :], do_ref[first:keys, :]
        query_t, grad_out_t = query.T, grad_out.T
        total = jnp.zeros((size, width), F32)
        for head in range(width // HEAD):
            mine = group == head
            rows = slice(head * HEAD, (head + 1) * HEAD)
            scores = dot(jnp.where(mine, query, zero), k_ref[:keys, :], 1, 1) + bias
            probs = jnp.exp(scores - lse_ref[first:keys, head : head + 1])
            grad_prob = dot(jnp.where(mine, grad_out, zero), v_ref[:keys, :], 1, 1)
            delta = jnp.sum(probs * grad_prob, axis=-1, keepdims=True)
            grad_score = (probs * (grad_prob - delta)).astype(BF16)
            total = total + dot(grad_score, jnp.where(mine, k_ref[:keys, :], zero))
            dk_ref[rows, :keys] += dot(query_t[rows, :], grad_score)
            dv_ref[rows, :keys] += dot(grad_out_t[rows, :], probs.astype(BF16))
        dq_ref[first:keys, :] = total * SCORE_SCALE
    dk = dk_ref[...].T
    dv = dv_ref[...].T
    cosine, sine = cos_ref[...], sin_ref[...]
    key_grad = dk * cosine - swap_halves(dk) * sine
    grad = dq_ref[...]
    dq_ref[...] = grad * cosine - swap_halves(grad) * sine
    do_ref[...] = dv.astype(BF16)
    for r in range(count):
        rows = pl.ds(pl.multiple_of(pos_ref[r] * size, size), size)
        outs[r][:, :width] = dq_ref[rows, :].astype(BF16)
        outs[r][:, 2 * width :] = do_ref[rows, :]
    dq_ref[...] = key_grad
    for r in range(count):
        rows = pl.ds(pl.multiple_of(pos_ref[r] * size, size), size)
        outs[r][:, width : 2 * width] = dq_ref[rows, :].astype(BF16)


def attend_back(pos, start_col, kept, cosine, sine, blocks, late, weight):
    count = len(blocks)
    size, width = blocks[0][0].shape[1:]
    length = size * count
    vmem = pl.BlockSpec(memory_space=pltpu.VMEM)
    return pl.pallas_call(
        functools.partial(attn_bwd_kernel, tuple(p for _, p in blocks)),
        in_specs=[pl.BlockSpec(memory_space=pltpu.SMEM), vmem, pl.BlockSpec(memory_space=pl.ANY)]
        + [vmem] * 6
        + [vmem] * count,
        out_specs=[vmem] * count,
        out_shape=[jax.ShapeDtypeStruct((size, 3 * width), BF16)] * count,
        scratch_shapes=[pltpu.VMEM((length, width), BF16), pltpu.VMEM((length, width), F32)]
        + [pltpu.VMEM((width, length), F32)] * 2,
        compiler_params=params(),
        cost_estimate=brief(weight),
        name="attend_back",
    )(pos, start_col, late, *kept, cosine, sine, *(array for array, _ in blocks))


def add_sums(i, ref, values):
    sums = [jnp.sum(value, axis=0, keepdims=True) for value in values]
    sums += [jnp.zeros_like(sums[0])] * (8 - len(sums))
    share = jnp.concatenate(sums, axis=0)

    @pl.when(i == 0)
    def _():
        ref[...] = share

    @pl.when(i > 0)
    def _():
        ref[...] += share


def mlp_back_kernel(ats, weights, flag_ref, x_ref, cot_ref, slope_ref, vec_ref, *refs):
    pre_ref, two_ref, grads_ref, bias_ref, down_ref, up_ref = refs[-6:]
    once(
        (ats[0], flag_ref, refs[:weights], down_ref),
        (ats[1], flag_ref, refs[weights : 2 * weights], up_ref),
    )
    i = pl.program_id(0)
    grad_act = dot(cot_ref[...], down_ref[0], 1, 1)
    grad_pre = (grad_act * slope_ref[...].astype(F32)).astype(BF16)
    pre_ref[...] = grad_pre
    two = dot(grad_pre, up_ref[0], 1, 1)
    hat, _ = norm_rows(x_ref[...].astype(F32))
    two_ref[...] = two * vec_ref[2:3, :]
    add_sums(i, grads_ref, (two * hat, two))
    add_sums(i, bias_ref, (grad_pre.astype(F32),))


def mlp_back(flags, rows_all, cot_all, slope, down, up, vec, block, late):
    rows, dim = rows_all.shape
    hidden = slope.shape[1]
    return pl.pallas_call(
        functools.partial(mlp_back_kernel, (down.at, up.at), len(up.arrays)),
        grid=(rows // block,),
        in_specs=[
            pl.BlockSpec(memory_space=pltpu.SMEM), row_block(block, dim), row_block(block, dim),
            row_block(block, hidden), whole(vec),
        ]
        + down.specs()
        + up.specs()
        + [pl.BlockSpec(memory_space=pl.ANY)] * len(late),
        out_specs=[
            row_block(block, hidden), row_block(block, dim), fixed((8, dim)), fixed((8, hidden)),
        ],
        out_shape=[
            jax.ShapeDtypeStruct((rows, hidden), BF16),
            jax.ShapeDtypeStruct((rows, dim), F32),
            jax.ShapeDtypeStruct((8, dim), F32),
            jax.ShapeDtypeStruct((8, hidden), F32),
        ],
        scratch_shapes=[down.scratch(), up.scratch()],
        compiler_params=params(),
        cost_estimate=brief(8),
        name="mlp_back",
    )(flags, rows_all, cot_all, slope, vec, *down.arrays, *up.arrays, *late)


def input_grad_kernel(
    at, weights, count, flag_ref, row_ref, col_ref, x_ref, two_ref, vec_ref, *refs
):
    pieces = refs[weights : weights + count]
    dlin_ref, sum_ref, grads_ref, bias_ref, w_ref = refs[-5:]
    once((at, flag_ref, refs[:weights], w_ref))
    width = w_ref.shape[2]
    block = x_ref.shape[0]
    i = pl.program_id(0)

    @pl.when(i == 0)
    def _():
        gather_pieces(pieces, 3, row_ref, col_ref, block, dlin_ref)

    rows = pl.ds(pl.multiple_of(i * block, block), block)
    hat, _ = norm_rows(x_ref[...].astype(F32))
    dlin = dlin_ref[rows, :]
    one = dot(dlin[:, :width], w_ref[0], 1, 1)
    for part in (1, 2):
        one = one + dot(dlin[:, part * width : (part + 1) * width], w_ref[part], 1, 1)
    sum_ref[...] = (one * vec_ref[0:1, :] + two_ref[...]).astype(BF16)
    add_sums(i, grads_ref, (one * hat, one))
    add_sums(i, bias_ref, (dlin.astype(F32),))


def input_grad(flags, row_at, col_at, rows_all, pieces, weight, two_part, vec, block):
    rows, dim = rows_all.shape
    wide = 3 * weight.shape[2]
    return pl.pallas_call(
        functools.partial(input_grad_kernel, weight.at, len(weight.arrays), len(pieces)),
        grid_spec=pltpu.PrefetchScalarGridSpec(
            num_scalar_prefetch=3,
            grid=(rows // block,),
            in_specs=[row_block(block, dim), row_block(block, dim), whole(vec)]
            + weight.specs()
            + [whole(p) for p in pieces],
            out_specs=[
                fixed((rows, wide)), row_block(block, dim), fixed((8, dim)), fixed((8, wide)),
            ],
            scratch_shapes=[weight.scratch()],
        ),
        out_shape=[
            jax.ShapeDtypeStruct((rows, wide), BF16),
            jax.ShapeDtypeStruct((rows, dim), BF16),
            jax.ShapeDtypeStruct((8, dim), F32),
            jax.ShapeDtypeStruct((8, wide), F32),
        ],
        compiler_params=params(),
        cost_estimate=brief(),
        name="input_grad",
    )(flags, row_at, col_at, rows_all, two_part, vec, *weight.arrays, *pieces)


def by_xor(axis, count, step):
    return functools.partial(
        lax.ppermute, axis_name=axis, perm=[(i, i ^ step) for i in range(count)]
    )


def nothing(*refs):
    del refs


def after(values, *others):
    anywhere = pl.BlockSpec(memory_space=pl.ANY)
    return pl.pallas_call(
        nothing,
        in_specs=[anywhere] * (1 + len(others)),
        out_specs=anywhere,
        out_shape=jax.ShapeDtypeStruct(values.shape, values.dtype),
        input_output_aliases={0: 0},
        name="after",
    )(values, *others)


def first_token(values):
    def copy(source, target):
        target[...] = source[...]

    return pl.pallas_call(
        copy, out_shape=jax.ShapeDtypeStruct(values.shape, values.dtype), name="first"
    )(values)


class Weight:
    def __init__(self, own, at, token, shards, ranks):
        self.at, shape = at, list(own.shape)
        shape[at] *= shards
        self.shape = tuple(shape)
        if shards == 2 and ranks > 1:
            half = own.shape[1] // 2
            odd = lax.axis_index("ctx") & 1
            mine = lax.dynamic_slice_in_dim(own, odd * half, half, 1)
            mine = by_xor("shard", 2, 1)(after(mine, token))
            self.arrays = [own, mine, by_xor("ctx", ranks, 1)(mine)]
            self.token = mine
        else:
            self.arrays = [lax.all_gather(own, "shard", axis=at, tiled=True)]
            self.token = token

    def specs(self):
        return [whole(a) for a in self.arrays]

    def scratch(self):
        return pltpu.VMEM(self.shape, BF16)


def join(at, flag_ref, refs, full_ref):
    if len(refs) == 1:
        full_ref[...] = refs[0][...]
        return
    rows, cols = refs[0].shape[1:]
    half = rows // 2
    side, odd = flag_ref[0], flag_ref[1] & 1
    for where, first, ref in (
        (side, 0, refs[0]), (1 - side, odd * half, refs[1]), (1 - side, (1 - odd) * half, refs[2]),
    ):
        if at == 1:
            place = pl.ds(pl.multiple_of(where * rows + first, half), ref.shape[1])
            full_ref[:, place, :] = ref[...]
        else:
            place = pl.ds(pl.multiple_of(first, half), ref.shape[1])
            full_ref[:, place, pl.ds(pl.multiple_of(where * cols, cols), cols)] = ref[...]


def once(*joins):
    @pl.when(pl.program_id(0) == 0)
    def _():
        for args in joins:
            join(*args)


def halve(values, dim, axis, count, bit):
    mine = (lax.axis_index(axis) >> bit) & 1
    away = lax.dynamic_index_in_dim(values, 1 - mine, dim, keepdims=False)
    keep = lax.dynamic_index_in_dim(values, mine, dim, keepdims=False)
    return keep + by_xor(axis, count, 1 << bit)(away)


def axis_bits(axes):
    return [
        (axis, count, bit)
        for axis, count in axes
        for bit in reversed(range(count.bit_length() - 1))
    ]


def scatter_small(values, axes, order):
    bits = axis_bits(axes)
    values = values.reshape((2,) * len(bits) + (-1,) + values.shape[1:])
    for name in order:
        for entry in [e for e in reversed(bits) if e[0] == name]:
            values = halve(values, bits.index(entry), *entry)
            bits.remove(entry)
    return values


def split_kernel(outer, terms, bit_ref, *refs):
    sources, (away_ref, keep_ref) = refs[:terms], refs[-2:]
    size = away_ref.shape[0] // outer
    for a in range(outer):
        for ref, half in ((away_ref, 1 - bit_ref[0]), (keep_ref, bit_ref[0])):
            rows = pl.ds(pl.multiple_of((2 * a + half) * size, size), size)
            total = sources[0][rows, :].astype(F32)
            for source in sources[1:]:
                total = total + source[rows, :].astype(F32)
            ref[a * size : (a + 1) * size, :] = total.astype(BF16)


def halve_rows(terms, bits, entry):
    rows, wide = terms[0].shape
    vmem = pl.BlockSpec(memory_space=pltpu.VMEM)
    half = jax.ShapeDtypeStruct((rows // 2, wide), BF16)
    axis, count, bit = entry
    away, keep = pl.pallas_call(
        functools.partial(split_kernel, 1 << bits.index(entry), len(terms)),
        in_specs=[pl.BlockSpec(memory_space=pltpu.SMEM)] + [vmem] * len(terms),
        out_specs=[vmem, vmem],
        out_shape=[half, half],
        compiler_params=params(),
        cost_estimate=brief(),
        name="split",
    )(((lax.axis_index(axis) >> bit) & 1)[None], *terms)
    bits.remove(entry)
    return [keep, by_xor(axis, count, 1 << bit)(away)]


def quarters_kernel(flag_ref, keep_ref, came_ref, *refs):
    outs = refs[-4:]
    size = outs[0].shape[0]
    mine = flag_ref[0] * 2 + flag_ref[1] // 2
    for step, out in enumerate(outs):
        rows = pl.ds(pl.multiple_of((mine ^ step) * size, size), size)
        out[...] = (keep_ref[rows, :].astype(F32) + came_ref[rows, :].astype(F32)).astype(BF16)


def exchange_quarters(flags, terms, late):
    rows, wide = terms[0].shape
    vmem = pl.BlockSpec(memory_space=pltpu.VMEM)
    outs = pl.pallas_call(
        quarters_kernel,
        in_specs=[pl.BlockSpec(memory_space=pltpu.SMEM), vmem, vmem]
        + [pl.BlockSpec(memory_space=pl.ANY)] * len(late),
        out_specs=[vmem] * 4,
        out_shape=[jax.ShapeDtypeStruct((rows // 4, wide), BF16)] * 4,
        compiler_params=params(),
        cost_estimate=brief(),
        name="quarters",
    )(flags, *terms, *late)
    came = [outs[0]]
    for step in range(1, 4):
        perm = [(s * 4 + c, (s ^ (step >> 1)) * 4 + (c ^ ((step & 1) * 2))) for s in range(2) for c in range(4)]
        came.append(lax.ppermute(outs[step], ("shard", "ctx"), perm))
    return came, outs[0]


def group_kernel(count, small, flag_ref, *refs):
    lefts, rights = refs[0 : 2 * count : 2], refs[1 : 2 * count : 2]
    away_ref, keep_ref = refs[-2:]
    i = pl.program_id(0)
    core = jnp.where(i == 0, 1 - (flag_ref[1] & 1), flag_ref[1] & 1)

    def columns(ref, axis):
        parts = []
        for j in range(ref.shape[1] // 256):
            part = ref[:, pl.ds(pl.multiple_of((2 * j + core) * 128, 128), 128)]
            if axis == 0:
                part = jnp.concatenate([part, jnp.zeros((128 - part.shape[0], 128), F32)], axis=0).T
            parts.append(part)
        return jnp.concatenate(parts, axis=axis)

    first = 0
    values = []
    for left, right in zip(lefts, rights):
        values.append(dot(columns(left, 1), right[...], 0, 0).astype(BF16))
    if small:
        values.append(columns(refs[2 * count], 0).astype(BF16))
    for value in values:
        last = first + value.shape[1]

        @pl.when(i == 0)
        def _(value=value, first=first, last=last):
            away_ref[:, first:last] = value

        @pl.when(i > 0)
        def _(value=value, first=first, last=last):
            keep_ref[:, first:last] = value

        first = last


def group_grad(flags, pairs, small, axes, late):
    dim = pairs[0][0].shape[1]
    owners = 1
    for _, count in axes:
        owners *= count
    bits = axis_bits(axes)
    wide = sum(right.shape[1] for _, right in pairs) + (0 if small is None else 128)
    if dim // owners != 128:
        values = [dot(left, right, 0, 0).astype(BF16) for left, right in pairs]
        if small is not None:
            values.append(jnp.pad(small.T, ((0, 0), (0, 120))).astype(BF16))
        return halve_rows([jnp.concatenate(values, axis=1)], bits, bits[-1]), bits
    half = jax.ShapeDtypeStruct((dim // 2, wide), BF16)
    flat = [a for pair in pairs for a in pair] + ([] if small is None else [small])
    away, keep = pl.pallas_call(
        functools.partial(group_kernel, len(pairs), small is not None),
        grid=(2,),
        in_specs=[pl.BlockSpec(memory_space=pltpu.SMEM)] + [whole(a) for a in flat]
        + [pl.BlockSpec(memory_space=pl.ANY)] * len(late),
        out_specs=[fixed(half.shape), fixed(half.shape)],
        out_shape=[half, half],
        compiler_params=params(),
        cost_estimate=brief(),
        name="group_grad",
    )(flags, *flat, *late)
    return [keep, by_xor("ctx", dict(axes)["ctx"], 1)(away)], bits[:-1]


def scatter_group(flags, terms, bits, late):
    if len(bits) == 2:
        return exchange_quarters(flags, terms, late)
    bits = list(bits)
    while bits:
        terms = halve_rows(terms, bits, bits[-1])
    return terms, terms[0]


def total_kernel(terms, layouts, *refs):
    outs = refs[len(refs) - len(layouts) :]
    first = 0
    for out, (kind, wide) in zip(outs, layouts):
        cols = slice(first, first + wide)
        total = refs[0][:, cols].astype(F32)
        for ref in refs[1:terms]:
            total = total + ref[:, cols].astype(F32)
        if kind == "flip":
            out[...] = total.T
        elif kind == "small":
            out[...] = total.T[:8, :]
        elif kind == "three":
            for part in range(3):
                out[part] = total[:, part * wide // 3 : (part + 1) * wide // 3]
        else:
            out[...] = total
        first += wide


def group_total(terms, layouts, late):
    rows = terms[0].shape[0]
    shapes = {
        "flip": lambda w: (w, rows), "small": lambda w: (8, rows),
        "three": lambda w: (3, rows, w // 3), "keep": lambda w: (rows, w),
    }
    vmem = pl.BlockSpec(memory_space=pltpu.VMEM)
    return pl.pallas_call(
        functools.partial(total_kernel, len(terms), layouts),
        in_specs=[vmem] * len(terms) + [pl.BlockSpec(memory_space=pl.ANY)] * len(late),
        out_specs=[vmem] * len(layouts),
        out_shape=[jax.ShapeDtypeStruct(shapes[kind](w), F32) for kind, w in layouts],
        compiler_params=params(),
        cost_estimate=brief(3),
        name="group_total",
    )(*terms, *late)


def body(
    sizes, hidden_in, w_qkv, bias_qkv, w_dense, w_up, bias_up, w_down, vectors, block_deal,
    segments, cotangent,
):
    shards, ranks, tps = sizes
    rank = lax.axis_index("ctx")
    dim = hidden_in.shape[1]
    own_rows = hidden_in.shape[0]

    x_all = lax.all_gather(hidden_in, "tp", axis=0, tiled=True)
    heads = bias_qkv.shape[1]
    width = heads * HEAD
    half = vectors.shape[1]
    small = jnp.concatenate(
        [vectors.reshape(-1), bias_qkv.astype(F32).reshape(-1), bias_up.astype(F32).reshape(-1)]
    )
    pad = -small.shape[0] % 1024
    small = jnp.pad(small, (0, pad)).reshape(1, -1, 128)
    token = first_token(segments)
    if shards == 2:
        other = by_xor("shard", 2, 1)(small)
        first = lax.axis_index("shard") == 0
        small = jnp.concatenate([jnp.where(first, small, other), jnp.where(first, other, small)])
    else:
        small = lax.all_gather(small, "shard", axis=0, tiled=True)
    small = small.reshape(shards, -1)
    cut = 6 * half
    vec = small[:, :cut].reshape(shards, 6, half).transpose(1, 0, 2).reshape(6, dim)
    vec = jnp.pad(vec, ((0, 2), (0, 0)))
    share = bias_qkv.size
    qkv_bias = small[:, cut : cut + share].reshape((shards,) + bias_qkv.shape)
    qkv_bias = qkv_bias.transpose(1, 2, 0, 3).reshape(3, width)
    up_bias = small[:, cut + share : cut + share + bias_up.size].reshape((shards,) + bias_up.shape)
    up_bias = up_bias.transpose(1, 0, 2).reshape(1, -1)
    flags = jnp.stack([lax.axis_index("shard"), rank])
    weight_qkv = Weight(w_qkv, 1, token, shards, ranks)
    weight_up = Weight(w_up[None], 1, token, shards, ranks)
    weight_down = Weight(w_down[None], 2, token, shards, ranks)
    weight_dense = Weight(w_dense[None], 2, token, shards, ranks)

    deal = block_deal[0]
    seg_row = segments[0]
    group = seg_row.shape[0]
    block = group // deal.shape[0]
    quarters = deal.shape[0] // ranks
    rank_rows = quarters * block
    split = ranks // quarters
    pieces = width // split // GROUP
    length = group // quarters
    at = jnp.arange(group, dtype=jnp.int32)
    previous = jnp.concatenate([seg_row[:1] - 1, seg_row[:-1]])
    begins = lax.cummax(jnp.where(seg_row != previous, at, 0), axis=0)
    places = (at - begins).reshape(deal.shape[0], block)
    deal_by_rank = deal.reshape(ranks, quarters)
    my_deal = lax.dynamic_index_in_dim(deal_by_rank, rank, 0, keepdims=False)
    picked = my_deal[:, None] == jnp.arange(deal.shape[0], dtype=jnp.int32)[None, :]
    rank_place = jnp.sum(jnp.where(picked[:, :, None], places[None], 0), axis=1).reshape(-1)
    quarter = rank // split
    partners = rank ^ jnp.arange(ranks, dtype=jnp.int32)
    in_quarter = jnp.take(lax.dynamic_index_in_dim(deal_by_rank, quarter, 1, keepdims=False), partners)
    pos = in_quarter - quarter * ranks
    my_begins = lax.dynamic_slice_in_dim(begins, quarter * length, length) - quarter * length
    quarter_place = jnp.arange(length, dtype=jnp.int32) - my_begins
    start_col = my_begins[:, None]
    lane = jnp.arange(128, dtype=jnp.int32) % HEAD
    frequency = ROPE_BASE ** (-2.0 * (lane % (ROT // 2)).astype(F32) / ROT)
    frequency = jnp.where(lane < ROT, frequency, 0.0)
    sign = jnp.where(lane < ROT // 2, -1.0, 1.0)
    all_places = jnp.concatenate([rank_place, quarter_place]).astype(F32)
    angles = all_places[:, None] * frequency[None, :]
    cosine, sine = jnp.cos(angles), jnp.sin(angles) * sign[None, :]
    target_row, target_col = partners // split, partners % split

    ready = after(cotangent, vec, qkv_bias, up_bias, cosine, sine, start_col, pos)
    cot_all = lax.all_gather(ready, "tp", axis=0, tiled=True)

    full_one, sent = project(
        flags, split, ranks, x_all, vec, weight_qkv, qkv_bias, cosine[:rank_rows],
        sine[:rank_rows], block, weight_up.arrays + weight_down.arrays + weight_dense.arrays,
    )

    def swap(sent):
        return [by_xor("ctx", ranks, s)(piece) if s else piece for s, piece in enumerate(sent)]

    arrived = exchange(sent, pieces, ranks, 2)
    full_two, activated, slope, down_part = mlp(
        flags, x_all, vec, weight_up, up_bias, weight_down, block, sent[0]
    )
    out_pieces, kept, late = [], [], down_part
    for p in range(pieces):
        out, keep = attend(pos, start_col, arrived[p], late)
        if p:
            out = [out[0], after(out[1], *out_pieces[-ranks:])] + out[2:]
        out_pieces += swap(out)
        kept.append(keep)
        late = out[0]

    axes = (("shard", shards), ("ctx", ranks))
    tables = (cosine[rank_rows:], sine[rank_rows:])
    sent = attn_grad(flags, split, ranks, cot_all, weight_dense, block, out_pieces)
    arrived = exchange(sent, pieces, ranks, ranks)
    attended, partial = out_partial(
        flags, target_row, target_col, out_pieces, down_part, weight_dense, block, arrived[0][1][0]
    )
    summed = lax.psum_scatter(partial, "tp", scatter_dimension=0, tiled=True)
    grad_pieces, late = [], partial
    for p in range(pieces):
        grads = attend_back(pos, start_col, kept[p], *tables, arrived[p], late, 0 if p else 300)
        grad_pieces += swap(grads)
        late = grads[0]
    grad_pre, two_part, two_sums, grad_ubias = mlp_back(
        flags, x_all, cot_all, slope, weight_down, weight_up, vec, block,
        grad_pieces[: ranks * (pieces - 1)] + [late],
    )
    dlin, row_sum, one_sums, grad_qbias = input_grad(
        flags, target_row, target_col, x_all, grad_pieces, weight_qkv, two_part, vec, block
    )
    own_sum = lax.psum_scatter(after(row_sum, summed), "tp", scatter_dimension=0, tiled=True)

    first, bits = group_grad(flags, [(cot_all, activated), (cot_all, attended)], None, axes, (dlin,))
    second, _ = group_grad(flags, [(full_two, grad_pre)], None, axes, (first[0],))
    first, late = scatter_group(flags, first, bits, (second[0],))
    owners = shards * ranks
    each, share = HEAD // owners, dim // owners

    def by_owner(row, lines):
        row = row.reshape(lines, owners, each).transpose(1, 0, 2).reshape(owners, -1)
        return jnp.pad(row, ((0, 0), (0, share - lines * each))).reshape(1, dim)

    cot_rows = cotangent.astype(F32)
    cot_sum = jnp.sum(cot_rows, axis=0, keepdims=True)
    small_rows = jnp.concatenate(
        [
            one_sums[:2], two_sums[:2], cot_sum, cot_sum,
            by_owner(grad_qbias[0], 3 * heads), by_owner(grad_ubias[0], bias_up.shape[0]),
        ],
        axis=0,
    )
    third, _ = group_grad(flags, [(full_one, dlin)], small_rows, axes, (late,))
    second, late = scatter_group(flags, second, bits, (third[0],))
    hidden, wide = weight_up.shape[2], 3 * width
    grad_down, grad_dense = group_total(first, (("flip", hidden), ("flip", width)), (late,))
    third, late = scatter_group(flags, third, bits, (grad_dense,))
    (grad_up,) = group_total(second, (("keep", hidden),), (late,))
    grad_qkv, small_rows = group_total(third, (("three", wide), ("small", 128)), (grad_up,))
    grad_vec = scatter_small(small_rows[:6].T, (("tp", tps),), ("tp",)).T
    grad_qbias = small_rows[6, : 3 * heads * each].reshape(3, heads, each)
    grad_ubias = small_rows[7, : bias_up.shape[0] * each].reshape(bias_up.shape[0], each)

    rows_in = hidden_in.astype(F32)
    output = (rows_in + summed.astype(F32) + vec[4:5] + vec[5:6]).astype(BF16)
    own_sum = after(own_sum, grad_qkv).astype(F32)
    hat, inverse = norm_rows(rows_in)
    centered = own_sum - jnp.mean(own_sum, axis=-1, keepdims=True)
    along = jnp.mean(own_sum * hat, axis=-1, keepdims=True)
    grad_in = (cot_rows + inverse * (centered - hat * along)).astype(BF16)
    return (
        output, grad_in, grad_qkv, grad_qbias, grad_dense, grad_up, grad_ubias, grad_down,
        grad_vec,
    )


def solution(mesh):
    sizes = tuple(mesh.shape[name] for name in ("shard", "ctx", "tp"))
    return jax.shard_map(
        functools.partial(body, sizes),
        mesh=mesh,
        in_specs=(
            P(("shard", "ctx", "tp"), None),
            P(None, "shard", "tp"),
            P(None, "tp", "shard"),
            P("tp", "shard"),
            P("shard", "tp"),
            P("tp", "shard"),
            P("tp", "shard"),
            P(None, "shard"),
            P("shard", None),
            P("shard", None),
            P(("shard", "ctx", "tp"), None),
        ),
        out_specs=(
            P(("shard", "ctx", "tp"), None),
            P(("shard", "ctx", "tp"), None),
            P(None, ("shard", "ctx"), "tp"),
            P(None, "tp", ("shard", "ctx")),
            P("tp", ("shard", "ctx")),
            P(("shard", "ctx"), "tp"),
            P("tp", ("shard", "ctx")),
            P("tp", ("shard", "ctx")),
            P(None, ("shard", "ctx", "tp")),
        ),
        check_vma=False,
    )
```

```python
import functools

import jax
import jax.numpy as jnp
from jax import lax
from jax.experimental import pallas as pl
from jax.experimental.pallas import tpu as pltpu
from jax.sharding import PartitionSpec as P

HEAD = 64
GROUP = 128
ROT = 16
NORM_EPS = 1e-05
SCORE_SCALE = 0.125
ROPE_BASE = 10000.0
MASK_FILL = 1e30
F32 = jnp.float32
BF16 = jnp.bfloat16


def dot(left, right, left_dim=1, right_dim=0):
    return lax.dot_general(
        left, right, (((left_dim,), (right_dim,)), ((), ())), preferred_element_type=F32
    )


def params(mib=20):
    return pltpu.CompilerParams(vmem_limit_bytes=mib * 1024 * 1024)


def brief(us=0):
    return pl.CostEstimate(flops=int(us * 1.1e9) + 1, bytes_accessed=1, transcendentals=0)


def swap_halves(values):
    width = values.shape[-1]
    lane = lax.broadcasted_iota(jnp.int32, (1, width), 1) % HEAD
    ahead = pltpu.roll(values, width - ROT // 2, 1)
    behind = pltpu.roll(values, ROT // 2, 1)
    return jnp.where(lane < ROT // 2, ahead, behind)


def widen(table, width):
    return jnp.concatenate([table] * (width // table.shape[-1]), axis=-1)


def norm_rows(rows):
    center = rows - jnp.mean(rows, axis=-1, keepdims=True)
    inverse = lax.rsqrt(jnp.mean(center * center, axis=-1, keepdims=True) + NORM_EPS)
    return center * inverse, inverse


def whole(array):
    return pl.BlockSpec(
        array.shape, lambda *ids: (0,) * array.ndim, pipeline_mode=pl.Buffered(buffer_count=1)
    )


def in_hbm(array):
    return pltpu.with_memory_space_constraint(array, pltpu.HBM)


def row_block(block, cols):
    return pl.BlockSpec((block, cols), lambda i, *ids: (i, 0))


def piece_shapes(pieces, ranks, merged, shape):
    shapes = []
    for step in range(ranks):
        if 0 < step < merged:
            shapes.append((pieces,) + shape)
        else:
            shapes += [(1,) + shape] * pieces
    return shapes


def by_step(flat, pieces, ranks, merged):
    steps, at = [], 0
    for step in range(ranks):
        count = 1 if 0 < step < merged else pieces
        steps.append(flat[at : at + count])
        at += count
    return steps


def send_pieces(i, split, merged, flag_ref, flat, groups_ref, ranks):
    pieces = groups_ref.shape[0] // split
    for step, refs in enumerate(by_step(flat, pieces, ranks, merged)):

        @pl.when(i == step // split)
        def _(step=step, refs=refs):
            for p in range(pieces):
                group = p
                if split > 1:
                    group = ((flag_ref[1] ^ step) % split) * pieces + p
                if len(refs) == 1:
                    refs[0][p] = groups_ref[group]
                else:
                    refs[p][0] = groups_ref[group]


def exchange(flat, pieces, ranks, merged):
    came = [[] for _ in range(pieces)]
    for step, arrays in enumerate(by_step(flat, pieces, ranks, merged)):
        if step:
            arrays = [by_xor("ctx", ranks, step)(array) for array in arrays]
        for p in range(pieces):
            came[p].append((arrays[0], p) if len(arrays) == 1 else (arrays[p], 0))
    return came


def quarter_block(block, cols, split):
    return pl.BlockSpec((block, cols), lambda i, flags: ((flags[1] // split) ^ i, 0))


def fixed(shape):
    return pl.BlockSpec(shape, lambda *ids: (0,) * len(shape))


def qkv_kernel(
    split, ranks, at, weights, late, flag_ref, x_ref, vec_ref, bias_ref, cos_ref, sin_ref, *refs
):
    refs = refs[:weights] + refs[weights + late :]
    one_ref, groups_ref, w_ref = refs[weights], refs[-2], refs[-1]
    once((at, flag_ref, refs[:weights], w_ref))
    i = pl.program_id(0)
    hat, _ = norm_rows(x_ref[...].astype(F32))
    one = (hat * vec_ref[0:1, :] + vec_ref[1:2, :]).astype(BF16)
    one_ref[...] = one
    width = w_ref.shape[2]
    cosine, sine = widen(cos_ref[...], width), widen(sin_ref[...], width)
    for part in range(3):
        lin = dot(one, w_ref[part]) + bias_ref[part : part + 1, :]
        if part < 2:
            lin = lin * cosine + swap_halves(lin) * sine
        if part == 0:
            lin = lin * SCORE_SCALE
        low = lin.astype(BF16)
        for g in range(width // GROUP):
            groups_ref[g, :, part * GROUP : (part + 1) * GROUP] = low[:, g * GROUP : (g + 1) * GROUP]
    send_pieces(i, split, 2, flag_ref, refs[weights + 1 : -2], groups_ref, ranks)


def project(flags, split, ranks, rows_all, vec, weight, bias, cosine, sine, block, late):
    rows, dim = rows_all.shape
    width = weight.shape[2]
    groups = width // GROUP
    piece = (block, 3 * GROUP)
    shapes = piece_shapes(groups // split, ranks, 2, piece)
    result = pl.pallas_call(
        functools.partial(
            qkv_kernel, split, ranks, weight.at, len(weight.arrays), len(late)
        ),
        grid_spec=pltpu.PrefetchScalarGridSpec(
            num_scalar_prefetch=1,
            grid=(rows // block,),
            in_specs=[
                quarter_block(block, dim, split), whole(vec), whole(bias),
                quarter_block(block, cosine.shape[1], split),
                quarter_block(block, sine.shape[1], split),
            ]
            + weight.specs()
            + [pl.BlockSpec(memory_space=pl.ANY)] * len(late),
            out_specs=[quarter_block(block, dim, split)] + [fixed(shape) for shape in shapes],
            scratch_shapes=[pltpu.VMEM((groups,) + piece, BF16), weight.scratch()],
        ),
        out_shape=[pltpu.HBM((rows, dim), BF16)]
        + [jax.ShapeDtypeStruct(shape, BF16) for shape in shapes],
        compiler_params=params(12),
        cost_estimate=brief(300),
        name="norm_qkv",
    )(
        flags, in_hbm(rows_all), vec, bias, in_hbm(cosine), in_hbm(sine), *weight.hbm_first(),
        *late,
    )
    return result[0], result[1:]


def attn_grad_kernel(split, ranks, at, weights, late, flag_ref, cot_ref, *refs):
    refs = refs[:weights] + refs[weights + late :]
    groups_ref, w_ref = refs[-2:]
    once((at, flag_ref, refs[:weights], w_ref))
    grad = dot(cot_ref[...], w_ref[0], 1, 1).astype(BF16)
    for g in range(groups_ref.shape[0]):
        groups_ref[g] = grad[:, g * GROUP : (g + 1) * GROUP]
    send_pieces(pl.program_id(0), split, ranks, flag_ref, refs[weights:-2], groups_ref, ranks)


def attn_grad(flags, split, ranks, cot_all, weight, block, late):
    rows, dim = cot_all.shape
    groups = weight.shape[1] // GROUP
    piece = (block, GROUP)
    shapes = piece_shapes(groups // split, ranks, ranks, piece)
    result = pl.pallas_call(
        functools.partial(
            attn_grad_kernel, split, ranks, weight.at, len(weight.arrays), len(late)
        ),
        grid_spec=pltpu.PrefetchScalarGridSpec(
            num_scalar_prefetch=1,
            grid=(rows // block,),
            in_specs=[quarter_block(block, dim, split)]
            + weight.specs()
            + [pl.BlockSpec(memory_space=pl.ANY)] * len(late),
            out_specs=[fixed(shape) for shape in shapes],
            scratch_shapes=[pltpu.VMEM((groups,) + piece, BF16), weight.scratch()],
        ),
        out_shape=[jax.ShapeDtypeStruct(shape, BF16) for shape in shapes],
        compiler_params=params(8),
        cost_estimate=brief(300),
        name="attn_grad",
    )(flags, in_hbm(cot_all), *weight.hbm_first(), *late)
    return result


def mlp_kernel(ats, weights, flag_ref, x_ref, vec_ref, bias_ref, late_ref, *refs):
    two_ref, act_ref, slope_ref, part_ref, up_ref, down_ref = refs[-6:]
    once(
        (ats[0], flag_ref, refs[:weights], up_ref),
        (ats[1], flag_ref, refs[weights : 2 * weights], down_ref),
    )
    hat, _ = norm_rows(x_ref[...].astype(F32))
    two = (hat * vec_ref[2:3, :] + vec_ref[3:4, :]).astype(BF16)
    two_ref[...] = two
    pre = dot(two, up_ref[0]) + bias_ref[...]
    phi = 0.5 * (1.0 + lax.erf(pre * 0.7071067811865476))
    act = (pre * phi).astype(BF16)
    act_ref[...] = act
    slope = phi + pre * (0.3989422804014327 * jnp.exp(-0.5 * pre * pre))
    slope_ref[...] = slope.astype(BF16)
    part_ref[...] = dot(act, down_ref[0])


def mlp(flags, rows_all, vec, up, bias, down, block, late):
    rows, dim = rows_all.shape
    hidden = up.shape[2]
    return pl.pallas_call(
        functools.partial(mlp_kernel, (up.at, down.at), len(up.arrays)),
        grid=(rows // block,),
        in_specs=[
            pl.BlockSpec(memory_space=pltpu.SMEM), row_block(block, dim), whole(vec), whole(bias),
            pl.BlockSpec(memory_space=pl.ANY),
        ]
        + up.specs()
        + down.specs(),
        out_specs=[
            row_block(block, dim), row_block(block, hidden), row_block(block, hidden),
            row_block(block, dim),
        ],
        out_shape=[
            pltpu.HBM((rows, dim), BF16),
            pltpu.HBM((rows, hidden), BF16),
            pltpu.HBM((rows, hidden), BF16),
            pltpu.HBM((rows, dim), F32),
        ],
        scratch_shapes=[up.scratch(), down.scratch()],
        compiler_params=params(18),
        cost_estimate=brief(),
        name="mlp",
    )(flags, in_hbm(rows_all), vec, bias, late, *up.hbm_first(), *down.hbm_first())


def gather_pieces(pieces, parts, row_ref, col_ref, size, out_ref):
    full = out_ref.shape[1] // parts
    ranks = row_ref.shape[0]
    count = len(pieces) // ranks
    for index, piece in enumerate(pieces):
        r, p = index % ranks, index // ranks
        rows = pl.ds(pl.multiple_of(row_ref[r] * size, size), size)
        for part in range(parts):
            values = piece[:, part * GROUP : (part + 1) * GROUP]
            if count * GROUP == full:
                out_ref[rows, part * full + p * GROUP : part * full + (p + 1) * GROUP] = values
            else:
                column = part * full + (col_ref[r] * count + p) * GROUP
                out_ref[rows, pl.ds(pl.multiple_of(column, GROUP), GROUP)] = values


def out_kernel(at, weights, count, flag_ref, row_ref, col_ref, down_ref, late_ref, *refs):
    pieces = refs[weights : weights + count]
    attended_ref, out_ref, w_ref = refs[-3:]
    once((at, flag_ref, refs[:weights], w_ref))
    i = pl.program_id(0)
    block = out_ref.shape[0]

    @pl.when(i == 0)
    def _():
        ranks = row_ref.shape[0]
        local = len(pieces) - ranks + 1
        flat = []
        for p in range(local):
            flat += [pieces[p]] + [ref.at[p] if local > 1 else ref for ref in pieces[local:]]
        gather_pieces(flat, 1, row_ref, col_ref, block, attended_ref)

    rows = pl.ds(pl.multiple_of(i * block, block), block)
    out_ref[...] = (down_ref[...] + dot(attended_ref[rows, :], w_ref[0])).astype(BF16)


def out_partial(flags, row_at, col_at, pieces, down_part, weight, block, late):
    rows, dim = down_part.shape
    width = weight.shape[1]
    return pl.pallas_call(
        functools.partial(out_kernel, weight.at, len(weight.arrays), len(pieces)),
        grid_spec=pltpu.PrefetchScalarGridSpec(
            num_scalar_prefetch=3,
            grid=(rows // block,),
            in_specs=[row_block(block, dim), pl.BlockSpec(memory_space=pl.ANY)]
            + weight.specs()
            + [whole(p) for p in pieces],
            out_specs=[fixed((rows, width)), row_block(block, dim)],
            scratch_shapes=[weight.scratch()],
        ),
        out_shape=[
            pltpu.HBM((rows, width), BF16),
            pltpu.HBM((rows, dim), BF16),
        ],
        compiler_params=params(10),
        cost_estimate=brief(),
        name="out_partial",
    )(flags, row_at, col_at, in_hbm(down_part), late, *weight.hbm_first(), *pieces)


def pair_bias(start_ref, first, size, keys):
    query_at = lax.broadcasted_iota(jnp.int32, (size, keys), 0) + first
    key_at = lax.broadcasted_iota(jnp.int32, (size, keys), 1)
    allowed = (key_at <= query_at) & (key_at >= start_ref[first : first + size, :])
    return jnp.where(allowed, 0.0, -MASK_FILL)


def attn_fwd_kernel(at, before, pos_ref, start_ref, late_ref, *refs):
    count = len(at)
    blocks = [ref.at[p] for ref, p in zip(refs, at)]
    earlier, refs = refs[count : count + before], refs[count + before :]
    outs, refs = refs[:count], refs[count:]
    for source, target in zip(earlier, outs[1:]):
        target[0] = source[...]
    outs = [outs[0]] + [ref.at[1] if before else ref for ref in outs[1:]]
    q_ref, k_ref, v_ref, lse_ref, o_ref = refs
    size, width = outs[0].shape
    for r in range(count):
        rows = pl.ds(pl.multiple_of(pos_ref[r] * size, size), size)
        q_ref[rows, :] = blocks[r][:, :width]
        k_ref[rows, :] = blocks[r][:, width : 2 * width]
        v_ref[rows, :] = blocks[r][:, 2 * width :]
    group = lax.broadcasted_iota(jnp.int32, (1, width), 1) // HEAD
    lane = lax.broadcasted_iota(jnp.int32, (1, 128), 1)
    zero, unit = jnp.zeros((), BF16), jnp.ones((), BF16)
    for i in range(count):
        first, keys = i * size, (i + 1) * size
        bias = pair_bias(start_ref, first, size, keys)
        query = q_ref[first:keys, :]
        total = jnp.zeros((size, width), F32)
        tops = jnp.zeros((size, 128), F32)
        for head in range(width // HEAD):
            mine = group == head
            other = HEAD if head == 0 else 0
            scores = dot(jnp.where(mine, query, zero), k_ref[:keys, :], 1, 1) + bias
            top = jnp.max(scores, axis=-1, keepdims=True)
            terms = jnp.exp(scores - top).astype(BF16)
            mixed = dot(terms, jnp.where(mine, v_ref[:keys, :], unit))
            row_sum = mixed[:, other : other + 1]
            total = jnp.where(mine, mixed * (1.0 / row_sum), total)
            tops = jnp.where(lane == head, top + jnp.log(row_sum), tops)
        o_ref[first:keys, :] = total
        lse_ref[first:keys, :] = tops
    for r in range(count):
        rows = pl.ds(pl.multiple_of(pos_ref[r] * size, size), size)
        outs[r][...] = o_ref[rows, :].astype(BF16)


def attend(pos, start_col, blocks, late, earlier):
    count = len(blocks)
    size, wide = blocks[0][0].shape[1:]
    width, length = wide // 3, size * count
    shapes = [(size, width)] + [((2,) if earlier else ()) + (size, width)] * (count - 1)
    result = pl.pallas_call(
        functools.partial(attn_fwd_kernel, tuple(p for _, p in blocks), len(earlier)),
        grid=(1,),
        in_specs=[
            pl.BlockSpec(memory_space=pltpu.SMEM), whole(start_col),
            pl.BlockSpec(memory_space=pl.ANY),
        ]
        + [whole(array) for array, _ in blocks]
        + [whole(array) for array in earlier],
        out_specs=[fixed(shape) for shape in shapes]
        + [fixed((length, width))] * 3
        + [fixed((length, 128))],
        out_shape=[jax.ShapeDtypeStruct(shape, BF16) for shape in shapes]
        + [pltpu.HBM((length, width), BF16)] * 3
        + [pltpu.HBM((length, 128), F32)],
        scratch_shapes=[pltpu.VMEM((length, width), F32)],
        compiler_params=params(3 * count),
        cost_estimate=brief(),
        name="attend",
    )(pos, start_col, late, *(array for array, _ in blocks), *earlier)
    return list(result[:count]), result[count:]


def attn_bwd_kernel(at, pos_ref, start_ref, late_ref, q_ref, k_ref, v_ref, lse_ref, cos_ref, sin_ref, *refs):
    count = len(at)
    blocks, outs = [ref.at[p] for ref, p in zip(refs, at)], refs[count : 2 * count]
    do_ref, dq_ref, dk_ref, dv_ref = refs[2 * count :]
    size, width = blocks[0].shape
    for r in range(count):
        rows = pl.ds(pl.multiple_of(pos_ref[r] * size, size), size)
        do_ref[rows, :] = blocks[r][...]
    dk_ref[...] = jnp.zeros_like(dk_ref)
    dv_ref[...] = jnp.zeros_like(dv_ref)
    group = lax.broadcasted_iota(jnp.int32, (1, width), 1) // HEAD
    zero = jnp.zeros((), BF16)
    for i in range(count):
        first, keys = i * size, (i + 1) * size
        bias = pair_bias(start_ref, first, size, keys)
        query, grad_out = q_ref[first:keys, :], do_ref[first:keys, :]
        query_t, grad_out_t = query.T, grad_out.T
        total = jnp.zeros((size, width), F32)
        for head in range(width // HEAD):
            mine = group == head
            rows = slice(head * HEAD, (head + 1) * HEAD)
            scores = dot(jnp.where(mine, query, zero), k_ref[:keys, :], 1, 1) + bias
            probs = jnp.exp(scores - lse_ref[first:keys, head : head + 1])
            grad_prob = dot(jnp.where(mine, grad_out, zero), v_ref[:keys, :], 1, 1)
            delta = jnp.sum(probs * grad_prob, axis=-1, keepdims=True)
            grad_score = (probs * (grad_prob - delta)).astype(BF16)
            total = total + dot(grad_score, jnp.where(mine, k_ref[:keys, :], zero))
            dk_ref[rows, :keys] += dot(query_t[rows, :], grad_score)
            dv_ref[rows, :keys] += dot(grad_out_t[rows, :], probs.astype(BF16))
        dq_ref[first:keys, :] = total * SCORE_SCALE
    dk = dk_ref[...].T
    dv = dv_ref[...].T
    cosine, sine = cos_ref[...], sin_ref[...]
    key_grad = dk * cosine - swap_halves(dk) * sine
    grad = dq_ref[...]
    dq_ref[...] = grad * cosine - swap_halves(grad) * sine
    do_ref[...] = dv.astype(BF16)
    for r in range(count):
        rows = pl.ds(pl.multiple_of(pos_ref[r] * size, size), size)
        outs[r][:, :width] = dq_ref[rows, :].astype(BF16)
        outs[r][:, 2 * width :] = do_ref[rows, :]
    dq_ref[...] = key_grad
    for r in range(count):
        rows = pl.ds(pl.multiple_of(pos_ref[r] * size, size), size)
        outs[r][:, width : 2 * width] = dq_ref[rows, :].astype(BF16)


def attend_back(pos, start_col, kept, cosine, sine, blocks, late, weight):
    count = len(blocks)
    size, width = blocks[0][0].shape[1:]
    length = size * count
    return pl.pallas_call(
        functools.partial(attn_bwd_kernel, tuple(p for _, p in blocks)),
        grid=(1,),
        in_specs=[
            pl.BlockSpec(memory_space=pltpu.SMEM), whole(start_col),
            pl.BlockSpec(memory_space=pl.ANY),
        ]
        + [whole(array) for array in (*kept, cosine, sine)]
        + [whole(array) for array, _ in blocks],
        out_specs=[fixed((size, 3 * width))] * count,
        out_shape=[jax.ShapeDtypeStruct((size, 3 * width), BF16)] * count,
        scratch_shapes=[pltpu.VMEM((length, width), BF16), pltpu.VMEM((length, width), F32)]
        + [pltpu.VMEM((width, length), F32)] * 2,
        compiler_params=params(4 * count),
        cost_estimate=brief(weight),
        name="attend_back",
    )(
        pos, start_col, late, *[in_hbm(a) for a in (*kept, cosine, sine)],
        *(array for array, _ in blocks),
    )


def add_sums(i, ref, values):
    sums = [jnp.sum(value, axis=0, keepdims=True) for value in values]
    sums += [jnp.zeros_like(sums[0])] * (8 - len(sums))
    share = jnp.concatenate(sums, axis=0)

    @pl.when(i == 0)
    def _():
        ref[...] = share

    @pl.when(i > 0)
    def _():
        ref[...] += share


def mlp_back_kernel(ats, weights, flag_ref, x_ref, cot_ref, slope_ref, vec_ref, *refs):
    pre_ref, two_ref, grads_ref, bias_ref, down_ref, up_ref = refs[-6:]
    once(
        (ats[0], flag_ref, refs[:weights], down_ref),
        (ats[1], flag_ref, refs[weights : 2 * weights], up_ref),
    )
    i = pl.program_id(0)
    grad_act = dot(cot_ref[...], down_ref[0], 1, 1)
    grad_pre = (grad_act * slope_ref[...].astype(F32)).astype(BF16)
    pre_ref[...] = grad_pre
    two = dot(grad_pre, up_ref[0], 1, 1)
    hat, _ = norm_rows(x_ref[...].astype(F32))
    two_ref[...] = two * vec_ref[2:3, :]
    add_sums(i, grads_ref, (two * hat, two))
    add_sums(i, bias_ref, (grad_pre.astype(F32),))


def mlp_back(flags, rows_all, cot_all, slope, down, up, vec, block, late):
    rows, dim = rows_all.shape
    hidden = slope.shape[1]
    return pl.pallas_call(
        functools.partial(mlp_back_kernel, (down.at, up.at), len(up.arrays)),
        grid=(rows // block,),
        in_specs=[
            pl.BlockSpec(memory_space=pltpu.SMEM), row_block(block, dim), row_block(block, dim),
            row_block(block, hidden), whole(vec),
        ]
        + down.specs()
        + up.specs()
        + [pl.BlockSpec(memory_space=pl.ANY)] * len(late),
        out_specs=[
            row_block(block, hidden), row_block(block, dim), fixed((8, dim)), fixed((8, hidden)),
        ],
        out_shape=[
            pltpu.HBM((rows, hidden), BF16),
            jax.ShapeDtypeStruct((rows, dim), F32),
            jax.ShapeDtypeStruct((8, dim), F32),
            jax.ShapeDtypeStruct((8, hidden), F32),
        ],
        scratch_shapes=[down.scratch(), up.scratch()],
        compiler_params=params(18),
        cost_estimate=brief(8),
        name="mlp_back",
    )(
        flags, in_hbm(rows_all), in_hbm(cot_all), in_hbm(slope), vec, *down.hbm_first(),
        *up.hbm_first(), *late,
    )


def input_grad_kernel(
    at, weights, count, flag_ref, row_ref, col_ref, x_ref, two_ref, vec_ref, late_ref, *refs
):
    pieces = refs[weights : weights + count]
    dlin_ref, sum_ref, grads_ref, bias_ref, w_ref = refs[-5:]
    once((at, flag_ref, refs[:weights], w_ref))
    width = w_ref.shape[2]
    block = x_ref.shape[0]
    i = pl.program_id(0)

    @pl.when(i == 0)
    def _():
        gather_pieces(pieces, 3, row_ref, col_ref, block, dlin_ref)

    rows = pl.ds(pl.multiple_of(i * block, block), block)
    hat, _ = norm_rows(x_ref[...].astype(F32))
    dlin = dlin_ref[rows, :]
    one = dot(dlin[:, :width], w_ref[0], 1, 1)
    for part in (1, 2):
        one = one + dot(dlin[:, part * width : (part + 1) * width], w_ref[part], 1, 1)
    sum_ref[...] = (one * vec_ref[0:1, :] + two_ref[...]).astype(BF16)
    add_sums(i, grads_ref, (one * hat, one))
    add_sums(i, bias_ref, (dlin.astype(F32),))


def input_grad(flags, row_at, col_at, rows_all, pieces, weight, two_part, vec, block, late):
    rows, dim = rows_all.shape
    wide = 3 * weight.shape[2]
    return pl.pallas_call(
        functools.partial(input_grad_kernel, weight.at, len(weight.arrays), len(pieces)),
        grid_spec=pltpu.PrefetchScalarGridSpec(
            num_scalar_prefetch=3,
            grid=(rows // block,),
            in_specs=[
                row_block(block, dim), row_block(block, dim), whole(vec),
                pl.BlockSpec(memory_space=pl.ANY),
            ]
            + weight.specs()
            + [whole(p) for p in pieces],
            out_specs=[
                fixed((rows, wide)), row_block(block, dim), fixed((8, dim)), fixed((8, wide)),
            ],
            scratch_shapes=[weight.scratch()],
        ),
        out_shape=[
            jax.ShapeDtypeStruct((rows, wide), BF16),
            pltpu.HBM((rows, dim), BF16),
            jax.ShapeDtypeStruct((8, dim), F32),
            jax.ShapeDtypeStruct((8, wide), F32),
        ],
        compiler_params=params(12),
        cost_estimate=brief(),
        name="input_grad",
    )(flags, row_at, col_at, in_hbm(rows_all), two_part, vec, late, *weight.hbm_first(), *pieces)


def by_xor(axis, count, step):
    return functools.partial(
        lax.ppermute, axis_name=axis, perm=[(i, i ^ step) for i in range(count)]
    )


def nothing(*refs):
    del refs


def after(values, *others):
    anywhere = pl.BlockSpec(memory_space=pl.ANY)
    return pl.pallas_call(
        nothing,
        in_specs=[anywhere] * (1 + len(others)),
        out_specs=anywhere,
        out_shape=jax.ShapeDtypeStruct(values.shape, values.dtype),
        input_output_aliases={0: 0},
        name="after",
    )(values, *others)


def first_token(values):
    def copy(source, target):
        target[...] = source[...]

    return pl.pallas_call(
        copy, out_shape=jax.ShapeDtypeStruct(values.shape, values.dtype), name="first"
    )(values)


class Weight:
    def __init__(self, own, at, token, shards, ranks):
        self.at, shape = at, list(own.shape)
        shape[at] *= shards
        self.shape = tuple(shape)
        if shards == 2 and ranks > 1:
            half = own.shape[1] // 2
            odd = lax.axis_index("ctx") & 1
            mine = lax.dynamic_slice_in_dim(own, odd * half, half, 1)
            mine = by_xor("shard", 2, 1)(after(mine, token))
            self.arrays = [own, mine, by_xor("ctx", ranks, 1)(mine)]
            self.token = mine
        else:
            self.arrays = [lax.all_gather(own, "shard", axis=at, tiled=True)]
            self.token = token

    def specs(self):
        return [whole(a) for a in self.arrays]

    def scratch(self):
        return pltpu.VMEM(self.shape, BF16)

    def hbm_first(self):
        return [in_hbm(self.arrays[0])] + self.arrays[1:]


def join(at, flag_ref, refs, full_ref):
    if len(refs) == 1:
        full_ref[...] = refs[0][...]
        return
    rows, cols = refs[0].shape[1:]
    half = rows // 2
    side, odd = flag_ref[0], flag_ref[1] & 1
    for where, first, ref in (
        (side, 0, refs[0]), (1 - side, odd * half, refs[1]), (1 - side, (1 - odd) * half, refs[2]),
    ):
        if at == 1:
            place = pl.ds(pl.multiple_of(where * rows + first, half), ref.shape[1])
            full_ref[:, place, :] = ref[...]
        else:
            place = pl.ds(pl.multiple_of(first, half), ref.shape[1])
            full_ref[:, place, pl.ds(pl.multiple_of(where * cols, cols), cols)] = ref[...]


def once(*joins):
    @pl.when(pl.program_id(0) == 0)
    def _():
        for args in joins:
            join(*args)


def axis_bits(axes):
    return [
        (axis, count, bit)
        for axis, count in axes
        for bit in reversed(range(count.bit_length() - 1))
    ]


def split_kernel(outer, terms, bit_ref, *refs):
    sources, (away_ref, keep_ref) = refs[:terms], refs[-2:]
    size = away_ref.shape[0] // outer
    for a in range(outer):
        for ref, half in ((away_ref, 1 - bit_ref[0]), (keep_ref, bit_ref[0])):
            rows = pl.ds(pl.multiple_of((2 * a + half) * size, size), size)
            total = sources[0][rows, :].astype(F32)
            for source in sources[1:]:
                total = total + source[rows, :].astype(F32)
            ref[a * size : (a + 1) * size, :] = total.astype(BF16)


def halve_rows(terms, bits, entry):
    rows, wide = terms[0].shape
    vmem = pl.BlockSpec(memory_space=pltpu.VMEM)
    half = jax.ShapeDtypeStruct((rows // 2, wide), BF16)
    axis, count, bit = entry
    away, keep = pl.pallas_call(
        functools.partial(split_kernel, 1 << bits.index(entry), len(terms)),
        in_specs=[pl.BlockSpec(memory_space=pltpu.SMEM)] + [vmem] * len(terms),
        out_specs=[vmem, vmem],
        out_shape=[half, half],
        compiler_params=params(10),
        cost_estimate=brief(),
        name="split",
    )(((lax.axis_index(axis) >> bit) & 1)[None], *terms)
    bits.remove(entry)
    return [keep, by_xor(axis, count, 1 << bit)(away)]


def quarters_kernel(flag_ref, keep_ref, came_ref, *refs):
    outs = refs[-4:]
    size = outs[0].shape[0]
    mine = flag_ref[0] * 2 + flag_ref[1] // 2
    for step, out in enumerate(outs):
        rows = pl.ds(pl.multiple_of((mine ^ step) * size, size), size)
        out[...] = (keep_ref[rows, :].astype(F32) + came_ref[rows, :].astype(F32)).astype(BF16)


def exchange_quarters(flags, terms, late):
    rows, wide = terms[0].shape
    outs = pl.pallas_call(
        quarters_kernel,
        grid=(1,),
        in_specs=[pl.BlockSpec(memory_space=pltpu.SMEM)] + [whole(term) for term in terms]
        + [pl.BlockSpec(memory_space=pl.ANY)] * len(late),
        out_specs=[fixed((rows // 4, wide))] * 4,
        out_shape=[jax.ShapeDtypeStruct((rows // 4, wide), BF16)] * 4,
        compiler_params=params(10),
        cost_estimate=brief(),
        name="quarters",
    )(flags, in_hbm(terms[0]), terms[1], *late)
    came = [outs[0]]
    for step in range(1, 4):
        perm = [(s * 4 + c, (s ^ (step >> 1)) * 4 + (c ^ ((step & 1) * 2))) for s in range(2) for c in range(4)]
        came.append(lax.ppermute(outs[step], ("shard", "ctx"), perm))
    return came, outs[0]


def group_kernel(count, small, flag_ref, *refs):
    lefts, rights = refs[0 : 2 * count : 2], refs[1 : 2 * count : 2]
    away_ref, keep_ref = refs[-2:]
    i = pl.program_id(0)
    core = jnp.where(i == 0, 1 - (flag_ref[1] & 1), flag_ref[1] & 1)

    def columns(ref, axis):
        parts = []
        for j in range(ref.shape[1] // 256):
            part = ref[:, pl.ds(pl.multiple_of((2 * j + core) * 128, 128), 128)]
            if axis == 0:
                part = jnp.concatenate([part, jnp.zeros((128 - part.shape[0], 128), F32)], axis=0).T
            parts.append(part)
        return jnp.concatenate(parts, axis=axis)

    first = 0
    values = []
    for left, right in zip(lefts, rights):
        values.append(dot(columns(left, 1), right[...], 0, 0).astype(BF16))
    if small:
        values.append(columns(refs[2 * count], 0).astype(BF16))
    for value in values:
        last = first + value.shape[1]

        @pl.when(i == 0)
        def _(value=value, first=first, last=last):
            away_ref[:, first:last] = value

        @pl.when(i > 0)
        def _(value=value, first=first, last=last):
            keep_ref[:, first:last] = value

        first = last


def group_grad(flags, pairs, small, axes, late):
    dim = pairs[0][0].shape[1]
    owners = 1
    for _, count in axes:
        owners *= count
    bits = axis_bits(axes)
    wide = sum(right.shape[1] for _, right in pairs) + (0 if small is None else 128)
    if dim // owners != 128:
        values = [dot(left, right, 0, 0).astype(BF16) for left, right in pairs]
        if small is not None:
            values.append(jnp.pad(small.T, ((0, 0), (0, 120))).astype(BF16))
        return halve_rows([jnp.concatenate(values, axis=1)], bits, bits[-1]), bits
    half = jax.ShapeDtypeStruct((dim // 2, wide), BF16)
    flat = [in_hbm(a) for pair in pairs for a in pair] + ([] if small is None else [small])
    away, keep = pl.pallas_call(
        functools.partial(group_kernel, len(pairs), small is not None),
        grid=(2,),
        in_specs=[pl.BlockSpec(memory_space=pltpu.SMEM)] + [whole(a) for a in flat]
        + [pl.BlockSpec(memory_space=pl.ANY)] * len(late),
        out_specs=[fixed(half.shape), fixed(half.shape)],
        out_shape=[half, pltpu.HBM(half.shape, BF16)],
        compiler_params=params(16),
        cost_estimate=brief(),
        name="group_grad",
    )(flags, *flat, *late)
    return [keep, by_xor("ctx", dict(axes)["ctx"], 1)(away)], bits[:-1]


def scatter_group(flags, terms, bits, late):
    if len(bits) == 2:
        return exchange_quarters(flags, terms, late)
    bits = list(bits)
    while bits:
        terms = halve_rows(terms, bits, bits[-1])
    return terms, terms[0]


def total_kernel(terms, layouts, *refs):
    outs = refs[len(refs) - len(layouts) :]
    first = 0
    for out, (kind, wide) in zip(outs, layouts):
        cols = slice(first, first + wide)
        total = refs[0][:, cols].astype(F32)
        for ref in refs[1:terms]:
            total = total + ref[:, cols].astype(F32)
        if kind == "flip":
            out[...] = total.T
        elif kind == "small":
            out[...] = total.T[:8, :]
        elif kind == "three":
            for part in range(3):
                out[part] = total[:, part * wide // 3 : (part + 1) * wide // 3]
        else:
            out[...] = total
        first += wide


def group_total(terms, layouts, late, weight):
    rows = terms[0].shape[0]
    shapes = {
        "flip": lambda w: (w, rows), "small": lambda w: (8, rows),
        "three": lambda w: (3, rows, w // 3), "keep": lambda w: (rows, w),
    }
    vmem = pl.BlockSpec(memory_space=pltpu.VMEM)
    return pl.pallas_call(
        functools.partial(total_kernel, len(terms), layouts),
        in_specs=[vmem] * len(terms) + [pl.BlockSpec(memory_space=pl.ANY)] * len(late),
        out_specs=[vmem] * len(layouts),
        out_shape=[jax.ShapeDtypeStruct(shapes[kind](w), F32) for kind, w in layouts],
        compiler_params=params(10),
        cost_estimate=brief(weight),
        name="group_total",
    )(*terms, *late)


def body(
    sizes, hidden_in, w_qkv, bias_qkv, w_dense, w_up, bias_up, w_down, vectors, block_deal,
    segments, cotangent,
):
    shards, ranks, tps = sizes
    rank = lax.axis_index("ctx")
    dim = hidden_in.shape[1]
    own_rows = hidden_in.shape[0]

    x_all = lax.all_gather(hidden_in, "tp", axis=0, tiled=True)
    heads = bias_qkv.shape[1]
    width = heads * HEAD
    half = vectors.shape[1]
    small = jnp.concatenate(
        [vectors.reshape(-1), bias_qkv.astype(F32).reshape(-1), bias_up.astype(F32).reshape(-1)]
    )
    pad = -small.shape[0] % 1024
    small = jnp.pad(small, (0, pad)).reshape(1, -1, 128)
    token = first_token(segments)
    if shards == 2:
        other = by_xor("shard", 2, 1)(small)
        first = lax.axis_index("shard") == 0
        small = jnp.concatenate([jnp.where(first, small, other), jnp.where(first, other, small)])
    else:
        small = lax.all_gather(small, "shard", axis=0, tiled=True)
    small = small.reshape(shards, -1)
    cut = 6 * half
    vec = small[:, :cut].reshape(shards, 6, half).transpose(1, 0, 2).reshape(6, dim)
    vec = jnp.pad(vec, ((0, 2), (0, 0)))
    share = bias_qkv.size
    qkv_bias = small[:, cut : cut + share].reshape((shards,) + bias_qkv.shape)
    qkv_bias = qkv_bias.transpose(1, 2, 0, 3).reshape(3, width)
    up_bias = small[:, cut + share : cut + share + bias_up.size].reshape((shards,) + bias_up.shape)
    up_bias = up_bias.transpose(1, 0, 2).reshape(1, -1)
    flags = jnp.stack([lax.axis_index("shard"), rank])
    weight_qkv = Weight(w_qkv, 1, token, shards, ranks)
    weight_up = Weight(w_up[None], 1, token, shards, ranks)
    weight_down = Weight(w_down[None], 2, token, shards, ranks)
    weight_dense = Weight(w_dense[None], 2, token, shards, ranks)

    deal = block_deal[0]
    seg_row = segments[0]
    group = seg_row.shape[0]
    block = group // deal.shape[0]
    quarters = deal.shape[0] // ranks
    rank_rows = quarters * block
    split = ranks // quarters
    pieces = width // split // GROUP
    length = group // quarters
    at = jnp.arange(group, dtype=jnp.int32)
    previous = jnp.concatenate([seg_row[:1] - 1, seg_row[:-1]])
    begins = lax.cummax(jnp.where(seg_row != previous, at, 0), axis=0)
    places = (at - begins).reshape(deal.shape[0], block)
    deal_by_rank = deal.reshape(ranks, quarters)
    my_deal = lax.dynamic_index_in_dim(deal_by_rank, rank, 0, keepdims=False)
    picked = my_deal[:, None] == jnp.arange(deal.shape[0], dtype=jnp.int32)[None, :]
    rank_place = jnp.sum(jnp.where(picked[:, :, None], places[None], 0), axis=1).reshape(-1)
    quarter = rank // split
    partners = rank ^ jnp.arange(ranks, dtype=jnp.int32)
    in_quarter = jnp.take(lax.dynamic_index_in_dim(deal_by_rank, quarter, 1, keepdims=False), partners)
    pos = in_quarter - quarter * ranks
    my_begins = lax.dynamic_slice_in_dim(begins, quarter * length, length) - quarter * length
    quarter_place = jnp.arange(length, dtype=jnp.int32) - my_begins
    start_col = my_begins[:, None]
    lane = jnp.arange(128, dtype=jnp.int32) % HEAD
    frequency = ROPE_BASE ** (-2.0 * (lane % (ROT // 2)).astype(F32) / ROT)
    frequency = jnp.where(lane < ROT, frequency, 0.0)
    sign = jnp.where(lane < ROT // 2, -1.0, 1.0)
    all_places = jnp.concatenate([rank_place, quarter_place]).astype(F32)
    angles = all_places[:, None] * frequency[None, :]
    cosine, sine = jnp.cos(angles), jnp.sin(angles) * sign[None, :]
    target_row, target_col = partners // split, partners % split

    ready = after(cotangent, vec, qkv_bias, up_bias, cosine, sine, start_col, pos)
    cot_all = lax.all_gather(ready, "tp", axis=0, tiled=True)

    full_one, sent = project(
        flags, split, ranks, x_all, vec, weight_qkv, qkv_bias, cosine[:rank_rows],
        sine[:rank_rows], block, weight_up.arrays + weight_down.arrays + weight_dense.arrays,
    )

    def swap(sent):
        return [by_xor("ctx", ranks, s)(piece) if s else piece for s, piece in enumerate(sent)]

    arrived = exchange(sent, pieces, ranks, 2)
    full_two, activated, slope, down_part = mlp(
        flags, x_all, vec, weight_up, up_bias, weight_down, block, sent[0]
    )
    outs, kept, late = [], [], in_hbm(down_part)
    for p in range(pieces):
        out, keep = attend(pos, start_col, arrived[p], late, outs[0][1:] if p else [])
        outs.append(out)
        kept.append(keep)
        late = out[0]
    out_pieces = [out[0] for out in outs] + swap(outs[-1])[1:]

    axes = (("shard", shards), ("ctx", ranks))
    tables = (cosine[rank_rows:], sine[rank_rows:])
    attended, partial = out_partial(
        flags, target_row, target_col, out_pieces, down_part, weight_dense, block, late
    )
    summed = lax.psum_scatter(partial, "tp", scatter_dimension=0, tiled=True)
    sent = attn_grad(flags, split, ranks, cot_all, weight_dense, block, [in_hbm(partial)])
    arrived = exchange(sent, pieces, ranks, ranks)
    first, bits = group_grad(flags, [(cot_all, activated)], None, axes, (sent[0],))
    grad_pieces, late = [], in_hbm(first[0])
    for p in range(pieces):
        grads = attend_back(pos, start_col, kept[p], *tables, arrived[p], late, 0 if p else 6)
        grad_pieces += swap(grads)
        late = grads[0]
    grad_pre, two_part, two_sums, grad_ubias = mlp_back(
        flags, x_all, cot_all, slope, weight_down, weight_up, vec, block,
        grad_pieces[: ranks * (pieces - 1)] + [late],
    )
    first, late = scatter_group(flags, first, bits, (in_hbm(grad_pre),))
    dlin, row_sum, one_sums, grad_qbias = input_grad(
        flags, target_row, target_col, x_all, grad_pieces, weight_qkv, two_part, vec, block, late
    )
    own_sum = lax.psum_scatter(after(row_sum, summed), "tp", scatter_dimension=0, tiled=True)

    owners = shards * ranks
    each, share = HEAD // owners, dim // owners

    def by_owner(row, lines):
        row = row.reshape(lines, owners, each).transpose(1, 0, 2).reshape(owners, -1)
        return jnp.pad(row, ((0, 0), (0, share - lines * each))).reshape(1, dim)

    cot_rows = cotangent.astype(F32)
    cot_sum = jnp.sum(cot_rows, axis=0, keepdims=True)
    small_rows = jnp.concatenate(
        [
            one_sums[:2], two_sums[:2], cot_sum, cot_sum,
            by_owner(grad_qbias[0], 3 * heads), by_owner(grad_ubias[0], bias_up.shape[0]),
        ],
        axis=0,
    )
    hidden, wide = weight_up.shape[2], 3 * width
    second, _ = group_grad(flags, [(full_two, grad_pre)], small_rows, axes, (dlin,))
    (grad_down,) = group_total(first, (("flip", hidden),), (in_hbm(second[0]),), 12)
    second, late = scatter_group(flags, second, bits, (grad_down,))
    third, _ = group_grad(flags, [(full_one, dlin), (cot_all, attended)], None, axes, (late,))
    late = in_hbm(third[0])
    grad_up, small_rows = group_total(second, (("keep", hidden), ("small", 128)), (late,), 4)
    third, late = scatter_group(flags, third, bits, (grad_up,))
    grad_qkv, grad_dense = group_total(third, (("three", wide), ("flip", width)), (late,), 0)
    own = lax.axis_index("tp")
    lanes = small_rows[:6].reshape(6, tps, -1)
    vec_parts = [
        by_xor("tp", tps, step)(lax.dynamic_index_in_dim(lanes, own ^ step, 1, keepdims=False))
        for step in range(1, tps)
    ]
    grad_vec = sum(vec_parts, lax.dynamic_index_in_dim(lanes, own, 1, keepdims=False))
    grad_qbias = small_rows[6, : 3 * heads * each].reshape(3, heads, each)
    grad_ubias = small_rows[7, : bias_up.shape[0] * each].reshape(bias_up.shape[0], each)

    rows_in = hidden_in.astype(F32)
    output = (rows_in + summed.astype(F32) + vec[4:5] + vec[5:6]).astype(BF16)
    own_sum = after(own_sum, grad_qkv).astype(F32)
    hat, inverse = norm_rows(rows_in)
    centered = own_sum - jnp.mean(own_sum, axis=-1, keepdims=True)
    along = jnp.mean(own_sum * hat, axis=-1, keepdims=True)
    grad_in = (cot_rows + inverse * (centered - hat * along)).astype(BF16)
    return (
        output, grad_in, grad_qkv, grad_qbias, grad_dense, grad_up, grad_ubias, grad_down,
        grad_vec,
    )


def solution(mesh):
    sizes = tuple(mesh.shape[name] for name in ("shard", "ctx", "tp"))
    return jax.shard_map(
        functools.partial(body, sizes),
        mesh=mesh,
        in_specs=(
            P(("shard", "ctx", "tp"), None),
            P(None, "shard", "tp"),
            P(None, "tp", "shard"),
            P("tp", "shard"),
            P("shard", "tp"),
            P("tp", "shard"),
            P("tp", "shard"),
            P(None, "shard"),
            P("shard", None),
            P("shard", None),
            P(("shard", "ctx", "tp"), None),
        ),
        out_specs=(
            P(("shard", "ctx", "tp"), None),
            P(("shard", "ctx", "tp"), None),
            P(None, ("shard", "ctx"), "tp"),
            P(None, "tp", ("shard", "ctx")),
            P("tp", ("shard", "ctx")),
            P(("shard", "ctx"), "tp"),
            P("tp", ("shard", "ctx")),
            P("tp", ("shard", "ctx")),
            P(None, ("shard", "ctx", "tp")),
        ),
        check_vma=False,
    )
```

```python
import functools

import jax
import jax.numpy as jnp
from jax import lax
from jax.experimental import pallas as pl
from jax.experimental.pallas import tpu as pltpu
from jax.sharding import PartitionSpec as P

HEAD = 64
GROUP = 128
ROT = 16
NORM_EPS = 1e-05
SCORE_SCALE = 0.125
ROPE_BASE = 10000.0
MASK_FILL = 1e30
F32 = jnp.float32
BF16 = jnp.bfloat16


def dot(left, right, left_dim=1, right_dim=0):
    return lax.dot_general(
        left, right, (((left_dim,), (right_dim,)), ((), ())), preferred_element_type=F32
    )


def params(mib=20):
    return pltpu.CompilerParams(vmem_limit_bytes=mib * 1024 * 1024)


def brief(us=0):
    return pl.CostEstimate(flops=int(us * 1.1e9) + 1, bytes_accessed=1, transcendentals=0)


def swap_halves(values):
    width = values.shape[-1]
    lane = lax.broadcasted_iota(jnp.int32, (1, width), 1) % HEAD
    ahead = pltpu.roll(values, width - ROT // 2, 1)
    behind = pltpu.roll(values, ROT // 2, 1)
    return jnp.where(lane < ROT // 2, ahead, behind)


def widen(table, width):
    return jnp.concatenate([table] * (width // table.shape[-1]), axis=-1)


def norm_rows(rows):
    center = rows - jnp.mean(rows, axis=-1, keepdims=True)
    inverse = lax.rsqrt(jnp.mean(center * center, axis=-1, keepdims=True) + NORM_EPS)
    return center * inverse, inverse


def whole(array):
    return pl.BlockSpec(
        array.shape, lambda *ids: (0,) * array.ndim, pipeline_mode=pl.Buffered(buffer_count=1)
    )


def in_hbm(array):
    return pltpu.with_memory_space_constraint(array, pltpu.HBM)


def row_block(block, cols):
    return pl.BlockSpec((block, cols), lambda i, *ids: (i, 0))


def piece_shapes(pieces, ranks, merged, shape):
    shapes = []
    for step in range(ranks):
        if 0 < step < merged:
            shapes.append((pieces,) + shape)
        else:
            shapes += [(1,) + shape] * pieces
    return shapes


def by_step(flat, pieces, ranks, merged):
    steps, at = [], 0
    for step in range(ranks):
        count = 1 if 0 < step < merged else pieces
        steps.append(flat[at : at + count])
        at += count
    return steps


def send_pieces(i, split, merged, flag_ref, flat, groups_ref, ranks):
    pieces = groups_ref.shape[0] // split
    for step, refs in enumerate(by_step(flat, pieces, ranks, merged)):

        @pl.when(i == step // split)
        def _(step=step, refs=refs):
            for p in range(pieces):
                group = p
                if split > 1:
                    group = ((flag_ref[1] ^ step) % split) * pieces + p
                if len(refs) == 1:
                    refs[0][p] = groups_ref[group]
                else:
                    refs[p][0] = groups_ref[group]


def exchange(flat, pieces, ranks, merged):
    came = [[] for _ in range(pieces)]
    for step, arrays in enumerate(by_step(flat, pieces, ranks, merged)):
        if step:
            arrays = [by_xor("ctx", ranks, step)(array) for array in arrays]
        for p in range(pieces):
            came[p].append((arrays[0], p) if len(arrays) == 1 else (arrays[p], 0))
    return came


def quarter_block(block, cols, split):
    return pl.BlockSpec((block, cols), lambda i, flags: ((flags[1] // split) ^ i, 0))


def fixed(shape):
    return pl.BlockSpec(shape, lambda *ids: (0,) * len(shape))


def qkv_kernel(
    split, ranks, at, weights, late, flag_ref, x_ref, vec_ref, bias_ref, cos_ref, sin_ref, *refs
):
    refs = refs[:weights] + refs[weights + late :]
    one_ref, groups_ref, w_ref = refs[weights], refs[-2], refs[-1]
    once((at, flag_ref, refs[:weights], w_ref))
    i = pl.program_id(0)
    hat, _ = norm_rows(x_ref[...].astype(F32))
    one = (hat * vec_ref[0:1, :] + vec_ref[1:2, :]).astype(BF16)
    one_ref[...] = one
    width = w_ref.shape[2]
    cosine, sine = widen(cos_ref[...], width), widen(sin_ref[...], width)
    for part in range(3):
        lin = dot(one, w_ref[part]) + bias_ref[part : part + 1, :]
        if part < 2:
            lin = lin * cosine + swap_halves(lin) * sine
        if part == 0:
            lin = lin * SCORE_SCALE
        low = lin.astype(BF16)
        for g in range(width // GROUP):
            groups_ref[g, :, part * GROUP : (part + 1) * GROUP] = low[:, g * GROUP : (g + 1) * GROUP]
    send_pieces(i, split, 2, flag_ref, refs[weights + 1 : -2], groups_ref, ranks)


def project(flags, split, ranks, rows_all, vec, weight, bias, cosine, sine, block, late):
    rows, dim = rows_all.shape
    width = weight.shape[2]
    groups = width // GROUP
    piece = (block, 3 * GROUP)
    shapes = piece_shapes(groups // split, ranks, 2, piece)
    result = pl.pallas_call(
        functools.partial(
            qkv_kernel, split, ranks, weight.at, len(weight.arrays), len(late)
        ),
        grid_spec=pltpu.PrefetchScalarGridSpec(
            num_scalar_prefetch=1,
            grid=(rows // block,),
            in_specs=[
                quarter_block(block, dim, split), whole(vec), whole(bias),
                quarter_block(block, cosine.shape[1], split),
                quarter_block(block, sine.shape[1], split),
            ]
            + weight.specs()
            + [pl.BlockSpec(memory_space=pl.ANY)] * len(late),
            out_specs=[quarter_block(block, dim, split)] + [fixed(shape) for shape in shapes],
            scratch_shapes=[pltpu.VMEM((groups,) + piece, BF16), weight.scratch()],
        ),
        out_shape=[pltpu.HBM((rows, dim), BF16)]
        + [jax.ShapeDtypeStruct(shape, BF16) for shape in shapes],
        compiler_params=params(12),
        cost_estimate=brief(300),
        name="norm_qkv",
    )(
        flags, in_hbm(rows_all), vec, bias, in_hbm(cosine), in_hbm(sine), *weight.hbm_first(),
        *late,
    )
    return result[0], result[1:]


def attn_grad_kernel(split, ranks, at, weights, late, flag_ref, cot_ref, *refs):
    refs = refs[:weights] + refs[weights + late :]
    groups_ref, w_ref = refs[-2:]
    once((at, flag_ref, refs[:weights], w_ref))
    grad = dot(cot_ref[...], w_ref[0], 1, 1).astype(BF16)
    for g in range(groups_ref.shape[0]):
        groups_ref[g] = grad[:, g * GROUP : (g + 1) * GROUP]
    send_pieces(pl.program_id(0), split, ranks, flag_ref, refs[weights:-2], groups_ref, ranks)


def attn_grad(flags, split, ranks, cot_all, weight, block, late):
    rows, dim = cot_all.shape
    groups = weight.shape[1] // GROUP
    piece = (block, GROUP)
    shapes = piece_shapes(groups // split, ranks, ranks, piece)
    result = pl.pallas_call(
        functools.partial(
            attn_grad_kernel, split, ranks, weight.at, len(weight.arrays), len(late)
        ),
        grid_spec=pltpu.PrefetchScalarGridSpec(
            num_scalar_prefetch=1,
            grid=(rows // block,),
            in_specs=[quarter_block(block, dim, split)]
            + weight.specs()
            + [pl.BlockSpec(memory_space=pl.ANY)] * len(late),
            out_specs=[fixed(shape) for shape in shapes],
            scratch_shapes=[pltpu.VMEM((groups,) + piece, BF16), weight.scratch()],
        ),
        out_shape=[jax.ShapeDtypeStruct(shape, BF16) for shape in shapes],
        compiler_params=params(8),
        cost_estimate=brief(300),
        name="attn_grad",
    )(flags, in_hbm(cot_all), *weight.hbm_first(), *late)
    return result


def mlp_kernel(at, weights, flag_ref, x_ref, vec_ref, bias_ref, late_ref, *refs):
    two_ref, act_ref, slope_ref, up_ref = refs[-4:]
    once((at, flag_ref, refs[:weights], up_ref))
    hat, _ = norm_rows(x_ref[...].astype(F32))
    two = (hat * vec_ref[2:3, :] + vec_ref[3:4, :]).astype(BF16)
    two_ref[...] = two
    pre = dot(two, up_ref[0]) + bias_ref[...]
    phi = 0.5 * (1.0 + lax.erf(pre * 0.7071067811865476))
    act = (pre * phi).astype(BF16)
    act_ref[...] = act
    slope = phi + pre * (0.3989422804014327 * jnp.exp(-0.5 * pre * pre))
    slope_ref[...] = slope.astype(BF16)


def mlp(flags, rows_all, vec, up, bias, block, late):
    rows, dim = rows_all.shape
    hidden = up.shape[2]
    return pl.pallas_call(
        functools.partial(mlp_kernel, up.at, len(up.arrays)),
        grid=(rows // block,),
        in_specs=[
            pl.BlockSpec(memory_space=pltpu.SMEM), row_block(block, dim), whole(vec), whole(bias),
            pl.BlockSpec(memory_space=pl.ANY),
        ]
        + up.specs(),
        out_specs=[row_block(block, dim), row_block(block, hidden), row_block(block, hidden)],
        out_shape=[
            pltpu.HBM((rows, dim), BF16),
            pltpu.HBM((rows, hidden), BF16),
            pltpu.HBM((rows, hidden), BF16),
        ],
        scratch_shapes=[up.scratch()],
        compiler_params=params(18),
        cost_estimate=brief(),
        name="mlp",
    )(flags, in_hbm(rows_all), vec, bias, late, *up.hbm_first())


def gather_pieces(pieces, parts, row_ref, col_ref, size, out_ref):
    full = out_ref.shape[1] // parts
    ranks = row_ref.shape[0]
    count = len(pieces) // ranks
    for index, piece in enumerate(pieces):
        r, p = index % ranks, index // ranks
        rows = pl.ds(pl.multiple_of(row_ref[r] * size, size), size)
        for part in range(parts):
            values = piece[:, part * GROUP : (part + 1) * GROUP]
            if count * GROUP == full:
                out_ref[rows, part * full + p * GROUP : part * full + (p + 1) * GROUP] = values
            else:
                column = part * full + (col_ref[r] * count + p) * GROUP
                out_ref[rows, pl.ds(pl.multiple_of(column, GROUP), GROUP)] = values


def down_kernel(at, weights, flag_ref, act_ref, late_ref, *refs):
    out_ref, down_ref = refs[-2:]
    once((at, flag_ref, refs[:weights], down_ref))
    out_ref[...] = dot(act_ref[...], down_ref[0])


def mlp_down(flags, activated, down, block, late):
    rows, hidden = activated.shape
    dim = down.shape[2]
    return pl.pallas_call(
        functools.partial(down_kernel, down.at, len(down.arrays)),
        grid=(rows // block,),
        in_specs=[
            pl.BlockSpec(memory_space=pltpu.SMEM), row_block(block, hidden),
            pl.BlockSpec(memory_space=pl.ANY),
        ]
        + down.specs(),
        out_specs=row_block(block, dim),
        out_shape=jax.ShapeDtypeStruct((rows, dim), F32),
        scratch_shapes=[down.scratch()],
        compiler_params=params(14),
        cost_estimate=brief(),
        name="mlp_down",
    )(flags, in_hbm(activated), late, *down.hbm_first())


def out_kernel(at, weights, count, flag_ref, row_ref, col_ref, part_ref, *refs):
    pieces = refs[weights : weights + count]
    attended_ref, out_ref, w_ref = refs[-3:]
    once((at, flag_ref, refs[:weights], w_ref))
    i = pl.program_id(0)
    block = out_ref.shape[0]

    @pl.when(i == 0)
    def _():
        ranks = row_ref.shape[0]
        local = len(pieces) - ranks + 1
        flat = []
        for p in range(local):
            flat += [pieces[p]] + [ref.at[p] if local > 1 else ref for ref in pieces[local:]]
        gather_pieces(flat, 1, row_ref, col_ref, block, attended_ref)

    rows = pl.ds(pl.multiple_of(i * block, block), block)
    out_ref[...] = (part_ref[...] + dot(attended_ref[rows, :], w_ref[0])).astype(BF16)


def out_partial(flags, row_at, col_at, pieces, part, dense, block):
    rows = part.shape[0]
    width, dim = dense.shape[1:]
    return pl.pallas_call(
        functools.partial(out_kernel, dense.at, len(dense.arrays), len(pieces)),
        grid_spec=pltpu.PrefetchScalarGridSpec(
            num_scalar_prefetch=3,
            grid=(rows // block,),
            in_specs=[row_block(block, dim)] + dense.specs() + [whole(p) for p in pieces],
            out_specs=[fixed((rows, width)), row_block(block, dim)],
            scratch_shapes=[dense.scratch()],
        ),
        out_shape=[pltpu.HBM((rows, width), BF16), pltpu.HBM((rows, dim), BF16)],
        compiler_params=params(12),
        cost_estimate=brief(),
        name="out_partial",
    )(flags, row_at, col_at, part, *dense.hbm_first(), *pieces)


def pair_bias(start_ref, first, size, keys):
    query_at = lax.broadcasted_iota(jnp.int32, (size, keys), 0) + first
    key_at = lax.broadcasted_iota(jnp.int32, (size, keys), 1)
    allowed = (key_at <= query_at) & (key_at >= start_ref[first : first + size, :])
    return jnp.where(allowed, 0.0, -MASK_FILL)


def attn_fwd_kernel(at, before, pos_ref, start_ref, late_ref, *refs):
    count = len(at)
    blocks = [ref.at[p] for ref, p in zip(refs, at)]
    earlier, refs = refs[count : count + before], refs[count + before :]
    outs, refs = refs[:count], refs[count:]
    for source, target in zip(earlier, outs[1:]):
        target[0] = source[...]
    outs = [outs[0]] + [ref.at[1] if before else ref for ref in outs[1:]]
    q_ref, k_ref, v_ref, lse_ref, o_ref = refs
    size, width = outs[0].shape
    for r in range(count):
        rows = pl.ds(pl.multiple_of(pos_ref[r] * size, size), size)
        q_ref[rows, :] = blocks[r][:, :width]
        k_ref[rows, :] = blocks[r][:, width : 2 * width]
        v_ref[rows, :] = blocks[r][:, 2 * width :]
    group = lax.broadcasted_iota(jnp.int32, (1, width), 1) // HEAD
    lane = lax.broadcasted_iota(jnp.int32, (1, 128), 1)
    zero, unit = jnp.zeros((), BF16), jnp.ones((), BF16)
    for i in range(count):
        first, keys = i * size, (i + 1) * size
        bias = pair_bias(start_ref, first, size, keys)
        query = q_ref[first:keys, :]
        total = jnp.zeros((size, width), F32)
        tops = jnp.zeros((size, 128), F32)
        for head in range(width // HEAD):
            mine = group == head
            other = HEAD if head == 0 else 0
            scores = dot(jnp.where(mine, query, zero), k_ref[:keys, :], 1, 1) + bias
            top = jnp.max(scores, axis=-1, keepdims=True)
            terms = jnp.exp(scores - top).astype(BF16)
            mixed = dot(terms, jnp.where(mine, v_ref[:keys, :], unit))
            row_sum = mixed[:, other : other + 1]
            total = jnp.where(mine, mixed * (1.0 / row_sum), total)
            tops = jnp.where(lane == head, top + jnp.log(row_sum), tops)
        o_ref[first:keys, :] = total
        lse_ref[first:keys, :] = tops
    for r in range(count):
        rows = pl.ds(pl.multiple_of(pos_ref[r] * size, size), size)
        outs[r][...] = o_ref[rows, :].astype(BF16)


def attend(pos, start_col, blocks, late, earlier):
    count = len(blocks)
    size, wide = blocks[0][0].shape[1:]
    width, length = wide // 3, size * count
    shapes = [(size, width)] + [((2,) if earlier else ()) + (size, width)] * (count - 1)
    result = pl.pallas_call(
        functools.partial(attn_fwd_kernel, tuple(p for _, p in blocks), len(earlier)),
        grid=(1,),
        in_specs=[
            pl.BlockSpec(memory_space=pltpu.SMEM), whole(start_col),
            pl.BlockSpec(memory_space=pl.ANY),
        ]
        + [whole(array) for array, _ in blocks]
        + [whole(array) for array in earlier],
        out_specs=[fixed(shape) for shape in shapes]
        + [fixed((length, width))] * 3
        + [fixed((length, 128))],
        out_shape=[jax.ShapeDtypeStruct(shape, BF16) for shape in shapes]
        + [pltpu.HBM((length, width), BF16)] * 3
        + [pltpu.HBM((length, 128), F32)],
        scratch_shapes=[pltpu.VMEM((length, width), F32)],
        compiler_params=params(3 * count),
        cost_estimate=brief(),
        name="attend",
    )(pos, start_col, late, *(array for array, _ in blocks), *earlier)
    return list(result[:count]), result[count:]


def attn_bwd_kernel(at, pos_ref, start_ref, late_ref, q_ref, k_ref, v_ref, lse_ref, cos_ref, sin_ref, *refs):
    count = len(at)
    blocks, outs = [ref.at[p] for ref, p in zip(refs, at)], refs[count : 2 * count]
    do_ref, dq_ref, dk_ref, dv_ref = refs[2 * count :]
    size, width = blocks[0].shape
    for r in range(count):
        rows = pl.ds(pl.multiple_of(pos_ref[r] * size, size), size)
        do_ref[rows, :] = blocks[r][...]
    dk_ref[...] = jnp.zeros_like(dk_ref)
    dv_ref[...] = jnp.zeros_like(dv_ref)
    group = lax.broadcasted_iota(jnp.int32, (1, width), 1) // HEAD
    zero = jnp.zeros((), BF16)
    for i in range(count):
        first, keys = i * size, (i + 1) * size
        bias = pair_bias(start_ref, first, size, keys)
        query, grad_out = q_ref[first:keys, :], do_ref[first:keys, :]
        query_t, grad_out_t = query.T, grad_out.T
        total = jnp.zeros((size, width), F32)
        for head in range(width // HEAD):
            mine = group == head
            rows = slice(head * HEAD, (head + 1) * HEAD)
            scores = dot(jnp.where(mine, query, zero), k_ref[:keys, :], 1, 1) + bias
            probs = jnp.exp(scores - lse_ref[first:keys, head : head + 1])
            grad_prob = dot(jnp.where(mine, grad_out, zero), v_ref[:keys, :], 1, 1)
            delta = jnp.sum(probs * grad_prob, axis=-1, keepdims=True)
            grad_score = (probs * (grad_prob - delta)).astype(BF16)
            total = total + dot(grad_score, jnp.where(mine, k_ref[:keys, :], zero))
            dk_ref[rows, :keys] += dot(query_t[rows, :], grad_score)
            dv_ref[rows, :keys] += dot(grad_out_t[rows, :], probs.astype(BF16))
        dq_ref[first:keys, :] = total * SCORE_SCALE
    dk = dk_ref[...].T
    dv = dv_ref[...].T
    cosine, sine = cos_ref[...], sin_ref[...]
    key_grad = dk * cosine - swap_halves(dk) * sine
    grad = dq_ref[...]
    dq_ref[...] = grad * cosine - swap_halves(grad) * sine
    do_ref[...] = dv.astype(BF16)
    for r in range(count):
        rows = pl.ds(pl.multiple_of(pos_ref[r] * size, size), size)
        outs[r][:, :width] = dq_ref[rows, :].astype(BF16)
        outs[r][:, 2 * width :] = do_ref[rows, :]
    dq_ref[...] = key_grad
    for r in range(count):
        rows = pl.ds(pl.multiple_of(pos_ref[r] * size, size), size)
        outs[r][:, width : 2 * width] = dq_ref[rows, :].astype(BF16)


def attend_back(pos, start_col, kept, cosine, sine, blocks, late, weight):
    count = len(blocks)
    size, width = blocks[0][0].shape[1:]
    length = size * count
    return pl.pallas_call(
        functools.partial(attn_bwd_kernel, tuple(p for _, p in blocks)),
        grid=(1,),
        in_specs=[
            pl.BlockSpec(memory_space=pltpu.SMEM), whole(start_col),
            pl.BlockSpec(memory_space=pl.ANY),
        ]
        + [whole(array) for array in (*kept, cosine, sine)]
        + [whole(array) for array, _ in blocks],
        out_specs=[fixed((size, 3 * width))] * count,
        out_shape=[jax.ShapeDtypeStruct((size, 3 * width), BF16)] * count,
        scratch_shapes=[pltpu.VMEM((length, width), BF16), pltpu.VMEM((length, width), F32)]
        + [pltpu.VMEM((width, length), F32)] * 2,
        compiler_params=params(4 * count),
        cost_estimate=brief(weight),
        name="attend_back",
    )(
        pos, start_col, late, *[in_hbm(a) for a in (*kept, cosine, sine)],
        *(array for array, _ in blocks),
    )


def add_sums(i, ref, values):
    sums = [jnp.sum(value, axis=0, keepdims=True) for value in values]
    sums += [jnp.zeros_like(sums[0])] * (8 - len(sums))
    share = jnp.concatenate(sums, axis=0)

    @pl.when(i == 0)
    def _():
        ref[...] = share

    @pl.when(i > 0)
    def _():
        ref[...] += share


def mlp_back_kernel(ats, weights, flag_ref, x_ref, cot_ref, slope_ref, vec_ref, *refs):
    pre_ref, two_ref, grads_ref, bias_ref, down_ref, up_ref = refs[-6:]
    once(
        (ats[0], flag_ref, refs[:weights], down_ref),
        (ats[1], flag_ref, refs[weights : 2 * weights], up_ref),
    )
    i = pl.program_id(0)
    grad_act = dot(cot_ref[...], down_ref[0], 1, 1)
    grad_pre = (grad_act * slope_ref[...].astype(F32)).astype(BF16)
    pre_ref[...] = grad_pre
    two = dot(grad_pre, up_ref[0], 1, 1)
    hat, _ = norm_rows(x_ref[...].astype(F32))
    two_ref[...] = two * vec_ref[2:3, :]
    add_sums(i, grads_ref, (two * hat, two))
    add_sums(i, bias_ref, (grad_pre.astype(F32),))


def mlp_back(flags, rows_all, cot_all, slope, down, up, vec, block, late):
    rows, dim = rows_all.shape
    hidden = slope.shape[1]
    return pl.pallas_call(
        functools.partial(mlp_back_kernel, (down.at, up.at), len(up.arrays)),
        grid=(rows // block,),
        in_specs=[
            pl.BlockSpec(memory_space=pltpu.SMEM), row_block(block, dim), row_block(block, dim),
            row_block(block, hidden), whole(vec),
        ]
        + down.specs()
        + up.specs()
        + [pl.BlockSpec(memory_space=pl.ANY)] * len(late),
        out_specs=[
            row_block(block, hidden), row_block(block, dim), fixed((8, dim)), fixed((8, hidden)),
        ],
        out_shape=[
            jax.ShapeDtypeStruct((rows, hidden), BF16),
            jax.ShapeDtypeStruct((rows, dim), F32),
            jax.ShapeDtypeStruct((8, dim), F32),
            jax.ShapeDtypeStruct((8, hidden), F32),
        ],
        scratch_shapes=[down.scratch(), up.scratch()],
        compiler_params=params(18),
        cost_estimate=brief(8),
        name="mlp_back",
    )(
        flags, in_hbm(rows_all), in_hbm(cot_all), in_hbm(slope), vec, *down.hbm_first(),
        *up.hbm_first(), *late,
    )


def input_grad_kernel(
    at, weights, count, flag_ref, row_ref, col_ref, x_ref, two_ref, vec_ref, late_ref, *refs
):
    pieces = refs[weights : weights + count]
    dlin_ref, sum_ref, grads_ref, bias_ref, w_ref = refs[-5:]
    once((at, flag_ref, refs[:weights], w_ref))
    width = w_ref.shape[2]
    block = x_ref.shape[0]
    i = pl.program_id(0)

    @pl.when(i == 0)
    def _():
        gather_pieces(pieces, 3, row_ref, col_ref, block, dlin_ref)

    rows = pl.ds(pl.multiple_of(i * block, block), block)
    hat, _ = norm_rows(x_ref[...].astype(F32))
    dlin = dlin_ref[rows, :]
    one = dot(dlin[:, :width], w_ref[0], 1, 1)
    for part in (1, 2):
        one = one + dot(dlin[:, part * width : (part + 1) * width], w_ref[part], 1, 1)
    sum_ref[...] = (one * vec_ref[0:1, :] + two_ref[...]).astype(BF16)
    add_sums(i, grads_ref, (one * hat, one))
    add_sums(i, bias_ref, (dlin.astype(F32),))


def input_grad(flags, row_at, col_at, rows_all, pieces, weight, two_part, vec, block, late):
    rows, dim = rows_all.shape
    wide = 3 * weight.shape[2]
    return pl.pallas_call(
        functools.partial(input_grad_kernel, weight.at, len(weight.arrays), len(pieces)),
        grid_spec=pltpu.PrefetchScalarGridSpec(
            num_scalar_prefetch=3,
            grid=(rows // block,),
            in_specs=[
                row_block(block, dim), row_block(block, dim), whole(vec),
                pl.BlockSpec(memory_space=pl.ANY),
            ]
            + weight.specs()
            + [whole(p) for p in pieces],
            out_specs=[
                fixed((rows, wide)), row_block(block, dim), fixed((8, dim)), fixed((8, wide)),
            ],
            scratch_shapes=[weight.scratch()],
        ),
        out_shape=[
            jax.ShapeDtypeStruct((rows, wide), BF16),
            pltpu.HBM((rows, dim), BF16),
            jax.ShapeDtypeStruct((8, dim), F32),
            jax.ShapeDtypeStruct((8, wide), F32),
        ],
        compiler_params=params(12),
        cost_estimate=brief(),
        name="input_grad",
    )(flags, row_at, col_at, in_hbm(rows_all), two_part, vec, late, *weight.hbm_first(), *pieces)


def by_xor(axis, count, step):
    return functools.partial(
        lax.ppermute, axis_name=axis, perm=[(i, i ^ step) for i in range(count)]
    )


def nothing(*refs):
    del refs


def after(values, *others):
    anywhere = pl.BlockSpec(memory_space=pl.ANY)
    return pl.pallas_call(
        nothing,
        in_specs=[anywhere] * (1 + len(others)),
        out_specs=anywhere,
        out_shape=jax.ShapeDtypeStruct(values.shape, values.dtype),
        input_output_aliases={0: 0},
        name="after",
    )(values, *others)


def first_token(values):
    def copy(source, target):
        target[...] = source[...]

    return pl.pallas_call(
        copy, out_shape=jax.ShapeDtypeStruct(values.shape, values.dtype), name="first"
    )(values)


class Weight:
    def __init__(self, own, at, token, shards, ranks):
        self.at, shape = at, list(own.shape)
        shape[at] *= shards
        self.shape = tuple(shape)
        if shards == 2 and ranks > 1:
            half = own.shape[1] // 2
            odd = lax.axis_index("ctx") & 1
            mine = lax.dynamic_slice_in_dim(own, odd * half, half, 1)
            mine = by_xor("shard", 2, 1)(after(mine, token))
            self.arrays = [own, mine, by_xor("ctx", ranks, 1)(mine)]
            self.token = mine
        else:
            self.arrays = [lax.all_gather(own, "shard", axis=at, tiled=True)]
            self.token = token

    def specs(self):
        return [whole(a) for a in self.arrays]

    def scratch(self):
        return pltpu.VMEM(self.shape, BF16)

    def hbm_first(self):
        return [in_hbm(self.arrays[0])] + self.arrays[1:]


def join(at, flag_ref, refs, full_ref):
    if len(refs) == 1:
        full_ref[...] = refs[0][...]
        return
    rows, cols = refs[0].shape[1:]
    half = rows // 2
    side, odd = flag_ref[0], flag_ref[1] & 1
    for where, first, ref in (
        (side, 0, refs[0]), (1 - side, odd * half, refs[1]), (1 - side, (1 - odd) * half, refs[2]),
    ):
        if at == 1:
            place = pl.ds(pl.multiple_of(where * rows + first, half), ref.shape[1])
            full_ref[:, place, :] = ref[...]
        else:
            place = pl.ds(pl.multiple_of(first, half), ref.shape[1])
            full_ref[:, place, pl.ds(pl.multiple_of(where * cols, cols), cols)] = ref[...]


def once(*joins):
    @pl.when(pl.program_id(0) == 0)
    def _():
        for args in joins:
            join(*args)


def axis_bits(axes):
    return [
        (axis, count, bit)
        for axis, count in axes
        for bit in reversed(range(count.bit_length() - 1))
    ]


def split_kernel(outer, terms, bit_ref, *refs):
    sources, (away_ref, keep_ref) = refs[:terms], refs[-2:]
    size = away_ref.shape[0] // outer
    for a in range(outer):
        for ref, half in ((away_ref, 1 - bit_ref[0]), (keep_ref, bit_ref[0])):
            rows = pl.ds(pl.multiple_of((2 * a + half) * size, size), size)
            total = sources[0][rows, :].astype(F32)
            for source in sources[1:]:
                total = total + source[rows, :].astype(F32)
            ref[a * size : (a + 1) * size, :] = total.astype(BF16)


def halve_rows(terms, bits, entry):
    rows, wide = terms[0].shape
    vmem = pl.BlockSpec(memory_space=pltpu.VMEM)
    half = jax.ShapeDtypeStruct((rows // 2, wide), BF16)
    axis, count, bit = entry
    away, keep = pl.pallas_call(
        functools.partial(split_kernel, 1 << bits.index(entry), len(terms)),
        in_specs=[pl.BlockSpec(memory_space=pltpu.SMEM)] + [vmem] * len(terms),
        out_specs=[vmem, vmem],
        out_shape=[half, half],
        compiler_params=params(10),
        cost_estimate=brief(),
        name="split",
    )(((lax.axis_index(axis) >> bit) & 1)[None], *terms)
    bits.remove(entry)
    return [keep, by_xor(axis, count, 1 << bit)(away)]


def quarters_kernel(flag_ref, keep_ref, came_ref, *refs):
    outs = refs[-4:]
    size = outs[0].shape[0]
    mine = flag_ref[0] * 2 + flag_ref[1] // 2
    for step, out in enumerate(outs):
        rows = pl.ds(pl.multiple_of((mine ^ step) * size, size), size)
        out[...] = (keep_ref[rows, :].astype(F32) + came_ref[rows, :].astype(F32)).astype(BF16)


def exchange_quarters(flags, terms, late):
    rows, wide = terms[0].shape
    outs = pl.pallas_call(
        quarters_kernel,
        grid=(1,),
        in_specs=[pl.BlockSpec(memory_space=pltpu.SMEM)] + [whole(term) for term in terms]
        + [pl.BlockSpec(memory_space=pl.ANY)] * len(late),
        out_specs=[fixed((rows // 4, wide))] * 4,
        out_shape=[jax.ShapeDtypeStruct((rows // 4, wide), BF16)] * 4,
        compiler_params=params(10),
        cost_estimate=brief(),
        name="quarters",
    )(flags, in_hbm(terms[0]), terms[1], *late)
    came = [outs[0]]
    for step in range(1, 4):
        perm = [(s * 4 + c, (s ^ (step >> 1)) * 4 + (c ^ ((step & 1) * 2))) for s in range(2) for c in range(4)]
        came.append(lax.ppermute(outs[step], ("shard", "ctx"), perm))
    return came, outs[0]


def group_kernel(count, small, late, flag_ref, *refs):
    ins, (away_ref, keep_ref) = refs[: len(refs) - 2 - late], refs[-2:]
    i = pl.program_id(0)

    def values():
        for k in range(count):
            left = jnp.concatenate([ins[3 * k][...], ins[3 * k + 1][...]], axis=1)
            yield dot(left, ins[3 * k + 2][...], 0, 0).astype(BF16)
        if small:
            parts = [
                jnp.concatenate([ref[...], jnp.zeros((120, 128), F32)], axis=0).T
                for ref in ins[3 * count :]
            ]
            yield jnp.concatenate(parts, axis=0).astype(BF16)

    first = 0
    for value in values():
        last = first + value.shape[1]

        @pl.when(i == 0)
        def _(value=value, first=first, last=last):
            away_ref[:, first:last] = value

        @pl.when(i > 0)
        def _(value=value, first=first, last=last):
            keep_ref[:, first:last] = value

        first = last


def owner_columns(rows, side):
    def block(i, j, flags):
        core = jnp.where(i == 0, 1 - (flags[1] & 1), flags[1] & 1)
        return (0, 4 * j + 2 * side + core)

    return pl.BlockSpec((rows, 128), block)


def group_grad(flags, pairs, small, axes, late):
    dim = pairs[0][0].shape[1]
    owners = 1
    for _, count in axes:
        owners *= count
    bits = axis_bits(axes)
    wide = sum(right.shape[1] for _, right in pairs) + (0 if small is None else 128)
    if dim // owners != 128:
        values = [dot(left, right, 0, 0).astype(BF16) for left, right in pairs]
        if small is not None:
            values.append(jnp.pad(small.T, ((0, 0), (0, 120))).astype(BF16))
        return halve_rows([jnp.concatenate(values, axis=1)], bits, bits[-1]), bits
    steps = dim // 512
    specs, flat = [], []
    for left, right in pairs:
        specs += [owner_columns(left.shape[0], side) for side in (0, 1)] + [whole(right)]
        flat += [in_hbm(left), in_hbm(left), right]
    if small is not None:
        specs += [owner_columns(small.shape[0], side) for side in (0, 1)]
        flat += [small, small]
    away, keep = pl.pallas_call(
        functools.partial(group_kernel, len(pairs), small is not None, len(late)),
        grid_spec=pltpu.PrefetchScalarGridSpec(
            num_scalar_prefetch=1,
            grid=(2, steps),
            in_specs=specs + [pl.BlockSpec(memory_space=pl.ANY)] * len(late),
            out_specs=[
                pl.BlockSpec((256, wide), lambda i, j, flags: (jnp.where(i == 0, j, steps - 1), 0)),
                pl.BlockSpec((256, wide), lambda i, j, flags: (jnp.where(i == 0, 0, j), 0)),
            ],
        ),
        out_shape=[
            pltpu.HBM((dim // 2, wide), BF16), pltpu.HBM((dim // 2, wide), BF16),
        ],
        compiler_params=params(16),
        cost_estimate=brief(),
        name="group_grad",
    )(flags, *flat, *late)
    return [keep, by_xor("ctx", dict(axes)["ctx"], 1)(away)], bits[:-1]


def scatter_group(flags, terms, bits, late):
    if len(bits) == 2:
        return exchange_quarters(flags, terms, late)
    bits = list(bits)
    while bits:
        terms = halve_rows(terms, bits, bits[-1])
    return terms, terms[0]


def total_kernel(terms, layouts, *refs):
    outs = refs[len(refs) - len(layouts) :]
    first = 0
    for out, (kind, wide) in zip(outs, layouts):
        cols = slice(first, first + wide)
        total = refs[0][:, cols].astype(F32)
        for ref in refs[1:terms]:
            total = total + ref[:, cols].astype(F32)
        if kind == "flip":
            out[...] = total.T
        elif kind == "small":
            out[...] = total.T[:8, :]
        elif kind == "three":
            for part in range(3):
                out[part] = total[:, part * wide // 3 : (part + 1) * wide // 3]
        else:
            out[...] = total
        first += wide


def group_total(terms, layouts, late, weight):
    rows = terms[0].shape[0]
    shapes = {
        "flip": lambda w: (w, rows), "small": lambda w: (8, rows),
        "three": lambda w: (3, rows, w // 3), "keep": lambda w: (rows, w),
    }
    vmem = pl.BlockSpec(memory_space=pltpu.VMEM)
    return pl.pallas_call(
        functools.partial(total_kernel, len(terms), layouts),
        in_specs=[vmem] * len(terms) + [pl.BlockSpec(memory_space=pl.ANY)] * len(late),
        out_specs=[vmem] * len(layouts),
        out_shape=[pltpu.HBM(shapes[kind](w), F32) for kind, w in layouts],
        compiler_params=params(10),
        cost_estimate=brief(weight),
        name="group_total",
    )(*terms, *late)


def body(
    sizes, hidden_in, w_qkv, bias_qkv, w_dense, w_up, bias_up, w_down, vectors, block_deal,
    segments, cotangent,
):
    shards, ranks, tps = sizes
    rank = lax.axis_index("ctx")
    dim = hidden_in.shape[1]
    own_rows = hidden_in.shape[0]

    x_all = lax.all_gather(hidden_in, "tp", axis=0, tiled=True)
    heads = bias_qkv.shape[1]
    width = heads * HEAD
    half = vectors.shape[1]
    small = jnp.concatenate(
        [vectors.reshape(-1), bias_qkv.astype(F32).reshape(-1), bias_up.astype(F32).reshape(-1)]
    )
    pad = -small.shape[0] % 1024
    small = jnp.pad(small, (0, pad)).reshape(1, -1, 128)
    token = first_token(segments)
    if shards == 2:
        other = by_xor("shard", 2, 1)(small)
        first = lax.axis_index("shard") == 0
        small = jnp.concatenate([jnp.where(first, small, other), jnp.where(first, other, small)])
    else:
        small = lax.all_gather(small, "shard", axis=0, tiled=True)
    small = small.reshape(shards, -1)
    cut = 6 * half
    vec = small[:, :cut].reshape(shards, 6, half).transpose(1, 0, 2).reshape(6, dim)
    vec = jnp.pad(vec, ((0, 2), (0, 0)))
    share = bias_qkv.size
    qkv_bias = small[:, cut : cut + share].reshape((shards,) + bias_qkv.shape)
    qkv_bias = qkv_bias.transpose(1, 2, 0, 3).reshape(3, width)
    up_bias = small[:, cut + share : cut + share + bias_up.size].reshape((shards,) + bias_up.shape)
    up_bias = up_bias.transpose(1, 0, 2).reshape(1, -1)
    flags = jnp.stack([lax.axis_index("shard"), rank])
    weight_qkv = Weight(w_qkv, 1, token, shards, ranks)
    weight_up = Weight(w_up[None], 1, token, shards, ranks)
    weight_down = Weight(w_down[None], 2, token, shards, ranks)
    weight_dense = Weight(w_dense[None], 2, token, shards, ranks)

    deal = block_deal[0]
    seg_row = segments[0]
    group = seg_row.shape[0]
    block = group // deal.shape[0]
    quarters = deal.shape[0] // ranks
    rank_rows = quarters * block
    split = ranks // quarters
    pieces = width // split // GROUP
    length = group // quarters
    at = jnp.arange(group, dtype=jnp.int32)
    previous = jnp.concatenate([seg_row[:1] - 1, seg_row[:-1]])
    begins = lax.cummax(jnp.where(seg_row != previous, at, 0), axis=0)
    places = (at - begins).reshape(deal.shape[0], block)
    deal_by_rank = deal.reshape(ranks, quarters)
    my_deal = lax.dynamic_index_in_dim(deal_by_rank, rank, 0, keepdims=False)
    picked = my_deal[:, None] == jnp.arange(deal.shape[0], dtype=jnp.int32)[None, :]
    rank_place = jnp.sum(jnp.where(picked[:, :, None], places[None], 0), axis=1).reshape(-1)
    quarter = rank // split
    partners = rank ^ jnp.arange(ranks, dtype=jnp.int32)
    in_quarter = jnp.take(lax.dynamic_index_in_dim(deal_by_rank, quarter, 1, keepdims=False), partners)
    pos = in_quarter - quarter * ranks
    my_begins = lax.dynamic_slice_in_dim(begins, quarter * length, length) - quarter * length
    quarter_place = jnp.arange(length, dtype=jnp.int32) - my_begins
    start_col = my_begins[:, None]
    lane = jnp.arange(128, dtype=jnp.int32) % HEAD
    frequency = ROPE_BASE ** (-2.0 * (lane % (ROT // 2)).astype(F32) / ROT)
    frequency = jnp.where(lane < ROT, frequency, 0.0)
    sign = jnp.where(lane < ROT // 2, -1.0, 1.0)
    all_places = jnp.concatenate([rank_place, quarter_place]).astype(F32)
    angles = all_places[:, None] * frequency[None, :]
    cosine, sine = jnp.cos(angles), jnp.sin(angles) * sign[None, :]
    target_row, target_col = partners // split, partners % split

    cot_rows = cotangent.astype(F32)
    cot_sum = jnp.sum(cot_rows, axis=0, keepdims=True)
    ready = after(cotangent, cot_sum, vec, qkv_bias, up_bias, cosine, sine, start_col, pos)
    cot_all = lax.all_gather(ready, "tp", axis=0, tiled=True)

    full_one, sent = project(
        flags, split, ranks, x_all, vec, weight_qkv, qkv_bias, cosine[:rank_rows],
        sine[:rank_rows], block, weight_up.arrays + weight_down.arrays + weight_dense.arrays,
    )

    def swap(sent):
        return [by_xor("ctx", ranks, s)(piece) if s else piece for s, piece in enumerate(sent)]

    arrived = exchange(sent, pieces, ranks, 2)
    full_two, activated, slope = mlp(
        flags, x_all, vec, weight_up, up_bias, block, sent[0]
    )
    outs, kept, late = [], [], in_hbm(slope)
    for p in range(pieces):
        out, keep = attend(pos, start_col, arrived[p], late, outs[0][1:] if p else [])
        outs.append(out)
        kept.append(keep)
        late = out[0]
    out_pieces = [out[0] for out in outs] + swap(outs[-1])[1:]

    axes = (("shard", shards), ("ctx", ranks))
    tables = (cosine[rank_rows:], sine[rank_rows:])
    part = mlp_down(flags, activated, weight_down, block, late)
    attended, partial = out_partial(
        flags, target_row, target_col, out_pieces, part, weight_dense, block
    )
    summed = lax.psum_scatter(partial, "tp", scatter_dimension=0, tiled=True)
    sent = attn_grad(flags, split, ranks, cot_all, weight_dense, block, [in_hbm(partial)])
    arrived = exchange(sent, pieces, ranks, ranks)
    first, bits = group_grad(flags, [(cot_all, activated)], None, axes, (sent[0],))
    grad_pieces, late = [], in_hbm(first[0])
    for p in range(pieces):
        grads = attend_back(pos, start_col, kept[p], *tables, arrived[p], late, 0 if p else 6)
        grad_pieces += swap(grads)
        late = grads[0]
    grad_pre, two_part, two_sums, grad_ubias = mlp_back(
        flags, x_all, cot_all, slope, weight_down, weight_up, vec, block,
        grad_pieces[: ranks * (pieces - 1)] + [late],
    )
    second, _ = group_grad(flags, [(full_two, grad_pre)], None, axes, (first[1],) if len(first) > 1 else ())
    dlin, row_sum, one_sums, grad_qbias = input_grad(
        flags, target_row, target_col, x_all, grad_pieces, weight_qkv, two_part, vec, block,
        in_hbm(second[0]),
    )
    first, late = scatter_group(flags, first, bits, (dlin,))
    own_sum = lax.psum_scatter(after(row_sum, summed), "tp", scatter_dimension=0, tiled=True)

    owners = shards * ranks
    each, share = HEAD // owners, dim // owners

    def by_owner(row, lines):
        row = row.reshape(lines, owners, each).transpose(1, 0, 2).reshape(owners, -1)
        return jnp.pad(row, ((0, 0), (0, share - lines * each))).reshape(1, dim)

    small_rows = jnp.concatenate(
        [
            one_sums[:2], two_sums[:2], cot_sum, cot_sum,
            by_owner(grad_qbias[0], 3 * heads), by_owner(grad_ubias[0], bias_up.shape[0]),
        ],
        axis=0,
    )
    hidden, wide = weight_up.shape[2], 3 * width
    third, _ = group_grad(
        flags, [(full_one, dlin), (cot_all, attended)], small_rows, axes, (late,)
    )
    (grad_down,) = group_total(first, (("flip", hidden),), (in_hbm(third[0]),), 12)
    third, late = scatter_group(flags, third, bits, (in_hbm(grad_down),))
    second, late = scatter_group(flags, second, bits, (late,))
    grad_qkv, grad_dense, small_rows = group_total(
        third, (("three", wide), ("flip", width), ("small", 128)), (late,), 4
    )
    rows_in = hidden_in.astype(F32)
    output = (rows_in + summed.astype(F32) + vec[4:5] + vec[5:6]).astype(BF16)
    own_sum = after(own_sum, in_hbm(grad_dense)).astype(F32)
    hat, inverse = norm_rows(rows_in)
    centered = own_sum - jnp.mean(own_sum, axis=-1, keepdims=True)
    along = jnp.mean(own_sum * hat, axis=-1, keepdims=True)
    grad_in = (cot_rows + inverse * (centered - hat * along)).astype(BF16)
    grad_vec = small_rows[:6].reshape((6,) + (2,) * (tps.bit_length() - 1) + (-1,))
    for bit in reversed(range(tps.bit_length() - 1)):
        mine = (lax.axis_index("tp") >> bit) & 1
        keep = lax.dynamic_index_in_dim(grad_vec, mine, 1, keepdims=False)
        away = lax.dynamic_index_in_dim(grad_vec, 1 - mine, 1, keepdims=False)
        if bit == 0:
            away = after(away, in_hbm(grad_in))
        grad_vec = keep + by_xor("tp", tps, 1 << bit)(away)
    grad_qbias = small_rows[6, : 3 * heads * each].reshape(3, heads, each)
    grad_ubias = small_rows[7, : bias_up.shape[0] * each].reshape(bias_up.shape[0], each)

    (grad_up,) = group_total(second, (("keep", hidden),), (in_hbm(grad_in),), 0)
    return (
        output, grad_in, grad_qkv, grad_qbias, grad_dense, grad_up, grad_ubias, grad_down,
        grad_vec,
    )


def solution(mesh):
    sizes = tuple(mesh.shape[name] for name in ("shard", "ctx", "tp"))
    return jax.shard_map(
        functools.partial(body, sizes),
        mesh=mesh,
        in_specs=(
            P(("shard", "ctx", "tp"), None),
            P(None, "shard", "tp"),
            P(None, "tp", "shard"),
            P("tp", "shard"),
            P("shard", "tp"),
            P("tp", "shard"),
            P("tp", "shard"),
            P(None, "shard"),
            P("shard", None),
            P("shard", None),
            P(("shard", "ctx", "tp"), None),
        ),
        out_specs=(
            P(("shard", "ctx", "tp"), None),
            P(("shard", "ctx", "tp"), None),
            P(None, ("shard", "ctx"), "tp"),
            P(None, "tp", ("shard", "ctx")),
            P("tp", ("shard", "ctx")),
            P(("shard", "ctx"), "tp"),
            P("tp", ("shard", "ctx")),
            P("tp", ("shard", "ctx")),
            P(None, ("shard", "ctx", "tp")),
        ),
        check_vma=False,
    )
```

```python
import functools

import jax
import jax.numpy as jnp
from jax import lax
from jax.experimental import pallas as pl
from jax.experimental.pallas import tpu as pltpu
from jax.sharding import PartitionSpec as P

HEAD = 64
GROUP = 128
ROT = 16
NORM_EPS = 1e-05
SCORE_SCALE = 0.125
ROPE_BASE = 10000.0
MASK_FILL = 1e30
F32 = jnp.float32
BF16 = jnp.bfloat16


def dot(left, right, left_dim=1, right_dim=0):
    return lax.dot_general(
        left, right, (((left_dim,), (right_dim,)), ((), ())), preferred_element_type=F32
    )


def params(mib=20):
    return pltpu.CompilerParams(vmem_limit_bytes=mib * 1024 * 1024)


def brief(us=0):
    return pl.CostEstimate(flops=int(us * 1.1e9) + 1, bytes_accessed=1, transcendentals=0)


def swap_halves(values):
    width = values.shape[-1]
    lane = lax.broadcasted_iota(jnp.int32, (1, width), 1) % HEAD
    ahead = pltpu.roll(values, width - ROT // 2, 1)
    behind = pltpu.roll(values, ROT // 2, 1)
    return jnp.where(lane < ROT // 2, ahead, behind)


def widen(table, width):
    return jnp.concatenate([table] * (width // table.shape[-1]), axis=-1)


def norm_rows(rows):
    center = rows - jnp.mean(rows, axis=-1, keepdims=True)
    inverse = lax.rsqrt(jnp.mean(center * center, axis=-1, keepdims=True) + NORM_EPS)
    return center * inverse, inverse


def whole(array):
    return pl.BlockSpec(
        array.shape, lambda *ids: (0,) * array.ndim, pipeline_mode=pl.Buffered(buffer_count=1)
    )


def in_hbm(array):
    return pltpu.with_memory_space_constraint(array, pltpu.HBM)


def row_block(block, cols):
    return pl.BlockSpec((block, cols), lambda i, *ids: (i, 0))


def piece_shapes(pieces, ranks, merged, shape):
    shapes = []
    for step in range(ranks):
        if 0 < step < merged:
            shapes.append((pieces,) + shape)
        else:
            shapes += [(1,) + shape] * pieces
    return shapes


def by_step(flat, pieces, ranks, merged):
    steps, at = [], 0
    for step in range(ranks):
        count = 1 if 0 < step < merged else pieces
        steps.append(flat[at : at + count])
        at += count
    return steps


def send_pieces(i, split, merged, flag_ref, flat, groups_ref, ranks):
    pieces = groups_ref.shape[0] // split
    for step, refs in enumerate(by_step(flat, pieces, ranks, merged)):

        @pl.when(i == step // split)
        def _(step=step, refs=refs):
            for p in range(pieces):
                group = p
                if split > 1:
                    group = ((flag_ref[1] ^ step) % split) * pieces + p
                if len(refs) == 1:
                    refs[0][p] = groups_ref[group]
                else:
                    refs[p][0] = groups_ref[group]


def exchange(flat, pieces, ranks, merged):
    came = [[] for _ in range(pieces)]
    for step, arrays in enumerate(by_step(flat, pieces, ranks, merged)):
        if step:
            arrays = [by_xor("ctx", ranks, step)(array) for array in arrays]
        for p in range(pieces):
            came[p].append((arrays[0], p) if len(arrays) == 1 else (arrays[p], 0))
    return came


def quarter_block(block, cols, split):
    return pl.BlockSpec((block, cols), lambda i, flags: ((flags[1] // split) ^ i, 0))


def fixed(shape):
    return pl.BlockSpec(shape, lambda *ids: (0,) * len(shape))


def qkv_kernel(
    split, ranks, at, weights, late, flag_ref, x_ref, vec_ref, bias_ref, cos_ref, sin_ref, *refs
):
    refs = refs[:weights] + refs[weights + late :]
    one_ref, groups_ref, w_ref = refs[weights], refs[-2], refs[-1]
    once((at, flag_ref, refs[:weights], w_ref))
    i = pl.program_id(0)
    hat, _ = norm_rows(x_ref[...].astype(F32))
    one = (hat * vec_ref[0:1, :] + vec_ref[1:2, :]).astype(BF16)
    one_ref[...] = one
    width = w_ref.shape[2]
    cosine, sine = widen(cos_ref[...], width), widen(sin_ref[...], width)
    for part in range(3):
        lin = dot(one, w_ref[part]) + bias_ref[part : part + 1, :]
        if part < 2:
            lin = lin * cosine + swap_halves(lin) * sine
        if part == 0:
            lin = lin * SCORE_SCALE
        low = lin.astype(BF16)
        for g in range(width // GROUP):
            groups_ref[g, :, part * GROUP : (part + 1) * GROUP] = low[:, g * GROUP : (g + 1) * GROUP]
    send_pieces(i, split, 2, flag_ref, refs[weights + 1 : -2], groups_ref, ranks)


def project(flags, split, ranks, rows_all, vec, weight, bias, cosine, sine, block, late):
    rows, dim = rows_all.shape
    width = weight.shape[2]
    groups = width // GROUP
    piece = (block, 3 * GROUP)
    shapes = piece_shapes(groups // split, ranks, 2, piece)
    result = pl.pallas_call(
        functools.partial(
            qkv_kernel, split, ranks, weight.at, len(weight.arrays), len(late)
        ),
        grid_spec=pltpu.PrefetchScalarGridSpec(
            num_scalar_prefetch=1,
            grid=(rows // block,),
            in_specs=[
                quarter_block(block, dim, split), whole(vec), whole(bias),
                quarter_block(block, cosine.shape[1], split),
                quarter_block(block, sine.shape[1], split),
            ]
            + weight.specs()
            + [pl.BlockSpec(memory_space=pl.ANY)] * len(late),
            out_specs=[quarter_block(block, dim, split)] + [fixed(shape) for shape in shapes],
            scratch_shapes=[pltpu.VMEM((groups,) + piece, BF16), weight.scratch()],
        ),
        out_shape=[pltpu.HBM((rows, dim), BF16)]
        + [jax.ShapeDtypeStruct(shape, BF16) for shape in shapes],
        compiler_params=params(12),
        cost_estimate=brief(300),
        name="norm_qkv",
    )(
        flags, in_hbm(rows_all), vec, bias, in_hbm(cosine), in_hbm(sine), *weight.hbm_first(),
        *late,
    )
    return result[0], result[1:]


def attn_grad_kernel(split, ranks, at, weights, late, flag_ref, cot_ref, *refs):
    refs = refs[:weights] + refs[weights + late :]
    groups_ref, w_ref = refs[-2:]
    once((at, flag_ref, refs[:weights], w_ref))
    grad = dot(cot_ref[...], w_ref[0], 1, 1).astype(BF16)
    for g in range(groups_ref.shape[0]):
        groups_ref[g] = grad[:, g * GROUP : (g + 1) * GROUP]
    send_pieces(pl.program_id(0), split, ranks, flag_ref, refs[weights:-2], groups_ref, ranks)


def attn_grad(flags, split, ranks, cot_all, weight, block, late):
    rows, dim = cot_all.shape
    groups = weight.shape[1] // GROUP
    piece = (block, GROUP)
    shapes = piece_shapes(groups // split, ranks, ranks, piece)
    result = pl.pallas_call(
        functools.partial(
            attn_grad_kernel, split, ranks, weight.at, len(weight.arrays), len(late)
        ),
        grid_spec=pltpu.PrefetchScalarGridSpec(
            num_scalar_prefetch=1,
            grid=(rows // block,),
            in_specs=[quarter_block(block, dim, split)]
            + weight.specs()
            + [pl.BlockSpec(memory_space=pl.ANY)] * len(late),
            out_specs=[fixed(shape) for shape in shapes],
            scratch_shapes=[pltpu.VMEM((groups,) + piece, BF16), weight.scratch()],
        ),
        out_shape=[jax.ShapeDtypeStruct(shape, BF16) for shape in shapes],
        compiler_params=params(8),
        cost_estimate=brief(300),
        name="attn_grad",
    )(flags, in_hbm(cot_all), *weight.hbm_first(), *late)
    return result


def mlp_kernel(at, weights, flag_ref, x_ref, vec_ref, bias_ref, late_ref, *refs):
    two_ref, act_ref, slope_ref, up_ref = refs[-4:]
    once((at, flag_ref, refs[:weights], up_ref))
    hat, _ = norm_rows(x_ref[...].astype(F32))
    two = (hat * vec_ref[2:3, :] + vec_ref[3:4, :]).astype(BF16)
    two_ref[...] = two
    pre = dot(two, up_ref[0]) + bias_ref[...]
    phi = 0.5 * (1.0 + lax.erf(pre * 0.7071067811865476))
    act = (pre * phi).astype(BF16)
    act_ref[...] = act
    slope = phi + pre * (0.3989422804014327 * jnp.exp(-0.5 * pre * pre))
    slope_ref[...] = slope.astype(BF16)


def mlp(flags, rows_all, vec, up, bias, block, late):
    rows, dim = rows_all.shape
    hidden = up.shape[2]
    return pl.pallas_call(
        functools.partial(mlp_kernel, up.at, len(up.arrays)),
        grid=(rows // block,),
        in_specs=[
            pl.BlockSpec(memory_space=pltpu.SMEM), row_block(block, dim), whole(vec), whole(bias),
            pl.BlockSpec(memory_space=pl.ANY),
        ]
        + up.specs(),
        out_specs=[row_block(block, dim), row_block(block, hidden), row_block(block, hidden)],
        out_shape=[
            pltpu.HBM((rows, dim), BF16),
            pltpu.HBM((rows, hidden), BF16),
            pltpu.HBM((rows, hidden), BF16),
        ],
        scratch_shapes=[up.scratch()],
        compiler_params=params(18),
        cost_estimate=brief(),
        name="mlp",
    )(flags, in_hbm(rows_all), vec, bias, late, *up.hbm_first())


def gather_pieces(pieces, parts, row_ref, col_ref, size, out_ref):
    full = out_ref.shape[1] // parts
    ranks = row_ref.shape[0]
    count = len(pieces) // ranks
    for index, piece in enumerate(pieces):
        r, p = index % ranks, index // ranks
        rows = pl.ds(pl.multiple_of(row_ref[r] * size, size), size)
        for part in range(parts):
            values = piece[:, part * GROUP : (part + 1) * GROUP]
            if count * GROUP == full:
                out_ref[rows, part * full + p * GROUP : part * full + (p + 1) * GROUP] = values
            else:
                column = part * full + (col_ref[r] * count + p) * GROUP
                out_ref[rows, pl.ds(pl.multiple_of(column, GROUP), GROUP)] = values


def down_kernel(at, weights, flag_ref, act_ref, late_ref, *refs):
    out_ref, down_ref = refs[-2:]
    once((at, flag_ref, refs[:weights], down_ref))
    out_ref[...] = dot(act_ref[...], down_ref[0])


def mlp_down(flags, activated, down, block, late):
    rows, hidden = activated.shape
    dim = down.shape[2]
    return pl.pallas_call(
        functools.partial(down_kernel, down.at, len(down.arrays)),
        grid=(rows // block,),
        in_specs=[
            pl.BlockSpec(memory_space=pltpu.SMEM), row_block(block, hidden),
            pl.BlockSpec(memory_space=pl.ANY),
        ]
        + down.specs(),
        out_specs=row_block(block, dim),
        out_shape=jax.ShapeDtypeStruct((rows, dim), F32),
        scratch_shapes=[down.scratch()],
        compiler_params=params(14),
        cost_estimate=brief(),
        name="mlp_down",
    )(flags, in_hbm(activated), late, *down.hbm_first())


def out_kernel(at, weights, count, flag_ref, row_ref, col_ref, part_ref, *refs):
    pieces = refs[weights : weights + count]
    attended_ref, out_ref, w_ref = refs[-3:]
    once((at, flag_ref, refs[:weights], w_ref))
    i = pl.program_id(0)
    block = out_ref.shape[0]

    @pl.when(i == 0)
    def _():
        ranks = row_ref.shape[0]
        local = len(pieces) - ranks + 1
        flat = []
        for p in range(local):
            flat += [pieces[p]] + [ref.at[p] if local > 1 else ref for ref in pieces[local:]]
        gather_pieces(flat, 1, row_ref, col_ref, block, attended_ref)

    rows = pl.ds(pl.multiple_of(i * block, block), block)
    out_ref[...] = (part_ref[...] + dot(attended_ref[rows, :], w_ref[0])).astype(BF16)


def out_partial(flags, row_at, col_at, pieces, part, dense, block):
    rows = part.shape[0]
    width, dim = dense.shape[1:]
    return pl.pallas_call(
        functools.partial(out_kernel, dense.at, len(dense.arrays), len(pieces)),
        grid_spec=pltpu.PrefetchScalarGridSpec(
            num_scalar_prefetch=3,
            grid=(rows // block,),
            in_specs=[row_block(block, dim)] + dense.specs() + [whole(p) for p in pieces],
            out_specs=[fixed((rows, width)), row_block(block, dim)],
            scratch_shapes=[dense.scratch()],
        ),
        out_shape=[pltpu.HBM((rows, width), BF16), pltpu.HBM((rows, dim), BF16)],
        compiler_params=params(12),
        cost_estimate=brief(),
        name="out_partial",
    )(flags, row_at, col_at, part, *dense.hbm_first(), *pieces)


def pair_bias(start_ref, first, size, keys):
    query_at = lax.broadcasted_iota(jnp.int32, (size, keys), 0) + first
    key_at = lax.broadcasted_iota(jnp.int32, (size, keys), 1)
    allowed = (key_at <= query_at) & (key_at >= start_ref[first : first + size, :])
    return jnp.where(allowed, 0.0, -MASK_FILL)


def attn_fwd_kernel(at, before, pos_ref, start_ref, late_ref, *refs):
    count = len(at)
    blocks = [ref.at[p] for ref, p in zip(refs, at)]
    earlier, refs = refs[count : count + before], refs[count + before :]
    outs, refs = refs[:count], refs[count:]
    for source, target in zip(earlier, outs[1:]):
        target[0] = source[...]
    outs = [outs[0]] + [ref.at[1] if before else ref for ref in outs[1:]]
    q_ref, k_ref, v_ref, lse_ref, o_ref = refs
    size, width = outs[0].shape
    for r in range(count):
        rows = pl.ds(pl.multiple_of(pos_ref[r] * size, size), size)
        q_ref[rows, :] = blocks[r][:, :width]
        k_ref[rows, :] = blocks[r][:, width : 2 * width]
        v_ref[rows, :] = blocks[r][:, 2 * width :]
    group = lax.broadcasted_iota(jnp.int32, (1, width), 1) // HEAD
    lane = lax.broadcasted_iota(jnp.int32, (1, 128), 1)
    zero, unit = jnp.zeros((), BF16), jnp.ones((), BF16)
    for i in range(count):
        first, keys = i * size, (i + 1) * size
        bias = pair_bias(start_ref, first, size, keys)
        query = q_ref[first:keys, :]
        total = jnp.zeros((size, width), F32)
        tops = jnp.zeros((size, 128), F32)
        heads = range(width // HEAD)
        scores = [
            dot(jnp.where(group == head, query, zero), k_ref[:keys, :], 1, 1) + bias
            for head in heads
        ]
        highest = [jnp.max(score, axis=-1, keepdims=True) for score in scores]
        terms = [jnp.exp(score - top).astype(BF16) for score, top in zip(scores, highest)]
        for head in heads:
            mine = group == head
            other = HEAD if head == 0 else 0
            mixed = dot(terms[head], jnp.where(mine, v_ref[:keys, :], unit))
            row_sum = mixed[:, other : other + 1]
            total = jnp.where(mine, mixed * (1.0 / row_sum), total)
            tops = jnp.where(lane == head, highest[head] + jnp.log(row_sum), tops)
        o_ref[first:keys, :] = total
        lse_ref[first:keys, :] = tops
    for r in range(count):
        rows = pl.ds(pl.multiple_of(pos_ref[r] * size, size), size)
        outs[r][...] = o_ref[rows, :].astype(BF16)


def attend(pos, start_col, blocks, late, earlier):
    count = len(blocks)
    size, wide = blocks[0][0].shape[1:]
    width, length = wide // 3, size * count
    shapes = [(size, width)] + [((2,) if earlier else ()) + (size, width)] * (count - 1)
    result = pl.pallas_call(
        functools.partial(attn_fwd_kernel, tuple(p for _, p in blocks), len(earlier)),
        grid=(1,),
        in_specs=[
            pl.BlockSpec(memory_space=pltpu.SMEM), whole(start_col),
            pl.BlockSpec(memory_space=pl.ANY),
        ]
        + [whole(array) for array, _ in blocks]
        + [whole(array) for array in earlier],
        out_specs=[fixed(shape) for shape in shapes]
        + [fixed((length, width))] * 3
        + [fixed((length, 128))],
        out_shape=[jax.ShapeDtypeStruct(shape, BF16) for shape in shapes]
        + [pltpu.HBM((length, width), BF16)] * 3
        + [pltpu.HBM((length, 128), F32)],
        scratch_shapes=[pltpu.VMEM((length, width), F32)],
        compiler_params=params(3 * count),
        cost_estimate=brief(),
        name="attend",
    )(pos, start_col, late, *(array for array, _ in blocks), *earlier)
    return list(result[:count]), result[count:]


def attn_bwd_kernel(at, pos_ref, start_ref, late_ref, q_ref, k_ref, v_ref, lse_ref, cos_ref, sin_ref, *refs):
    count = len(at)
    blocks, outs = [ref.at[p] for ref, p in zip(refs, at)], refs[count : 2 * count]
    do_ref, dq_ref, dk_ref, dv_ref = refs[2 * count :]
    size, width = blocks[0].shape
    for r in range(count):
        rows = pl.ds(pl.multiple_of(pos_ref[r] * size, size), size)
        do_ref[rows, :] = blocks[r][...]
    dk_ref[...] = jnp.zeros_like(dk_ref)
    dv_ref[...] = jnp.zeros_like(dv_ref)
    group = lax.broadcasted_iota(jnp.int32, (1, width), 1) // HEAD
    zero = jnp.zeros((), BF16)
    for i in range(count):
        first, keys = i * size, (i + 1) * size
        bias = pair_bias(start_ref, first, size, keys)
        query, grad_out = q_ref[first:keys, :], do_ref[first:keys, :]
        query_t, grad_out_t = query.T, grad_out.T
        total = jnp.zeros((size, width), F32)
        heads = range(width // HEAD)
        scores = [
            dot(jnp.where(group == head, query, zero), k_ref[:keys, :], 1, 1) + bias
            for head in heads
        ]
        grad_probs = [
            dot(jnp.where(group == head, grad_out, zero), v_ref[:keys, :], 1, 1) for head in heads
        ]
        probs = [
            jnp.exp(scores[head] - lse_ref[first:keys, head : head + 1]) for head in heads
        ]
        for head in heads:
            rows = slice(head * HEAD, (head + 1) * HEAD)
            dv_ref[rows, :keys] += dot(grad_out_t[rows, :], probs[head].astype(BF16))
        for head in heads:
            rows = slice(head * HEAD, (head + 1) * HEAD)
            weighted = probs[head] * grad_probs[head]
            delta = jnp.sum(weighted, axis=-1, keepdims=True)
            grad_score = (probs[head] * (grad_probs[head] - delta)).astype(BF16)
            total = total + dot(grad_score, jnp.where(group == head, k_ref[:keys, :], zero))
            dk_ref[rows, :keys] += dot(query_t[rows, :], grad_score)
        dq_ref[first:keys, :] = total * SCORE_SCALE
    dk = dk_ref[...].T
    dv = dv_ref[...].T
    cosine, sine = cos_ref[...], sin_ref[...]
    key_grad = dk * cosine - swap_halves(dk) * sine
    grad = dq_ref[...]
    dq_ref[...] = grad * cosine - swap_halves(grad) * sine
    do_ref[...] = dv.astype(BF16)
    for r in range(count):
        rows = pl.ds(pl.multiple_of(pos_ref[r] * size, size), size)
        outs[r][:, :width] = dq_ref[rows, :].astype(BF16)
        outs[r][:, 2 * width :] = do_ref[rows, :]
    dq_ref[...] = key_grad
    for r in range(count):
        rows = pl.ds(pl.multiple_of(pos_ref[r] * size, size), size)
        outs[r][:, width : 2 * width] = dq_ref[rows, :].astype(BF16)


def attend_back(pos, start_col, kept, cosine, sine, blocks, late, weight):
    count = len(blocks)
    size, width = blocks[0][0].shape[1:]
    length = size * count
    return pl.pallas_call(
        functools.partial(attn_bwd_kernel, tuple(p for _, p in blocks)),
        grid=(1,),
        in_specs=[
            pl.BlockSpec(memory_space=pltpu.SMEM), whole(start_col),
            pl.BlockSpec(memory_space=pl.ANY),
        ]
        + [whole(array) for array in (*kept, cosine, sine)]
        + [whole(array) for array, _ in blocks],
        out_specs=[fixed((size, 3 * width))] * count,
        out_shape=[jax.ShapeDtypeStruct((size, 3 * width), BF16)] * count,
        scratch_shapes=[pltpu.VMEM((length, width), BF16), pltpu.VMEM((length, width), F32)]
        + [pltpu.VMEM((width, length), F32)] * 2,
        compiler_params=params(4 * count),
        cost_estimate=brief(weight),
        name="attend_back",
    )(
        pos, start_col, late, *[in_hbm(a) for a in (*kept, cosine, sine)],
        *(array for array, _ in blocks),
    )


def add_sums(i, ref, values):
    sums = [jnp.sum(value, axis=0, keepdims=True) for value in values]
    sums += [jnp.zeros_like(sums[0])] * (8 - len(sums))
    share = jnp.concatenate(sums, axis=0)

    @pl.when(i == 0)
    def _():
        ref[...] = share

    @pl.when(i > 0)
    def _():
        ref[...] += share


def mlp_back_kernel(ats, weights, flag_ref, x_ref, cot_ref, slope_ref, vec_ref, *refs):
    pre_ref, two_ref, grads_ref, bias_ref, down_ref, up_ref = refs[-6:]
    once(
        (ats[0], flag_ref, refs[:weights], down_ref),
        (ats[1], flag_ref, refs[weights : 2 * weights], up_ref),
    )
    i = pl.program_id(0)
    grad_act = dot(cot_ref[...], down_ref[0], 1, 1)
    grad_pre = (grad_act * slope_ref[...].astype(F32)).astype(BF16)
    pre_ref[...] = grad_pre
    two = dot(grad_pre, up_ref[0], 1, 1)
    hat, _ = norm_rows(x_ref[...].astype(F32))
    two_ref[...] = two * vec_ref[2:3, :]
    add_sums(i, grads_ref, (two * hat, two))
    add_sums(i, bias_ref, (grad_pre.astype(F32),))


def mlp_back(flags, rows_all, cot_all, slope, down, up, vec, block, late):
    rows, dim = rows_all.shape
    hidden = slope.shape[1]
    return pl.pallas_call(
        functools.partial(mlp_back_kernel, (down.at, up.at), len(up.arrays)),
        grid=(rows // block,),
        in_specs=[
            pl.BlockSpec(memory_space=pltpu.SMEM), row_block(block, dim), row_block(block, dim),
            row_block(block, hidden), whole(vec),
        ]
        + down.specs()
        + up.specs()
        + [pl.BlockSpec(memory_space=pl.ANY)] * len(late),
        out_specs=[
            row_block(block, hidden), row_block(block, dim), fixed((8, dim)), fixed((8, hidden)),
        ],
        out_shape=[
            pltpu.HBM((rows, hidden), BF16),
            jax.ShapeDtypeStruct((rows, dim), F32),
            jax.ShapeDtypeStruct((8, dim), F32),
            jax.ShapeDtypeStruct((8, hidden), F32),
        ],
        scratch_shapes=[down.scratch(), up.scratch()],
        compiler_params=params(18),
        cost_estimate=brief(8),
        name="mlp_back",
    )(
        flags, in_hbm(rows_all), in_hbm(cot_all), in_hbm(slope), vec, *down.hbm_first(),
        *up.hbm_first(), *late,
    )


def input_grad_kernel(
    at, weights, count, flag_ref, row_ref, col_ref, x_ref, two_ref, vec_ref, late_ref, *refs
):
    pieces = refs[weights : weights + count]
    dlin_ref, sum_ref, grads_ref, bias_ref, w_ref = refs[-5:]
    once((at, flag_ref, refs[:weights], w_ref))
    width = w_ref.shape[2]
    block = x_ref.shape[0]
    i = pl.program_id(0)

    @pl.when(i == 0)
    def _():
        gather_pieces(pieces, 3, row_ref, col_ref, block, dlin_ref)

    rows = pl.ds(pl.multiple_of(i * block, block), block)
    hat, _ = norm_rows(x_ref[...].astype(F32))
    dlin = dlin_ref[rows, :]
    one = dot(dlin[:, :width], w_ref[0], 1, 1)
    for part in (1, 2):
        one = one + dot(dlin[:, part * width : (part + 1) * width], w_ref[part], 1, 1)
    sum_ref[...] = (one * vec_ref[0:1, :] + two_ref[...]).astype(BF16)
    add_sums(i, grads_ref, (one * hat, one))
    add_sums(i, bias_ref, (dlin.astype(F32),))


def input_grad(flags, row_at, col_at, rows_all, pieces, weight, two_part, vec, block, late):
    rows, dim = rows_all.shape
    wide = 3 * weight.shape[2]
    return pl.pallas_call(
        functools.partial(input_grad_kernel, weight.at, len(weight.arrays), len(pieces)),
        grid_spec=pltpu.PrefetchScalarGridSpec(
            num_scalar_prefetch=3,
            grid=(rows // block,),
            in_specs=[
                row_block(block, dim), row_block(block, dim), whole(vec),
                pl.BlockSpec(memory_space=pl.ANY),
            ]
            + weight.specs()
            + [whole(p) for p in pieces],
            out_specs=[
                fixed((rows, wide)), row_block(block, dim), fixed((8, dim)), fixed((8, wide)),
            ],
            scratch_shapes=[weight.scratch()],
        ),
        out_shape=[
            jax.ShapeDtypeStruct((rows, wide), BF16),
            pltpu.HBM((rows, dim), BF16),
            jax.ShapeDtypeStruct((8, dim), F32),
            jax.ShapeDtypeStruct((8, wide), F32),
        ],
        compiler_params=params(12),
        cost_estimate=brief(),
        name="input_grad",
    )(flags, row_at, col_at, in_hbm(rows_all), two_part, vec, late, *weight.hbm_first(), *pieces)


def by_xor(axis, count, step):
    return functools.partial(
        lax.ppermute, axis_name=axis, perm=[(i, i ^ step) for i in range(count)]
    )


def nothing(*refs):
    del refs


def after(values, *others):
    anywhere = pl.BlockSpec(memory_space=pl.ANY)
    return pl.pallas_call(
        nothing,
        in_specs=[anywhere] * (1 + len(others)),
        out_specs=anywhere,
        out_shape=jax.ShapeDtypeStruct(values.shape, values.dtype),
        input_output_aliases={0: 0},
        name="after",
    )(values, *others)


def first_token(values):
    def copy(source, target):
        target[...] = source[...]

    return pl.pallas_call(
        copy, out_shape=jax.ShapeDtypeStruct(values.shape, values.dtype), name="first"
    )(values)


class Weight:
    def __init__(self, own, at, token, shards, ranks):
        self.at, shape = at, list(own.shape)
        shape[at] *= shards
        self.shape = tuple(shape)
        if shards == 2 and ranks > 1:
            half = own.shape[1] // 2
            odd = lax.axis_index("ctx") & 1
            mine = lax.dynamic_slice_in_dim(own, odd * half, half, 1)
            mine = by_xor("shard", 2, 1)(after(mine, token))
            self.arrays = [own, mine, by_xor("ctx", ranks, 1)(mine)]
            self.token = mine
        else:
            self.arrays = [lax.all_gather(own, "shard", axis=at, tiled=True)]
            self.token = token

    def specs(self):
        return [whole(a) for a in self.arrays]

    def scratch(self):
        return pltpu.VMEM(self.shape, BF16)

    def hbm_first(self):
        return [in_hbm(self.arrays[0])] + self.arrays[1:]


def join(at, flag_ref, refs, full_ref):
    if len(refs) == 1:
        full_ref[...] = refs[0][...]
        return
    rows, cols = refs[0].shape[1:]
    half = rows // 2
    side, odd = flag_ref[0], flag_ref[1] & 1
    for where, first, ref in (
        (side, 0, refs[0]), (1 - side, odd * half, refs[1]), (1 - side, (1 - odd) * half, refs[2]),
    ):
        if at == 1:
            place = pl.ds(pl.multiple_of(where * rows + first, half), ref.shape[1])
            full_ref[:, place, :] = ref[...]
        else:
            place = pl.ds(pl.multiple_of(first, half), ref.shape[1])
            full_ref[:, place, pl.ds(pl.multiple_of(where * cols, cols), cols)] = ref[...]


def once(*joins):
    @pl.when(pl.program_id(0) == 0)
    def _():
        for args in joins:
            join(*args)


def axis_bits(axes):
    return [
        (axis, count, bit)
        for axis, count in axes
        for bit in reversed(range(count.bit_length() - 1))
    ]


def split_kernel(outer, terms, bit_ref, *refs):
    sources, (away_ref, keep_ref) = refs[:terms], refs[-2:]
    size = away_ref.shape[0] // outer
    for a in range(outer):
        for ref, half in ((away_ref, 1 - bit_ref[0]), (keep_ref, bit_ref[0])):
            rows = pl.ds(pl.multiple_of((2 * a + half) * size, size), size)
            total = sources[0][rows, :].astype(F32)
            for source in sources[1:]:
                total = total + source[rows, :].astype(F32)
            ref[a * size : (a + 1) * size, :] = total.astype(BF16)


def halve_rows(terms, bits, entry):
    rows, wide = terms[0].shape
    vmem = pl.BlockSpec(memory_space=pltpu.VMEM)
    half = jax.ShapeDtypeStruct((rows // 2, wide), BF16)
    axis, count, bit = entry
    away, keep = pl.pallas_call(
        functools.partial(split_kernel, 1 << bits.index(entry), len(terms)),
        in_specs=[pl.BlockSpec(memory_space=pltpu.SMEM)] + [vmem] * len(terms),
        out_specs=[vmem, vmem],
        out_shape=[half, half],
        compiler_params=params(10),
        cost_estimate=brief(),
        name="split",
    )(((lax.axis_index(axis) >> bit) & 1)[None], *terms)
    bits.remove(entry)
    return [keep, by_xor(axis, count, 1 << bit)(away)]


def quarters_kernel(flag_ref, keep_ref, came_ref, *refs):
    outs = refs[-4:]
    size = outs[0].shape[0]
    mine = flag_ref[0] * 2 + flag_ref[1] // 2
    for step, out in enumerate(outs):
        rows = pl.ds(pl.multiple_of((mine ^ step) * size, size), size)
        out[...] = (keep_ref[rows, :].astype(F32) + came_ref[rows, :].astype(F32)).astype(BF16)


def exchange_quarters(flags, terms, late):
    rows, wide = terms[0].shape
    outs = pl.pallas_call(
        quarters_kernel,
        grid=(1,),
        in_specs=[pl.BlockSpec(memory_space=pltpu.SMEM)] + [whole(term) for term in terms]
        + [pl.BlockSpec(memory_space=pl.ANY)] * len(late),
        out_specs=[fixed((rows // 4, wide))] * 4,
        out_shape=[jax.ShapeDtypeStruct((rows // 4, wide), BF16)] * 4,
        compiler_params=params(10),
        cost_estimate=brief(),
        name="quarters",
    )(flags, in_hbm(terms[0]), terms[1], *late)
    came = [outs[0]]
    for step in range(1, 4):
        perm = [(s * 4 + c, (s ^ (step >> 1)) * 4 + (c ^ ((step & 1) * 2))) for s in range(2) for c in range(4)]
        came.append(lax.ppermute(outs[step], ("shard", "ctx"), perm))
    return came, outs[0]


def group_kernel(count, small, late, flag_ref, *refs):
    ins, (away_ref, keep_ref) = refs[: len(refs) - 2 - late], refs[-2:]
    i = pl.program_id(0)

    def values():
        for k in range(count):
            left = jnp.concatenate([ins[3 * k][...], ins[3 * k + 1][...]], axis=1)
            yield dot(left, ins[3 * k + 2][...], 0, 0).astype(BF16)
        if small:
            parts = [
                jnp.concatenate([ref[...], jnp.zeros((120, 128), F32)], axis=0).T
                for ref in ins[3 * count :]
            ]
            yield jnp.concatenate(parts, axis=0).astype(BF16)

    first = 0
    for value in values():
        last = first + value.shape[1]

        @pl.when(i == 0)
        def _(value=value, first=first, last=last):
            away_ref[:, first:last] = value

        @pl.when(i > 0)
        def _(value=value, first=first, last=last):
            keep_ref[:, first:last] = value

        first = last


def owner_columns(rows, side):
    def block(i, j, flags):
        core = jnp.where(i == 0, 1 - (flags[1] & 1), flags[1] & 1)
        return (0, 4 * j + 2 * side + core)

    return pl.BlockSpec((rows, 128), block)


def group_grad(flags, pairs, small, axes, late):
    dim = pairs[0][0].shape[1]
    owners = 1
    for _, count in axes:
        owners *= count
    bits = axis_bits(axes)
    wide = sum(right.shape[1] for _, right in pairs) + (0 if small is None else 128)
    if dim // owners != 128:
        values = [dot(left, right, 0, 0).astype(BF16) for left, right in pairs]
        if small is not None:
            values.append(jnp.pad(small.T, ((0, 0), (0, 120))).astype(BF16))
        return halve_rows([jnp.concatenate(values, axis=1)], bits, bits[-1]), bits
    steps = dim // 512
    specs, flat = [], []
    for left, right in pairs:
        specs += [owner_columns(left.shape[0], side) for side in (0, 1)] + [whole(right)]
        flat += [in_hbm(left), in_hbm(left), right]
    if small is not None:
        specs += [owner_columns(small.shape[0], side) for side in (0, 1)]
        flat += [small, small]
    away, keep = pl.pallas_call(
        functools.partial(group_kernel, len(pairs), small is not None, len(late)),
        grid_spec=pltpu.PrefetchScalarGridSpec(
            num_scalar_prefetch=1,
            grid=(2, steps),
            in_specs=specs + [pl.BlockSpec(memory_space=pl.ANY)] * len(late),
            out_specs=[
                pl.BlockSpec((256, wide), lambda i, j, flags: (jnp.where(i == 0, j, steps - 1), 0)),
                pl.BlockSpec((256, wide), lambda i, j, flags: (jnp.where(i == 0, 0, j), 0)),
            ],
        ),
        out_shape=[
            pltpu.HBM((dim // 2, wide), BF16), pltpu.HBM((dim // 2, wide), BF16),
        ],
        compiler_params=params(16),
        cost_estimate=brief(),
        name="group_grad",
    )(flags, *flat, *late)
    return [keep, by_xor("ctx", dict(axes)["ctx"], 1)(away)], bits[:-1]


def scatter_group(flags, terms, bits, late):
    if len(bits) == 2:
        return exchange_quarters(flags, terms, late)
    bits = list(bits)
    while bits:
        terms = halve_rows(terms, bits, bits[-1])
    return terms, terms[0]


def total_kernel(terms, layouts, *refs):
    outs = refs[len(refs) - len(layouts) :]
    first = 0
    for out, (kind, wide) in zip(outs, layouts):
        cols = slice(first, first + wide)
        total = refs[0][:, cols].astype(F32)
        for ref in refs[1:terms]:
            total = total + ref[:, cols].astype(F32)
        if kind == "flip":
            out[...] = total.T
        elif kind == "small":
            out[...] = total.T[:8, :]
        elif kind == "three":
            for part in range(3):
                out[part] = total[:, part * wide // 3 : (part + 1) * wide // 3]
        else:
            out[...] = total
        first += wide


def group_total(terms, layouts, late, weight):
    rows = terms[0].shape[0]
    shapes = {
        "flip": lambda w: (w, rows), "small": lambda w: (8, rows),
        "three": lambda w: (3, rows, w // 3), "keep": lambda w: (rows, w),
    }
    vmem = pl.BlockSpec(memory_space=pltpu.VMEM)
    return pl.pallas_call(
        functools.partial(total_kernel, len(terms), layouts),
        in_specs=[vmem] * len(terms) + [pl.BlockSpec(memory_space=pl.ANY)] * len(late),
        out_specs=[vmem] * len(layouts),
        out_shape=[pltpu.HBM(shapes[kind](w), F32) for kind, w in layouts],
        compiler_params=params(10),
        cost_estimate=brief(weight),
        name="group_total",
    )(*terms, *late)


def body(
    sizes, hidden_in, w_qkv, bias_qkv, w_dense, w_up, bias_up, w_down, vectors, block_deal,
    segments, cotangent,
):
    shards, ranks, tps = sizes
    rank = lax.axis_index("ctx")
    dim = hidden_in.shape[1]
    own_rows = hidden_in.shape[0]

    x_all = lax.all_gather(hidden_in, "tp", axis=0, tiled=True)
    heads = bias_qkv.shape[1]
    width = heads * HEAD
    half = vectors.shape[1]
    small = jnp.concatenate(
        [vectors.reshape(-1), bias_qkv.astype(F32).reshape(-1), bias_up.astype(F32).reshape(-1)]
    )
    pad = -small.shape[0] % 1024
    small = jnp.pad(small, (0, pad)).reshape(1, -1, 128)
    token = first_token(segments)
    if shards == 2:
        other = by_xor("shard", 2, 1)(small)
        first = lax.axis_index("shard") == 0
        small = jnp.concatenate([jnp.where(first, small, other), jnp.where(first, other, small)])
    else:
        small = lax.all_gather(small, "shard", axis=0, tiled=True)
    small = small.reshape(shards, -1)
    cut = 6 * half
    vec = small[:, :cut].reshape(shards, 6, half).transpose(1, 0, 2).reshape(6, dim)
    vec = jnp.pad(vec, ((0, 2), (0, 0)))
    share = bias_qkv.size
    qkv_bias = small[:, cut : cut + share].reshape((shards,) + bias_qkv.shape)
    qkv_bias = qkv_bias.transpose(1, 2, 0, 3).reshape(3, width)
    up_bias = small[:, cut + share : cut + share + bias_up.size].reshape((shards,) + bias_up.shape)
    up_bias = up_bias.transpose(1, 0, 2).reshape(1, -1)
    flags = jnp.stack([lax.axis_index("shard"), rank])
    weight_qkv = Weight(w_qkv, 1, token, shards, ranks)
    weight_up = Weight(w_up[None], 1, token, shards, ranks)
    weight_down = Weight(w_down[None], 2, token, shards, ranks)
    weight_dense = Weight(w_dense[None], 2, token, shards, ranks)

    deal = block_deal[0]
    seg_row = segments[0]
    group = seg_row.shape[0]
    block = group // deal.shape[0]
    quarters = deal.shape[0] // ranks
    rank_rows = quarters * block
    split = ranks // quarters
    pieces = width // split // GROUP
    length = group // quarters
    at = jnp.arange(group, dtype=jnp.int32)
    previous = jnp.concatenate([seg_row[:1] - 1, seg_row[:-1]])
    begins = lax.cummax(jnp.where(seg_row != previous, at, 0), axis=0)
    places = (at - begins).reshape(deal.shape[0], block)
    deal_by_rank = deal.reshape(ranks, quarters)
    my_deal = lax.dynamic_index_in_dim(deal_by_rank, rank, 0, keepdims=False)
    picked = my_deal[:, None] == jnp.arange(deal.shape[0], dtype=jnp.int32)[None, :]
    rank_place = jnp.sum(jnp.where(picked[:, :, None], places[None], 0), axis=1).reshape(-1)
    quarter = rank // split
    partners = rank ^ jnp.arange(ranks, dtype=jnp.int32)
    in_quarter = jnp.take(lax.dynamic_index_in_dim(deal_by_rank, quarter, 1, keepdims=False), partners)
    pos = in_quarter - quarter * ranks
    my_begins = lax.dynamic_slice_in_dim(begins, quarter * length, length) - quarter * length
    quarter_place = jnp.arange(length, dtype=jnp.int32) - my_begins
    start_col = my_begins[:, None]
    lane = jnp.arange(128, dtype=jnp.int32) % HEAD
    frequency = ROPE_BASE ** (-2.0 * (lane % (ROT // 2)).astype(F32) / ROT)
    frequency = jnp.where(lane < ROT, frequency, 0.0)
    sign = jnp.where(lane < ROT // 2, -1.0, 1.0)
    all_places = jnp.concatenate([rank_place, quarter_place]).astype(F32)
    angles = all_places[:, None] * frequency[None, :]
    cosine, sine = jnp.cos(angles), jnp.sin(angles) * sign[None, :]
    target_row, target_col = partners // split, partners % split

    cot_rows = cotangent.astype(F32)
    cot_sum = jnp.sum(cot_rows, axis=0, keepdims=True)
    ready = after(cotangent, cot_sum, vec, qkv_bias, up_bias, cosine, sine, start_col, pos)
    cot_all = lax.all_gather(ready, "tp", axis=0, tiled=True)

    full_one, sent = project(
        flags, split, ranks, x_all, vec, weight_qkv, qkv_bias, cosine[:rank_rows],
        sine[:rank_rows], block, weight_up.arrays + weight_down.arrays + weight_dense.arrays,
    )

    def swap(sent):
        return [by_xor("ctx", ranks, s)(piece) if s else piece for s, piece in enumerate(sent)]

    arrived = exchange(sent, pieces, ranks, 2)
    full_two, activated, slope = mlp(
        flags, x_all, vec, weight_up, up_bias, block, sent[0]
    )
    outs, kept, late = [], [], in_hbm(slope)
    for p in range(pieces):
        out, keep = attend(pos, start_col, arrived[p], late, outs[0][1:] if p else [])
        outs.append(out)
        kept.append(keep)
        late = out[0]
    out_pieces = [out[0] for out in outs] + swap(outs[-1])[1:]

    axes = (("shard", shards), ("ctx", ranks))
    tables = (cosine[rank_rows:], sine[rank_rows:])
    part = mlp_down(flags, activated, weight_down, block, late)
    attended, partial = out_partial(
        flags, target_row, target_col, out_pieces, part, weight_dense, block
    )
    summed = lax.psum_scatter(partial, "tp", scatter_dimension=0, tiled=True)
    sent = attn_grad(flags, split, ranks, cot_all, weight_dense, block, [in_hbm(partial)])
    arrived = exchange(sent, pieces, ranks, ranks)
    first, bits = group_grad(flags, [(cot_all, activated)], None, axes, (sent[0],))
    grad_pieces, late = [], in_hbm(first[0])
    for p in range(pieces):
        grads = attend_back(pos, start_col, kept[p], *tables, arrived[p], late, 0 if p else 6)
        grad_pieces += swap(grads)
        late = grads[0]
    grad_pre, two_part, two_sums, grad_ubias = mlp_back(
        flags, x_all, cot_all, slope, weight_down, weight_up, vec, block,
        grad_pieces[: ranks * (pieces - 1)] + [late],
    )
    dlin, row_sum, one_sums, grad_qbias = input_grad(
        flags, target_row, target_col, x_all, grad_pieces, weight_qkv, two_part, vec, block,
        first[-1],
    )
    first, late = scatter_group(flags, first, bits, (dlin,))
    own_sum = lax.psum_scatter(after(row_sum, summed), "tp", scatter_dimension=0, tiled=True)

    owners = shards * ranks
    each, share = HEAD // owners, dim // owners

    def by_owner(row, lines):
        row = row.reshape(lines, owners, each).transpose(1, 0, 2).reshape(owners, -1)
        return jnp.pad(row, ((0, 0), (0, share - lines * each))).reshape(1, dim)

    small_rows = jnp.concatenate(
        [
            one_sums[:2], two_sums[:2], cot_sum, cot_sum,
            by_owner(grad_qbias[0], 3 * heads), by_owner(grad_ubias[0], bias_up.shape[0]),
        ],
        axis=0,
    )
    hidden, wide = weight_up.shape[2], 3 * width
    third, _ = group_grad(
        flags, [(full_one, dlin), (cot_all, attended)], small_rows, axes, (late,)
    )
    (grad_down,) = group_total(first, (("flip", hidden),), (in_hbm(third[0]),), 10)
    third, late = scatter_group(flags, third, bits, (in_hbm(grad_down),))
    second, _ = group_grad(flags, [(full_two, grad_pre)], None, axes, (late,))
    grad_qkv, grad_dense, small_rows = group_total(
        third, (("three", wide), ("flip", width), ("small", 128)), (in_hbm(second[0]),), 8
    )
    second, late = scatter_group(flags, second, bits, (in_hbm(grad_dense),))
    rows_in = hidden_in.astype(F32)
    output = (rows_in + summed.astype(F32) + vec[4:5] + vec[5:6]).astype(BF16)
    own_sum = after(own_sum, in_hbm(grad_dense)).astype(F32)
    hat, inverse = norm_rows(rows_in)
    centered = own_sum - jnp.mean(own_sum, axis=-1, keepdims=True)
    along = jnp.mean(own_sum * hat, axis=-1, keepdims=True)
    grad_in = (cot_rows + inverse * (centered - hat * along)).astype(BF16)
    grad_vec = small_rows[:6].reshape((6,) + (2,) * (tps.bit_length() - 1) + (-1,))
    for bit in reversed(range(tps.bit_length() - 1)):
        mine = (lax.axis_index("tp") >> bit) & 1
        keep = lax.dynamic_index_in_dim(grad_vec, mine, 1, keepdims=False)
        away = lax.dynamic_index_in_dim(grad_vec, 1 - mine, 1, keepdims=False)
        away = after(away, in_hbm(grad_in)) if bit == 0 else after(away, late)
        grad_vec = keep + by_xor("tp", tps, 1 << bit)(away)
    grad_qbias = small_rows[6, : 3 * heads * each].reshape(3, heads, each)
    grad_ubias = small_rows[7, : bias_up.shape[0] * each].reshape(bias_up.shape[0], each)

    (grad_up,) = group_total(second, (("keep", hidden),), (in_hbm(grad_in),), 0)
    return (
        output, grad_in, grad_qkv, grad_qbias, grad_dense, grad_up, grad_ubias, grad_down,
        grad_vec,
    )


def solution(mesh):
    sizes = tuple(mesh.shape[name] for name in ("shard", "ctx", "tp"))
    return jax.shard_map(
        functools.partial(body, sizes),
        mesh=mesh,
        in_specs=(
            P(("shard", "ctx", "tp"), None),
            P(None, "shard", "tp"),
            P(None, "tp", "shard"),
            P("tp", "shard"),
            P("shard", "tp"),
            P("tp", "shard"),
            P("tp", "shard"),
            P(None, "shard"),
            P("shard", None),
            P("shard", None),
            P(("shard", "ctx", "tp"), None),
        ),
        out_specs=(
            P(("shard", "ctx", "tp"), None),
            P(("shard", "ctx", "tp"), None),
            P(None, ("shard", "ctx"), "tp"),
            P(None, "tp", ("shard", "ctx")),
            P("tp", ("shard", "ctx")),
            P(("shard", "ctx"), "tp"),
            P("tp", ("shard", "ctx")),
            P("tp", ("shard", "ctx")),
            P(None, ("shard", "ctx", "tp")),
        ),
        check_vma=False,
    )
```

```python
import functools

import jax
import jax.numpy as jnp
from jax import lax
from jax.experimental import pallas as pl
from jax.experimental.pallas import tpu as pltpu
from jax.sharding import PartitionSpec as P

HEAD = 64
GROUP = 128
ROT = 16
NORM_EPS = 1e-05
SCORE_SCALE = 0.125
ROPE_BASE = 10000.0
MASK_FILL = 1e30
F32 = jnp.float32
BF16 = jnp.bfloat16


def dot(left, right, left_dim=1, right_dim=0):
    return lax.dot_general(
        left, right, (((left_dim,), (right_dim,)), ((), ())), preferred_element_type=F32
    )


def params(mib=20):
    return pltpu.CompilerParams(vmem_limit_bytes=mib * 1024 * 1024)


def brief(us=0):
    return pl.CostEstimate(flops=int(us * 1.1e9) + 1, bytes_accessed=1, transcendentals=0)


def swap_halves(values):
    width = values.shape[-1]
    lane = lax.broadcasted_iota(jnp.int32, (1, width), 1) % HEAD
    ahead = pltpu.roll(values, width - ROT // 2, 1)
    behind = pltpu.roll(values, ROT // 2, 1)
    return jnp.where(lane < ROT // 2, ahead, behind)


def widen(table, width):
    return jnp.concatenate([table] * (width // table.shape[-1]), axis=-1)


def norm_rows(rows):
    center = rows - jnp.mean(rows, axis=-1, keepdims=True)
    inverse = lax.rsqrt(jnp.mean(center * center, axis=-1, keepdims=True) + NORM_EPS)
    return center * inverse, inverse


def whole(array):
    return pl.BlockSpec(
        array.shape, lambda *ids: (0,) * array.ndim, pipeline_mode=pl.Buffered(buffer_count=1)
    )


def in_hbm(array):
    return pltpu.with_memory_space_constraint(array, pltpu.HBM)


def row_block(block, cols):
    return pl.BlockSpec((block, cols), lambda i, *ids: (i, 0))


def piece_shapes(pieces, ranks, merged, shape):
    shapes = []
    for step in range(ranks):
        if 0 < step < merged:
            shapes.append((pieces,) + shape)
        else:
            shapes += [(1,) + shape] * pieces
    return shapes


def by_step(flat, pieces, ranks, merged):
    steps, at = [], 0
    for step in range(ranks):
        count = 1 if 0 < step < merged else pieces
        steps.append(flat[at : at + count])
        at += count
    return steps


def send_pieces(i, split, merged, flag_ref, flat, groups_ref, ranks):
    pieces = groups_ref.shape[0] // split
    for step, refs in enumerate(by_step(flat, pieces, ranks, merged)):

        @pl.when(i == step // split)
        def _(step=step, refs=refs):
            for p in range(pieces):
                group = p
                if split > 1:
                    group = ((flag_ref[1] ^ step) % split) * pieces + p
                if len(refs) == 1:
                    refs[0][p] = groups_ref[group]
                else:
                    refs[p][0] = groups_ref[group]


def exchange(flat, pieces, ranks, merged):
    came = [[] for _ in range(pieces)]
    for step, arrays in enumerate(by_step(flat, pieces, ranks, merged)):
        if step:
            arrays = [by_xor("ctx", ranks, step)(array) for array in arrays]
        for p in range(pieces):
            came[p].append((arrays[0], p) if len(arrays) == 1 else (arrays[p], 0))
    return came


def quarter_block(block, cols, split):
    return pl.BlockSpec((block, cols), lambda i, flags: ((flags[1] // split) ^ i, 0))


def fixed(shape):
    return pl.BlockSpec(shape, lambda *ids: (0,) * len(shape))


def qkv_kernel(
    split, ranks, at, weights, late, flag_ref, x_ref, vec_ref, bias_ref, cos_ref, sin_ref, *refs
):
    refs = refs[:weights] + refs[weights + late :]
    one_ref, groups_ref, w_ref = refs[weights], refs[-2], refs[-1]
    once((at, flag_ref, refs[:weights], w_ref))
    i = pl.program_id(0)
    hat, _ = norm_rows(x_ref[...].astype(F32))
    one = (hat * vec_ref[0:1, :] + vec_ref[1:2, :]).astype(BF16)
    one_ref[...] = one
    width = w_ref.shape[2]
    cosine, sine = widen(cos_ref[...], width), widen(sin_ref[...], width)
    for part in range(3):
        lin = dot(one, w_ref[part]) + bias_ref[part : part + 1, :]
        if part < 2:
            lin = lin * cosine + swap_halves(lin) * sine
        if part == 0:
            lin = lin * SCORE_SCALE
        low = lin.astype(BF16)
        for g in range(width // GROUP):
            groups_ref[g, :, part * GROUP : (part + 1) * GROUP] = low[:, g * GROUP : (g + 1) * GROUP]
    send_pieces(i, split, 2, flag_ref, refs[weights + 1 : -2], groups_ref, ranks)


def project(flags, split, ranks, rows_all, vec, weight, bias, cosine, sine, block, late):
    rows, dim = rows_all.shape
    width = weight.shape[2]
    groups = width // GROUP
    piece = (block, 3 * GROUP)
    shapes = piece_shapes(groups // split, ranks, 2, piece)
    result = pl.pallas_call(
        functools.partial(
            qkv_kernel, split, ranks, weight.at, len(weight.arrays), len(late)
        ),
        grid_spec=pltpu.PrefetchScalarGridSpec(
            num_scalar_prefetch=1,
            grid=(rows // block,),
            in_specs=[
                quarter_block(block, dim, split), whole(vec), whole(bias),
                quarter_block(block, cosine.shape[1], split),
                quarter_block(block, sine.shape[1], split),
            ]
            + weight.specs()
            + [pl.BlockSpec(memory_space=pl.ANY)] * len(late),
            out_specs=[quarter_block(block, dim, split)] + [fixed(shape) for shape in shapes],
            scratch_shapes=[pltpu.VMEM((groups,) + piece, BF16), weight.scratch()],
        ),
        out_shape=[pltpu.HBM((rows, dim), BF16)]
        + [jax.ShapeDtypeStruct(shape, BF16) for shape in shapes],
        compiler_params=params(12),
        cost_estimate=brief(300),
        name="norm_qkv",
    )(
        flags, in_hbm(rows_all), vec, bias, in_hbm(cosine), in_hbm(sine), *weight.hbm_first(),
        *late,
    )
    return result[0], result[1:]


def attn_grad_kernel(split, ranks, at, weights, late, flag_ref, cot_ref, *refs):
    refs = refs[:weights] + refs[weights + late :]
    groups_ref, w_ref = refs[-2:]
    once((at, flag_ref, refs[:weights], w_ref))
    grad = dot(cot_ref[...], w_ref[0], 1, 1).astype(BF16)
    for g in range(groups_ref.shape[0]):
        groups_ref[g] = grad[:, g * GROUP : (g + 1) * GROUP]
    send_pieces(pl.program_id(0), split, ranks, flag_ref, refs[weights:-2], groups_ref, ranks)


def attn_grad(flags, split, ranks, cot_all, weight, block, late):
    rows, dim = cot_all.shape
    groups = weight.shape[1] // GROUP
    piece = (block, GROUP)
    shapes = piece_shapes(groups // split, ranks, ranks, piece)
    result = pl.pallas_call(
        functools.partial(
            attn_grad_kernel, split, ranks, weight.at, len(weight.arrays), len(late)
        ),
        grid_spec=pltpu.PrefetchScalarGridSpec(
            num_scalar_prefetch=1,
            grid=(rows // block,),
            in_specs=[quarter_block(block, dim, split)]
            + weight.specs()
            + [pl.BlockSpec(memory_space=pl.ANY)] * len(late),
            out_specs=[fixed(shape) for shape in shapes],
            scratch_shapes=[pltpu.VMEM((groups,) + piece, BF16), weight.scratch()],
        ),
        out_shape=[jax.ShapeDtypeStruct(shape, BF16) for shape in shapes],
        compiler_params=params(8),
        cost_estimate=brief(300),
        name="attn_grad",
    )(flags, in_hbm(cot_all), *weight.hbm_first(), *late)
    return result


def mlp_kernel(at, weights, flag_ref, x_ref, vec_ref, bias_ref, late_ref, *refs):
    two_ref, act_ref, slope_ref, up_ref = refs[-4:]
    once((at, flag_ref, refs[:weights], up_ref))
    hat, _ = norm_rows(x_ref[...].astype(F32))
    two = (hat * vec_ref[2:3, :] + vec_ref[3:4, :]).astype(BF16)
    two_ref[...] = two
    pre = dot(two, up_ref[0]) + bias_ref[...]
    phi = 0.5 * (1.0 + lax.erf(pre * 0.7071067811865476))
    act = (pre * phi).astype(BF16)
    act_ref[...] = act
    slope = phi + pre * (0.3989422804014327 * jnp.exp(-0.5 * pre * pre))
    slope_ref[...] = slope.astype(BF16)


def mlp(flags, rows_all, vec, up, bias, block, late):
    rows, dim = rows_all.shape
    hidden = up.shape[2]
    return pl.pallas_call(
        functools.partial(mlp_kernel, up.at, len(up.arrays)),
        grid=(rows // block,),
        in_specs=[
            pl.BlockSpec(memory_space=pltpu.SMEM), row_block(block, dim), whole(vec), whole(bias),
            pl.BlockSpec(memory_space=pl.ANY),
        ]
        + up.specs(),
        out_specs=[row_block(block, dim), row_block(block, hidden), row_block(block, hidden)],
        out_shape=[
            pltpu.HBM((rows, dim), BF16),
            pltpu.HBM((rows, hidden), BF16),
            pltpu.HBM((rows, hidden), BF16),
        ],
        scratch_shapes=[up.scratch()],
        compiler_params=params(18),
        cost_estimate=brief(),
        name="mlp",
    )(flags, in_hbm(rows_all), vec, bias, late, *up.hbm_first())


def gather_pieces(pieces, parts, row_ref, col_ref, size, out_ref):
    full = out_ref.shape[1] // parts
    ranks = row_ref.shape[0]
    count = len(pieces) // ranks
    for index, piece in enumerate(pieces):
        r, p = index % ranks, index // ranks
        rows = pl.ds(pl.multiple_of(row_ref[r] * size, size), size)
        for part in range(parts):
            values = piece[:, part * GROUP : (part + 1) * GROUP]
            if count * GROUP == full:
                out_ref[rows, part * full + p * GROUP : part * full + (p + 1) * GROUP] = values
            else:
                column = part * full + (col_ref[r] * count + p) * GROUP
                out_ref[rows, pl.ds(pl.multiple_of(column, GROUP), GROUP)] = values


def down_kernel(at, weights, flag_ref, act_ref, late_ref, *refs):
    out_ref, down_ref = refs[-2:]
    once((at, flag_ref, refs[:weights], down_ref))
    out_ref[...] = dot(act_ref[...], down_ref[0])


def mlp_down(flags, activated, down, block, late):
    rows, hidden = activated.shape
    dim = down.shape[2]
    return pl.pallas_call(
        functools.partial(down_kernel, down.at, len(down.arrays)),
        grid=(rows // block,),
        in_specs=[
            pl.BlockSpec(memory_space=pltpu.SMEM), row_block(block, hidden),
            pl.BlockSpec(memory_space=pl.ANY),
        ]
        + down.specs(),
        out_specs=row_block(block, dim),
        out_shape=jax.ShapeDtypeStruct((rows, dim), F32),
        scratch_shapes=[down.scratch()],
        compiler_params=params(14),
        cost_estimate=brief(),
        name="mlp_down",
    )(flags, in_hbm(activated), late, *down.hbm_first())


def out_kernel(at, weights, count, flag_ref, row_ref, col_ref, part_ref, *refs):
    pieces = refs[weights : weights + count]
    attended_ref, out_ref, w_ref = refs[-3:]
    once((at, flag_ref, refs[:weights], w_ref))
    i = pl.program_id(0)
    block = out_ref.shape[0]

    @pl.when(i == 0)
    def _():
        ranks = row_ref.shape[0]
        local = len(pieces) - ranks + 1
        flat = []
        for p in range(local):
            flat += [pieces[p]] + [ref.at[p] if local > 1 else ref for ref in pieces[local:]]
        gather_pieces(flat, 1, row_ref, col_ref, block, attended_ref)

    rows = pl.ds(pl.multiple_of(i * block, block), block)
    out_ref[...] = (part_ref[...] + dot(attended_ref[rows, :], w_ref[0])).astype(BF16)


def out_partial(flags, row_at, col_at, pieces, part, dense, block):
    rows = part.shape[0]
    width, dim = dense.shape[1:]
    return pl.pallas_call(
        functools.partial(out_kernel, dense.at, len(dense.arrays), len(pieces)),
        grid_spec=pltpu.PrefetchScalarGridSpec(
            num_scalar_prefetch=3,
            grid=(rows // block,),
            in_specs=[row_block(block, dim)] + dense.specs() + [whole(p) for p in pieces],
            out_specs=[fixed((rows, width)), row_block(block, dim)],
            scratch_shapes=[dense.scratch()],
        ),
        out_shape=[pltpu.HBM((rows, width), BF16), pltpu.HBM((rows, dim), BF16)],
        compiler_params=params(12),
        cost_estimate=brief(),
        name="out_partial",
    )(flags, row_at, col_at, part, *dense.hbm_first(), *pieces)


def pair_bias(start_ref, first, size, keys):
    query_at = lax.broadcasted_iota(jnp.int32, (size, keys), 0) + first
    key_at = lax.broadcasted_iota(jnp.int32, (size, keys), 1)
    allowed = (key_at <= query_at) & (key_at >= start_ref[first : first + size, :])
    return jnp.where(allowed, 0.0, -MASK_FILL)


def attn_fwd_kernel(at, before, pos_ref, start_ref, late_ref, *refs):
    count = len(at)
    blocks = [ref.at[p] for ref, p in zip(refs, at)]
    earlier, refs = refs[count : count + before], refs[count + before :]
    outs, refs = refs[:count], refs[count:]
    for source, target in zip(earlier, outs[1:]):
        target[0] = source[...]
    outs = [outs[0]] + [ref.at[1] if before else ref for ref in outs[1:]]
    q_ref, k_ref, v_ref, lse_ref, o_ref = refs
    size, width = outs[0].shape
    for r in range(count):
        rows = pl.ds(pl.multiple_of(pos_ref[r] * size, size), size)
        q_ref[rows, :] = blocks[r][:, :width]
        k_ref[rows, :] = blocks[r][:, width : 2 * width]
        v_ref[rows, :] = blocks[r][:, 2 * width :]
    group = lax.broadcasted_iota(jnp.int32, (1, width), 1) // HEAD
    lane = lax.broadcasted_iota(jnp.int32, (1, 128), 1)
    zero, unit = jnp.zeros((), BF16), jnp.ones((), BF16)
    for i in range(count):
        first, keys = i * size, (i + 1) * size
        bias = pair_bias(start_ref, first, size, keys)
        query = q_ref[first:keys, :]
        total = jnp.zeros((size, width), F32)
        tops = jnp.zeros((size, 128), F32)
        heads = range(width // HEAD)
        scores = [
            dot(jnp.where(group == head, query, zero), k_ref[:keys, :], 1, 1) + bias
            for head in heads
        ]
        highest = [jnp.max(score, axis=-1, keepdims=True) for score in scores]
        terms = [jnp.exp(score - top).astype(BF16) for score, top in zip(scores, highest)]
        for head in heads:
            mine = group == head
            other = HEAD if head == 0 else 0
            mixed = dot(terms[head], jnp.where(mine, v_ref[:keys, :], unit))
            row_sum = mixed[:, other : other + 1]
            total = jnp.where(mine, mixed * (1.0 / row_sum), total)
            tops = jnp.where(lane == head, highest[head] + jnp.log(row_sum), tops)
        o_ref[first:keys, :] = total
        lse_ref[first:keys, :] = tops
    for r in range(count):
        rows = pl.ds(pl.multiple_of(pos_ref[r] * size, size), size)
        outs[r][...] = o_ref[rows, :].astype(BF16)


def attend(pos, start_col, blocks, late, earlier):
    count = len(blocks)
    size, wide = blocks[0][0].shape[1:]
    width, length = wide // 3, size * count
    shapes = [(size, width)] + [((2,) if earlier else ()) + (size, width)] * (count - 1)
    result = pl.pallas_call(
        functools.partial(attn_fwd_kernel, tuple(p for _, p in blocks), len(earlier)),
        grid=(1,),
        in_specs=[
            pl.BlockSpec(memory_space=pltpu.SMEM), whole(start_col),
            pl.BlockSpec(memory_space=pl.ANY),
        ]
        + [whole(array) for array, _ in blocks]
        + [whole(array) for array in earlier],
        out_specs=[fixed(shape) for shape in shapes]
        + [fixed((length, width))] * 3
        + [fixed((length, 128))],
        out_shape=[jax.ShapeDtypeStruct(shape, BF16) for shape in shapes]
        + [pltpu.HBM((length, width), BF16)] * 3
        + [pltpu.HBM((length, 128), F32)],
        scratch_shapes=[pltpu.VMEM((length, width), F32)],
        compiler_params=params(3 * count),
        cost_estimate=brief(),
        name="attend",
    )(pos, start_col, late, *(array for array, _ in blocks), *earlier)
    return list(result[:count]), result[count:]


def attn_bwd_kernel(at, pos_ref, start_ref, late_ref, q_ref, k_ref, v_ref, lse_ref, cos_ref, sin_ref, *refs):
    count = len(at)
    blocks, outs = [ref.at[p] for ref, p in zip(refs, at)], refs[count : 2 * count]
    do_ref, dq_ref, dk_ref, dv_ref = refs[2 * count :]
    size, width = blocks[0].shape
    for r in range(count):
        rows = pl.ds(pl.multiple_of(pos_ref[r] * size, size), size)
        do_ref[rows, :] = blocks[r][...]
    group = lax.broadcasted_iota(jnp.int32, (1, width), 1) // HEAD
    zero = jnp.zeros((), BF16)
    def add(ref, rows, keys, value):
        if keys == ref.shape[1]:
            ref[rows, :keys] = value
        else:
            ref[rows, :keys] += value

    for i in reversed(range(count)):
        first, keys = i * size, (i + 1) * size
        bias = pair_bias(start_ref, first, size, keys)
        query, grad_out = q_ref[first:keys, :], do_ref[first:keys, :]
        query_t, grad_out_t = query.T, grad_out.T
        total = jnp.zeros((size, width), F32)
        heads = range(width // HEAD)
        scores = [
            dot(jnp.where(group == head, query, zero), k_ref[:keys, :], 1, 1) + bias
            for head in heads
        ]
        grad_probs = [
            dot(jnp.where(group == head, grad_out, zero), v_ref[:keys, :], 1, 1) for head in heads
        ]
        probs = [
            jnp.exp(scores[head] - lse_ref[first:keys, head : head + 1]) for head in heads
        ]
        for head in heads:
            rows = slice(head * HEAD, (head + 1) * HEAD)
            add(dv_ref, rows, keys, dot(grad_out_t[rows, :], probs[head].astype(BF16)))
        for head in heads:
            rows = slice(head * HEAD, (head + 1) * HEAD)
            weighted = probs[head] * grad_probs[head]
            delta = jnp.sum(weighted, axis=-1, keepdims=True)
            grad_score = (probs[head] * (grad_probs[head] - delta)).astype(BF16)
            total = total + dot(grad_score, jnp.where(group == head, k_ref[:keys, :], zero))
            add(dk_ref, rows, keys, dot(query_t[rows, :], grad_score))
        dq_ref[first:keys, :] = total * SCORE_SCALE
    dk = dk_ref[...].T
    dv = dv_ref[...].T
    cosine, sine = cos_ref[...], sin_ref[...]
    key_grad = dk * cosine - swap_halves(dk) * sine
    grad = dq_ref[...]
    dq_ref[...] = grad * cosine - swap_halves(grad) * sine
    do_ref[...] = dv.astype(BF16)
    for r in range(count):
        rows = pl.ds(pl.multiple_of(pos_ref[r] * size, size), size)
        outs[r][:, :width] = dq_ref[rows, :].astype(BF16)
        outs[r][:, 2 * width :] = do_ref[rows, :]
    dq_ref[...] = key_grad
    for r in range(count):
        rows = pl.ds(pl.multiple_of(pos_ref[r] * size, size), size)
        outs[r][:, width : 2 * width] = dq_ref[rows, :].astype(BF16)


def attend_back(pos, start_col, kept, cosine, sine, blocks, late, weight):
    count = len(blocks)
    size, width = blocks[0][0].shape[1:]
    length = size * count
    return pl.pallas_call(
        functools.partial(attn_bwd_kernel, tuple(p for _, p in blocks)),
        grid=(1,),
        in_specs=[
            pl.BlockSpec(memory_space=pltpu.SMEM), whole(start_col),
            pl.BlockSpec(memory_space=pl.ANY),
        ]
        + [whole(array) for array in (*kept, cosine, sine)]
        + [whole(array) for array, _ in blocks],
        out_specs=[fixed((size, 3 * width))] * count,
        out_shape=[jax.ShapeDtypeStruct((size, 3 * width), BF16)] * count,
        scratch_shapes=[pltpu.VMEM((length, width), BF16), pltpu.VMEM((length, width), F32)]
        + [pltpu.VMEM((width, length), F32)] * 2,
        compiler_params=params(4 * count),
        cost_estimate=brief(weight),
        name="attend_back",
    )(
        pos, start_col, late, *[in_hbm(a) for a in (*kept, cosine, sine)],
        *(array for array, _ in blocks),
    )


def add_sums(i, ref, values):
    sums = [jnp.sum(value, axis=0, keepdims=True) for value in values]
    sums += [jnp.zeros_like(sums[0])] * (8 - len(sums))
    share = jnp.concatenate(sums, axis=0)

    @pl.when(i == 0)
    def _():
        ref[...] = share

    @pl.when(i > 0)
    def _():
        ref[...] += share


def mlp_back_kernel(ats, weights, flag_ref, x_ref, cot_ref, slope_ref, vec_ref, *refs):
    pre_ref, two_ref, grads_ref, bias_ref, down_ref, up_ref = refs[-6:]
    once(
        (ats[0], flag_ref, refs[:weights], down_ref),
        (ats[1], flag_ref, refs[weights : 2 * weights], up_ref),
    )
    i = pl.program_id(0)
    grad_act = dot(cot_ref[...], down_ref[0], 1, 1)
    grad_pre = (grad_act * slope_ref[...].astype(F32)).astype(BF16)
    pre_ref[...] = grad_pre
    two = dot(grad_pre, up_ref[0], 1, 1)
    hat, _ = norm_rows(x_ref[...].astype(F32))
    two_ref[...] = two * vec_ref[2:3, :]
    add_sums(i, grads_ref, (two * hat, two))
    add_sums(i, bias_ref, (grad_pre.astype(F32),))


def mlp_back(flags, rows_all, cot_all, slope, down, up, vec, block, late):
    rows, dim = rows_all.shape
    hidden = slope.shape[1]
    return pl.pallas_call(
        functools.partial(mlp_back_kernel, (down.at, up.at), len(up.arrays)),
        grid=(rows // block,),
        in_specs=[
            pl.BlockSpec(memory_space=pltpu.SMEM), row_block(block, dim), row_block(block, dim),
            row_block(block, hidden), whole(vec),
        ]
        + down.specs()
        + up.specs()
        + [pl.BlockSpec(memory_space=pl.ANY)] * len(late),
        out_specs=[
            row_block(block, hidden), row_block(block, dim), fixed((8, dim)), fixed((8, hidden)),
        ],
        out_shape=[
            pltpu.HBM((rows, hidden), BF16),
            jax.ShapeDtypeStruct((rows, dim), F32),
            jax.ShapeDtypeStruct((8, dim), F32),
            jax.ShapeDtypeStruct((8, hidden), F32),
        ],
        scratch_shapes=[down.scratch(), up.scratch()],
        compiler_params=params(18),
        cost_estimate=brief(8),
        name="mlp_back",
    )(
        flags, in_hbm(rows_all), in_hbm(cot_all), in_hbm(slope), vec, *down.hbm_first(),
        *up.hbm_first(), *late,
    )


def input_grad_kernel(
    at, weights, count, flag_ref, row_ref, col_ref, x_ref, two_ref, vec_ref, late_ref, *refs
):
    pieces = refs[weights : weights + count]
    dlin_ref, sum_ref, grads_ref, bias_ref, w_ref = refs[-5:]
    once((at, flag_ref, refs[:weights], w_ref))
    width = w_ref.shape[2]
    block = x_ref.shape[0]
    i = pl.program_id(0)

    @pl.when(i == 0)
    def _():
        gather_pieces(pieces, 3, row_ref, col_ref, block, dlin_ref)

    rows = pl.ds(pl.multiple_of(i * block, block), block)
    hat, _ = norm_rows(x_ref[...].astype(F32))
    dlin = dlin_ref[rows, :]
    one = dot(dlin[:, :width], w_ref[0], 1, 1)
    for part in (1, 2):
        one = one + dot(dlin[:, part * width : (part + 1) * width], w_ref[part], 1, 1)
    sum_ref[...] = (one * vec_ref[0:1, :] + two_ref[...]).astype(BF16)
    add_sums(i, grads_ref, (one * hat, one))
    add_sums(i, bias_ref, (dlin.astype(F32),))


def input_grad(flags, row_at, col_at, rows_all, pieces, weight, two_part, vec, block, late):
    rows, dim = rows_all.shape
    wide = 3 * weight.shape[2]
    return pl.pallas_call(
        functools.partial(input_grad_kernel, weight.at, len(weight.arrays), len(pieces)),
        grid_spec=pltpu.PrefetchScalarGridSpec(
            num_scalar_prefetch=3,
            grid=(rows // block,),
            in_specs=[
                row_block(block, dim), row_block(block, dim), whole(vec),
                pl.BlockSpec(memory_space=pl.ANY),
            ]
            + weight.specs()
            + [whole(p) for p in pieces],
            out_specs=[
                fixed((rows, wide)), row_block(block, dim), fixed((8, dim)), fixed((8, wide)),
            ],
            scratch_shapes=[weight.scratch()],
        ),
        out_shape=[
            jax.ShapeDtypeStruct((rows, wide), BF16),
            pltpu.HBM((rows, dim), BF16),
            jax.ShapeDtypeStruct((8, dim), F32),
            jax.ShapeDtypeStruct((8, wide), F32),
        ],
        compiler_params=params(12),
        cost_estimate=brief(),
        name="input_grad",
    )(flags, row_at, col_at, in_hbm(rows_all), two_part, vec, late, *weight.hbm_first(), *pieces)


def by_xor(axis, count, step):
    return functools.partial(
        lax.ppermute, axis_name=axis, perm=[(i, i ^ step) for i in range(count)]
    )


def nothing(*refs):
    del refs


def after(values, *others):
    anywhere = pl.BlockSpec(memory_space=pl.ANY)
    return pl.pallas_call(
        nothing,
        in_specs=[anywhere] * (1 + len(others)),
        out_specs=anywhere,
        out_shape=jax.ShapeDtypeStruct(values.shape, values.dtype),
        input_output_aliases={0: 0},
        name="after",
    )(values, *others)


def first_token(values):
    def copy(source, target):
        target[...] = source[...]

    return pl.pallas_call(
        copy, out_shape=jax.ShapeDtypeStruct(values.shape, values.dtype), name="first"
    )(values)


class Weight:
    def __init__(self, own, at, token, shards, ranks):
        self.at, shape = at, list(own.shape)
        shape[at] *= shards
        self.shape = tuple(shape)
        if shards == 2 and ranks > 1:
            half = own.shape[1] // 2
            odd = lax.axis_index("ctx") & 1
            mine = lax.dynamic_slice_in_dim(own, odd * half, half, 1)
            mine = by_xor("shard", 2, 1)(after(mine, token))
            self.arrays = [own, mine, by_xor("ctx", ranks, 1)(mine)]
            self.token = mine
        else:
            self.arrays = [lax.all_gather(own, "shard", axis=at, tiled=True)]
            self.token = token

    def specs(self):
        return [whole(a) for a in self.arrays]

    def scratch(self):
        return pltpu.VMEM(self.shape, BF16)

    def hbm_first(self):
        return [in_hbm(self.arrays[0])] + self.arrays[1:]


def join(at, flag_ref, refs, full_ref):
    if len(refs) == 1:
        full_ref[...] = refs[0][...]
        return
    rows, cols = refs[0].shape[1:]
    half = rows // 2
    side, odd = flag_ref[0], flag_ref[1] & 1
    for where, first, ref in (
        (side, 0, refs[0]), (1 - side, odd * half, refs[1]), (1 - side, (1 - odd) * half, refs[2]),
    ):
        if at == 1:
            place = pl.ds(pl.multiple_of(where * rows + first, half), ref.shape[1])
            full_ref[:, place, :] = ref[...]
        else:
            place = pl.ds(pl.multiple_of(first, half), ref.shape[1])
            full_ref[:, place, pl.ds(pl.multiple_of(where * cols, cols), cols)] = ref[...]


def once(*joins):
    @pl.when(pl.program_id(0) == 0)
    def _():
        for args in joins:
            join(*args)


def axis_bits(axes):
    return [
        (axis, count, bit)
        for axis, count in axes
        for bit in reversed(range(count.bit_length() - 1))
    ]


def split_kernel(outer, terms, bit_ref, *refs):
    sources, (away_ref, keep_ref) = refs[:terms], refs[-2:]
    size = away_ref.shape[0] // outer
    for a in range(outer):
        for ref, half in ((away_ref, 1 - bit_ref[0]), (keep_ref, bit_ref[0])):
            rows = pl.ds(pl.multiple_of((2 * a + half) * size, size), size)
            total = sources[0][rows, :].astype(F32)
            for source in sources[1:]:
                total = total + source[rows, :].astype(F32)
            ref[a * size : (a + 1) * size, :] = total.astype(BF16)


def halve_rows(terms, bits, entry):
    rows, wide = terms[0].shape
    vmem = pl.BlockSpec(memory_space=pltpu.VMEM)
    half = jax.ShapeDtypeStruct((rows // 2, wide), BF16)
    axis, count, bit = entry
    away, keep = pl.pallas_call(
        functools.partial(split_kernel, 1 << bits.index(entry), len(terms)),
        in_specs=[pl.BlockSpec(memory_space=pltpu.SMEM)] + [vmem] * len(terms),
        out_specs=[vmem, vmem],
        out_shape=[half, half],
        compiler_params=params(10),
        cost_estimate=brief(),
        name="split",
    )(((lax.axis_index(axis) >> bit) & 1)[None], *terms)
    bits.remove(entry)
    return [keep, by_xor(axis, count, 1 << bit)(away)]


def quarters_kernel(flag_ref, keep_ref, came_ref, *refs):
    outs = refs[-4:]
    size = outs[0].shape[0]
    mine = flag_ref[0] * 2 + flag_ref[1] // 2
    for step, out in enumerate(outs):
        rows = pl.ds(pl.multiple_of((mine ^ step) * size, size), size)
        out[...] = (keep_ref[rows, :].astype(F32) + came_ref[rows, :].astype(F32)).astype(BF16)


def exchange_quarters(flags, terms, late):
    rows, wide = terms[0].shape
    outs = pl.pallas_call(
        quarters_kernel,
        grid=(1,),
        in_specs=[pl.BlockSpec(memory_space=pltpu.SMEM)] + [whole(term) for term in terms]
        + [pl.BlockSpec(memory_space=pl.ANY)] * len(late),
        out_specs=[fixed((rows // 4, wide))] * 4,
        out_shape=[jax.ShapeDtypeStruct((rows // 4, wide), BF16)] * 4,
        compiler_params=params(10),
        cost_estimate=brief(),
        name="quarters",
    )(flags, in_hbm(terms[0]), terms[1], *late)
    came = [outs[0]]
    for step in range(1, 4):
        perm = [(s * 4 + c, (s ^ (step >> 1)) * 4 + (c ^ ((step & 1) * 2))) for s in range(2) for c in range(4)]
        came.append(lax.ppermute(outs[step], ("shard", "ctx"), perm))
    return came, outs[0]


def group_kernel(count, small, late, flag_ref, *refs):
    ins, (away_ref, keep_ref) = refs[: len(refs) - 2 - late], refs[-2:]
    i = pl.program_id(0)

    def values():
        for k in range(count):
            left = jnp.concatenate([ins[3 * k][...], ins[3 * k + 1][...]], axis=1)
            yield dot(left, ins[3 * k + 2][...], 0, 0).astype(BF16)
        if small:
            parts = [
                jnp.concatenate([ref[...], jnp.zeros((120, 128), F32)], axis=0).T
                for ref in ins[3 * count :]
            ]
            yield jnp.concatenate(parts, axis=0).astype(BF16)

    first = 0
    for value in values():
        last = first + value.shape[1]

        @pl.when(i == 0)
        def _(value=value, first=first, last=last):
            away_ref[:, first:last] = value

        @pl.when(i > 0)
        def _(value=value, first=first, last=last):
            keep_ref[:, first:last] = value

        first = last


def owner_columns(rows, side):
    def block(i, j, flags):
        core = jnp.where(i == 0, 1 - (flags[1] & 1), flags[1] & 1)
        return (0, 4 * j + 2 * side + core)

    return pl.BlockSpec((rows, 128), block)


def group_grad(flags, pairs, small, axes, late):
    dim = pairs[0][0].shape[1]
    owners = 1
    for _, count in axes:
        owners *= count
    bits = axis_bits(axes)
    wide = sum(right.shape[1] for _, right in pairs) + (0 if small is None else 128)
    if dim // owners != 128:
        values = [dot(left, right, 0, 0).astype(BF16) for left, right in pairs]
        if small is not None:
            values.append(jnp.pad(small.T, ((0, 0), (0, 120))).astype(BF16))
        return halve_rows([jnp.concatenate(values, axis=1)], bits, bits[-1]), bits
    steps = dim // 512
    specs, flat = [], []
    for left, right in pairs:
        specs += [owner_columns(left.shape[0], side) for side in (0, 1)] + [whole(right)]
        flat += [in_hbm(left), in_hbm(left), right]
    if small is not None:
        specs += [owner_columns(small.shape[0], side) for side in (0, 1)]
        flat += [small, small]
    away, keep = pl.pallas_call(
        functools.partial(group_kernel, len(pairs), small is not None, len(late)),
        grid_spec=pltpu.PrefetchScalarGridSpec(
            num_scalar_prefetch=1,
            grid=(2, steps),
            in_specs=specs + [pl.BlockSpec(memory_space=pl.ANY)] * len(late),
            out_specs=[
                pl.BlockSpec((256, wide), lambda i, j, flags: (jnp.where(i == 0, j, steps - 1), 0)),
                pl.BlockSpec((256, wide), lambda i, j, flags: (jnp.where(i == 0, 0, j), 0)),
            ],
        ),
        out_shape=[
            pltpu.HBM((dim // 2, wide), BF16), pltpu.HBM((dim // 2, wide), BF16),
        ],
        compiler_params=params(16),
        cost_estimate=brief(),
        name="group_grad",
    )(flags, *flat, *late)
    return [keep, by_xor("ctx", dict(axes)["ctx"], 1)(away)], bits[:-1]


def scatter_group(flags, terms, bits, late):
    if len(bits) == 2:
        return exchange_quarters(flags, terms, late)
    bits = list(bits)
    while bits:
        terms = halve_rows(terms, bits, bits[-1])
    return terms, terms[0]


def total_kernel(terms, layouts, *refs):
    outs = refs[len(refs) - len(layouts) :]
    first = 0
    for out, (kind, wide) in zip(outs, layouts):
        cols = slice(first, first + wide)
        total = refs[0][:, cols].astype(F32)
        for ref in refs[1:terms]:
            total = total + ref[:, cols].astype(F32)
        if kind == "flip":
            out[...] = total.T
        elif kind == "small":
            out[...] = total.T[:8, :]
        elif kind == "three":
            for part in range(3):
                out[part] = total[:, part * wide // 3 : (part + 1) * wide // 3]
        else:
            out[...] = total
        first += wide


def group_total(terms, layouts, late, weight):
    rows = terms[0].shape[0]
    shapes = {
        "flip": lambda w: (w, rows), "small": lambda w: (8, rows),
        "three": lambda w: (3, rows, w // 3), "keep": lambda w: (rows, w),
    }
    vmem = pl.BlockSpec(memory_space=pltpu.VMEM)
    return pl.pallas_call(
        functools.partial(total_kernel, len(terms), layouts),
        in_specs=[vmem] * len(terms) + [pl.BlockSpec(memory_space=pl.ANY)] * len(late),
        out_specs=[vmem] * len(layouts),
        out_shape=[pltpu.HBM(shapes[kind](w), F32) for kind, w in layouts],
        compiler_params=params(10),
        cost_estimate=brief(weight),
        name="group_total",
    )(*terms, *late)


def body(
    sizes, hidden_in, w_qkv, bias_qkv, w_dense, w_up, bias_up, w_down, vectors, block_deal,
    segments, cotangent,
):
    shards, ranks, tps = sizes
    rank = lax.axis_index("ctx")
    dim = hidden_in.shape[1]
    own_rows = hidden_in.shape[0]

    x_all = lax.all_gather(hidden_in, "tp", axis=0, tiled=True)
    heads = bias_qkv.shape[1]
    width = heads * HEAD
    half = vectors.shape[1]
    small = jnp.concatenate(
        [vectors.reshape(-1), bias_qkv.astype(F32).reshape(-1), bias_up.astype(F32).reshape(-1)]
    )
    pad = -small.shape[0] % 1024
    small = jnp.pad(small, (0, pad)).reshape(1, -1, 128)
    token = first_token(segments)
    if shards == 2:
        other = by_xor("shard", 2, 1)(small)
        first = lax.axis_index("shard") == 0
        small = jnp.concatenate([jnp.where(first, small, other), jnp.where(first, other, small)])
    else:
        small = lax.all_gather(small, "shard", axis=0, tiled=True)
    small = small.reshape(shards, -1)
    cut = 6 * half
    vec = small[:, :cut].reshape(shards, 6, half).transpose(1, 0, 2).reshape(6, dim)
    vec = jnp.pad(vec, ((0, 2), (0, 0)))
    share = bias_qkv.size
    qkv_bias = small[:, cut : cut + share].reshape((shards,) + bias_qkv.shape)
    qkv_bias = qkv_bias.transpose(1, 2, 0, 3).reshape(3, width)
    up_bias = small[:, cut + share : cut + share + bias_up.size].reshape((shards,) + bias_up.shape)
    up_bias = up_bias.transpose(1, 0, 2).reshape(1, -1)
    flags = jnp.stack([lax.axis_index("shard"), rank])
    weight_qkv = Weight(w_qkv, 1, token, shards, ranks)
    weight_up = Weight(w_up[None], 1, token, shards, ranks)
    weight_down = Weight(w_down[None], 2, token, shards, ranks)
    weight_dense = Weight(w_dense[None], 2, token, shards, ranks)

    deal = block_deal[0]
    seg_row = segments[0]
    group = seg_row.shape[0]
    block = group // deal.shape[0]
    quarters = deal.shape[0] // ranks
    rank_rows = quarters * block
    split = ranks // quarters
    pieces = width // split // GROUP
    length = group // quarters
    at = jnp.arange(group, dtype=jnp.int32)
    previous = jnp.concatenate([seg_row[:1] - 1, seg_row[:-1]])
    begins = lax.cummax(jnp.where(seg_row != previous, at, 0), axis=0)
    places = (at - begins).reshape(deal.shape[0], block)
    deal_by_rank = deal.reshape(ranks, quarters)
    my_deal = lax.dynamic_index_in_dim(deal_by_rank, rank, 0, keepdims=False)
    picked = my_deal[:, None] == jnp.arange(deal.shape[0], dtype=jnp.int32)[None, :]
    rank_place = jnp.sum(jnp.where(picked[:, :, None], places[None], 0), axis=1).reshape(-1)
    quarter = rank // split
    partners = rank ^ jnp.arange(ranks, dtype=jnp.int32)
    in_quarter = jnp.take(lax.dynamic_index_in_dim(deal_by_rank, quarter, 1, keepdims=False), partners)
    pos = in_quarter - quarter * ranks
    my_begins = lax.dynamic_slice_in_dim(begins, quarter * length, length) - quarter * length
    quarter_place = jnp.arange(length, dtype=jnp.int32) - my_begins
    start_col = my_begins[:, None]
    lane = jnp.arange(128, dtype=jnp.int32) % HEAD
    frequency = ROPE_BASE ** (-2.0 * (lane % (ROT // 2)).astype(F32) / ROT)
    frequency = jnp.where(lane < ROT, frequency, 0.0)
    sign = jnp.where(lane < ROT // 2, -1.0, 1.0)
    all_places = jnp.concatenate([rank_place, quarter_place]).astype(F32)
    angles = all_places[:, None] * frequency[None, :]
    cosine, sine = jnp.cos(angles), jnp.sin(angles) * sign[None, :]
    target_row, target_col = partners // split, partners % split

    cot_rows = cotangent.astype(F32)
    cot_sum = jnp.sum(cot_rows, axis=0, keepdims=True)
    ready = after(cotangent, cot_sum, vec, qkv_bias, up_bias, cosine, sine, start_col, pos)
    cot_all = lax.all_gather(ready, "tp", axis=0, tiled=True)

    full_one, sent = project(
        flags, split, ranks, x_all, vec, weight_qkv, qkv_bias, cosine[:rank_rows],
        sine[:rank_rows], block, weight_up.arrays + weight_down.arrays + weight_dense.arrays,
    )

    def swap(sent):
        return [by_xor("ctx", ranks, s)(piece) if s else piece for s, piece in enumerate(sent)]

    arrived = exchange(sent, pieces, ranks, 2)
    full_two, activated, slope = mlp(
        flags, x_all, vec, weight_up, up_bias, block, sent[0]
    )
    outs, kept, late = [], [], in_hbm(slope)
    for p in range(pieces):
        out, keep = attend(pos, start_col, arrived[p], late, outs[0][1:] if p else [])
        outs.append(out)
        kept.append(keep)
        late = out[0]
    out_pieces = [out[0] for out in outs] + swap(outs[-1])[1:]

    axes = (("shard", shards), ("ctx", ranks))
    tables = (cosine[rank_rows:], sine[rank_rows:])
    part = mlp_down(flags, activated, weight_down, block, late)
    attended, partial = out_partial(
        flags, target_row, target_col, out_pieces, part, weight_dense, block
    )
    summed = lax.psum_scatter(partial, "tp", scatter_dimension=0, tiled=True)
    sent = attn_grad(flags, split, ranks, cot_all, weight_dense, block, [in_hbm(partial)])
    arrived = exchange(sent, pieces, ranks, ranks)
    first, bits = group_grad(flags, [(cot_all, activated)], None, axes, (sent[0],))
    grad_pieces, late = [], in_hbm(first[0])
    for p in range(pieces):
        grads = attend_back(pos, start_col, kept[p], *tables, arrived[p], late, 0 if p else 6)
        grad_pieces += swap(grads)
        late = grads[0]
    grad_pre, two_part, two_sums, grad_ubias = mlp_back(
        flags, x_all, cot_all, slope, weight_down, weight_up, vec, block,
        grad_pieces[: ranks * (pieces - 1)] + [late],
    )
    dlin, row_sum, one_sums, grad_qbias = input_grad(
        flags, target_row, target_col, x_all, grad_pieces, weight_qkv, two_part, vec, block,
        first[-1],
    )
    first, late = scatter_group(flags, first, bits, (dlin,))
    own_sum = lax.psum_scatter(after(row_sum, summed), "tp", scatter_dimension=0, tiled=True)

    owners = shards * ranks
    each, share = HEAD // owners, dim // owners

    def by_owner(row, lines):
        row = row.reshape(lines, owners, each).transpose(1, 0, 2).reshape(owners, -1)
        return jnp.pad(row, ((0, 0), (0, share - lines * each))).reshape(1, dim)

    small_rows = jnp.concatenate(
        [
            one_sums[:2], two_sums[:2], cot_sum, cot_sum,
            by_owner(grad_qbias[0], 3 * heads), by_owner(grad_ubias[0], bias_up.shape[0]),
        ],
        axis=0,
    )
    hidden, wide = weight_up.shape[2], 3 * width
    third, _ = group_grad(
        flags, [(full_one, dlin), (cot_all, attended)], small_rows, axes, (late,)
    )
    (grad_down,) = group_total(first, (("flip", hidden),), (in_hbm(third[0]),), 10)
    third, late = scatter_group(flags, third, bits, (in_hbm(grad_down),))
    second, _ = group_grad(flags, [(full_two, grad_pre)], None, axes, (late,))
    grad_qkv, grad_dense, small_rows = group_total(
        third, (("three", wide), ("flip", width), ("small", 128)), (in_hbm(second[0]),), 8
    )
    second, late = scatter_group(flags, second, bits, (in_hbm(grad_dense),))
    rows_in = hidden_in.astype(F32)
    output = (rows_in + summed.astype(F32) + vec[4:5] + vec[5:6]).astype(BF16)
    own_sum = after(own_sum, in_hbm(grad_dense)).astype(F32)
    hat, inverse = norm_rows(rows_in)
    centered = own_sum - jnp.mean(own_sum, axis=-1, keepdims=True)
    along = jnp.mean(own_sum * hat, axis=-1, keepdims=True)
    grad_in = (cot_rows + inverse * (centered - hat * along)).astype(BF16)
    grad_vec = small_rows[:6].reshape((6,) + (2,) * (tps.bit_length() - 1) + (-1,))
    for bit in reversed(range(tps.bit_length() - 1)):
        mine = (lax.axis_index("tp") >> bit) & 1
        keep = lax.dynamic_index_in_dim(grad_vec, mine, 1, keepdims=False)
        away = lax.dynamic_index_in_dim(grad_vec, 1 - mine, 1, keepdims=False)
        away = after(away, in_hbm(grad_in)) if bit == 0 else after(away, late)
        grad_vec = keep + by_xor("tp", tps, 1 << bit)(away)
    grad_qbias = small_rows[6, : 3 * heads * each].reshape(3, heads, each)
    grad_ubias = small_rows[7, : bias_up.shape[0] * each].reshape(bias_up.shape[0], each)

    (grad_up,) = group_total(second, (("keep", hidden),), (in_hbm(grad_in),), 0)
    return (
        output, grad_in, grad_qkv, grad_qbias, grad_dense, grad_up, grad_ubias, grad_down,
        grad_vec,
    )


def solution(mesh):
    sizes = tuple(mesh.shape[name] for name in ("shard", "ctx", "tp"))
    return jax.shard_map(
        functools.partial(body, sizes),
        mesh=mesh,
        in_specs=(
            P(("shard", "ctx", "tp"), None),
            P(None, "shard", "tp"),
            P(None, "tp", "shard"),
            P("tp", "shard"),
            P("shard", "tp"),
            P("tp", "shard"),
            P("tp", "shard"),
            P(None, "shard"),
            P("shard", None),
            P("shard", None),
            P(("shard", "ctx", "tp"), None),
        ),
        out_specs=(
            P(("shard", "ctx", "tp"), None),
            P(("shard", "ctx", "tp"), None),
            P(None, ("shard", "ctx"), "tp"),
            P(None, "tp", ("shard", "ctx")),
            P("tp", ("shard", "ctx")),
            P(("shard", "ctx"), "tp"),
            P("tp", ("shard", "ctx")),
            P("tp", ("shard", "ctx")),
            P(None, ("shard", "ctx", "tp")),
        ),
        check_vma=False,
    )
```
